32 devices in a mesh: req: 8 (over z, core), mp: 4 (over y, x).
Axes of the slice: x: 2, y: 2, z: 4, core: 2. Of those that a mesh axis runs over, the one named last changes fastest.
Arguments:
- tokens: bfloat16 [784, 7168], P('req', 'mp'), may hold values from -6 to 6
- layernorm_scale: float32 [7168], replicated, may hold values from 0.5 to 1.5
- layernorm_bias: float32 [7168], replicated, may hold values from -3 to 3
- query_key_value_weight: bfloat16 [3, 7168, 6144], P(None, 'req', 'mp'), may hold values from -0.0625 to 0.0625
- query_key_value_bias: float32 [3, 6144], P(None, 'mp'), may hold values from -3 to 3
- adapter_down_weight: bfloat16 [64, 7168, 32], P('req', 'mp'), may hold values from -0.0625 to 0.0625
- adapter_up_weight: bfloat16 [64, 2, 16, 6144], P('req', None, None, 'mp'), may hold values from -1.5 to 1.5
- adapter_index_table: int32 [8, 5], P('req'), may hold values from 0 to 63
- prompt_length_list: int32 [24], P('req'), may hold values from 1 to 32, 480 in all
- cache: bfloat16 [16, 2048, 2, 6144], P('req', None, None, 'mp'), may hold values from -320 to 320, as said below
- cache_length_list: int32 [16], P('req'), may hold values from 1 to 2048, 10240 in all
- output_weight: bfloat16 [6144, 7168], P('mp', 'req'), may hold values from -0.078125 to 0.078125
- output_bias: float32 [7168], P('mp'), may hold values from -3 to 3
Outputs:
- layer_out: bfloat16 [784, 7168], P('req', 'mp')
The draws below stay inside these ranges and needn't reach their ends.
Inputs may be any that keep to these rules, and one draw needn't show every extreme that they name: Each prompt fills the first prompt_length_list rows of its slot of 32 rows. Live cache positions are the first cache_length_list of each slot. `cache`: entries mostly of order one, though rare keys may be larger.
All inputs are finite; a program needn't handle non-finite values. No bound on the sum of `prompt_length_list` or of `cache_length_list` on one device may be relied on, other than what follows from the above.
Results may differ from the reference program's by a relative error of at most 0.015.
Values may be sent and summed in bfloat16 or wider, within the bound.
No kernel may reach another device: no remote copies, remote signals or barrier semaphores. Data moves between devices by JAX's collectives and lax.ppermute only.
A program may use at most 256 MiB of HBM per device.

```python
import math
import jax
import jax.numpy as jnp
import numpy as np
from jax import lax

MODEL_WIDTH = 7168
HEAD_DIM = 128
HEADS = 48
ADAPTER_RANK = 16
ADAPTER_COUNT = 64
DEC_DEV = 2
PSLOTS = 3
PLEN = 32
CACHE = 2048
HEAD_FEATURES = 6144
ROWS = 784
PROMPTS = 24
DECODES = 16
N_REQ = 8


def draw_cache(key, part):
    main_key = jax.random.fold_in(key, 0)
    entries = jnp.clip(jax.random.normal(main_key, (DECODES, CACHE, 2, HEADS * HEAD_DIM), jnp.float32), -8.0, 8.0)
    return entries.astype(jnp.bfloat16)


def plant(drawn, stream_key, low, largest):
    index_at = [jax.random.randint(jax.random.fold_in(stream_key, axis), (), 0, length) for axis, length in enumerate(drawn.shape)]
    main_axis = drawn.shape.index(max(drawn.shape))
    next_to = index_at[:main_axis] + [(index_at[main_axis] + 1) % drawn.shape[main_axis]] + index_at[main_axis + 1:]
    return drawn.at[tuple(index_at)].set(low).at[tuple(next_to)].set(largest)


def steps_of(stream_key, extent, cuts, low, high):
    loudness, own = 1.0, jax.random.fold_in(stream_key, 6)
    for position, parts in cuts:
        draws = jnp.exp(jax.random.uniform(jax.random.fold_in(own, position), (parts,), jnp.float32, low / len(cuts), high / len(cuts)))
        loudness = loudness * jnp.repeat(draws, extent[position] // parts).reshape([-1 if axis == position else 1 for axis in range(len(extent))])
    return loudness


def rank_bounds(number_of, lean):
    loads = [(1 << 20) // math.isqrt(grade ** lean) + 1 for grade in range(1, number_of + 1)]
    width = 1 + sum(loads) // (1 << 30)
    return np.cumsum(np.array([max(1, weight // width) for weight in loads]))


def ranked(rng, shape, count, slope):
    table = rank_bounds(count, slope)
    ticket = jax.random.randint(jax.random.fold_in(rng, 1), shape, 0, int(table[count - 1]))
    grade = jnp.searchsorted(jnp.asarray(table, jnp.int32), ticket, side="right")
    return jax.random.permutation(jax.random.fold_in(rng, 2), count)[grade].astype(jnp.int32)


def split_up(amount, total, bound, skew):
    weights = [(1 << 20) // math.isqrt(standing ** skew) + 1 for standing in range(2, amount + 1)]
    spare, holding = total - bound - (amount - 1), [1] * (amount - 1)
    while spare > 0:
        free = [i for i in range(amount - 1) if holding[i] < bound]
        pool, remaining = sum([weights[i] for i in free]), spare
        for i in free:
            addition = min(bound - holding[i], max(1, remaining * weights[i] // pool), spare)
            holding[i] = holding[i] + addition
            spare = spare - addition
    return np.array([bound] + holding)


def ragged_sizes(key, count, total, limit, lean):
    if count == 2:
        one = jax.random.randint(key, (), max(1, total - limit), min(limit, total - 1) + 1)
        return jnp.stack([one, total - one])
    tallies = jnp.asarray(split_up(count, total, limit, lean), jnp.int32)
    couples = (count - 1) // 2
    giver, taker = tallies[1:1 + 2 * couples:2], tallies[2:2 + 2 * couples:2]
    room = jnp.minimum(giver - 1, limit - taker)
    moved = jax.random.randint(jax.random.fold_in(key, 1), (couples,), 0, 1 << 20) % (room + 1)
    tallies = tallies.at[1:1 + 2 * couples:2].set(giver - moved).at[2:2 + 2 * couples:2].set(taker + moved)
    return tallies[jax.random.permutation(jax.random.fold_in(key, 2), count)]


def gaussian(stream_key, dims, spread, most, cuts=(), dtype=jnp.bfloat16):
    level = steps_of(stream_key, dims, cuts, -0.22, 0.18) if cuts else 1.0
    drawn = jax.random.normal(stream_key, dims, jnp.float32) * spread * level
    return jnp.minimum(jnp.maximum(drawn, -most), most).astype(dtype)


def setup_inputs(seed: int = 0) -> dict:
    key_of = jax.random.split(jax.random.key(seed), 14)
    tokens = gaussian(key_of[0], (ROWS, MODEL_WIDTH), 1.0, 6.0, ((0, 8), (1, 4)))
    layernorm_scale = jnp.clip(1.0 + 0.1 * jax.random.normal(key_of[1], (MODEL_WIDTH,), jnp.float32), 0.5, 1.5)
    layernorm_bias = gaussian(key_of[2], (MODEL_WIDTH,), 0.5, 3.0, (), jnp.float32)
    query_key_value_weight = gaussian(key_of[3], (3, MODEL_WIDTH, HEAD_FEATURES), MODEL_WIDTH ** -0.5, 0.0625, ((1, 8), (2, 4)))
    query_key_value_bias = gaussian(key_of[4], (3, HEAD_FEATURES), 0.5, 3.0, ((1, 4),), jnp.float32)
    adapter_down_weight = gaussian(key_of[5], (ADAPTER_COUNT, MODEL_WIDTH, 2 * ADAPTER_RANK), MODEL_WIDTH ** -0.5, 0.0625, ((0, 8), (1, 4)))
    adapter_up_weight = gaussian(key_of[6], (ADAPTER_COUNT, 2, ADAPTER_RANK, HEAD_FEATURES), ADAPTER_RANK ** -0.5, 1.5, ((0, 8), (3, 4)))
    adapter_index_table = plant(ranked(key_of[7], (N_REQ, PSLOTS + DEC_DEV), ADAPTER_COUNT, 2), jax.random.fold_in(key_of[7], 3), 0, ADAPTER_COUNT - 1).astype(jnp.int32)
    prompt_length_list = ragged_sizes(key_of[8], PROMPTS, PROMPTS * PLEN * 5 // 8, PLEN, 1).astype(jnp.int32)
    cache = draw_cache(jax.random.fold_in(key_of[13], 71), 0)
    cache_length_list = ragged_sizes(key_of[10], DECODES, DECODES * CACHE * 5 // 16, CACHE, 1).astype(jnp.int32)
    output_weight = gaussian(key_of[11], (HEAD_FEATURES, MODEL_WIDTH), HEAD_FEATURES ** -0.5, 0.078125, ((0, 4), (1, 8)))
    output_bias = gaussian(key_of[12], (MODEL_WIDTH,), 0.5, 3.0, ((0, 4),), jnp.float32)
    return dict(tokens=tokens, layernorm_scale=layernorm_scale, layernorm_bias=layernorm_bias, query_key_value_weight=query_key_value_weight, query_key_value_bias=query_key_value_bias, adapter_down_weight=adapter_down_weight, adapter_up_weight=adapter_up_weight, adapter_index_table=adapter_index_table, prompt_length_list=prompt_length_list, cache=cache, cache_length_list=cache_length_list, output_weight=output_weight, output_bias=output_bias)


def layer_norm(row_data, gain_vec, shift_vec):
    values = row_data.astype(jnp.float32)
    average = lax.optimization_barrier(jnp.mean(values, axis=-1, keepdims=True))
    centred = values - average
    variance = lax.optimization_barrier(jnp.mean(centred * centred, axis=-1, keepdims=True))
    scaled = centred * lax.rsqrt(variance + 1e-05)
    return (scaled * gain_vec + shift_vec).astype(jnp.bfloat16)

def reference(tokens, layernorm_scale, layernorm_bias, query_key_value_weight, query_key_value_bias, adapter_down_weight, adapter_up_weight, adapter_index_table, prompt_length_list, cache, cache_length_list, output_weight, output_bias):
    prompt_rows = PSLOTS * PLEN
    rows_dev = prompt_rows + DEC_DEV
    combined_width = HEADS * HEAD_DIM
    score_scale = HEAD_DIM ** (-0.5)
    normed = layer_norm(tokens, layernorm_scale, layernorm_bias)
    projected = jnp.stack([jnp.dot(normed, query_key_value_weight[adapter_membership], preferred_element_type=jnp.float32) for adapter_membership in range(3)], axis=1)
    projected = projected + query_key_value_bias[None]
    positions = jnp.arange(rows_dev)
    request_slot = jnp.where(positions < prompt_rows, positions // PLEN, PSLOTS + positions - prompt_rows).astype(jnp.int32)
    row_adapter = adapter_index_table[:, request_slot].reshape(-1)
    selection_mask = (row_adapter[:, None] == jnp.arange(ADAPTER_COUNT)[None, :]).astype(jnp.float32)
    down_weight_flat = jnp.transpose(adapter_down_weight, (1, 0, 2)).reshape(MODEL_WIDTH, ADAPTER_COUNT * 2 * ADAPTER_RANK)
    adapter_wise_sums = jnp.dot(normed, down_weight_flat, preferred_element_type=jnp.float32).reshape(-1, ADAPTER_COUNT, 2 * ADAPTER_RANK)
    reduced_rank_rows = jnp.einsum('na,nae->ne', selection_mask, adapter_wise_sums).astype(jnp.bfloat16)
    broadcast_rank_rows = (selection_mask.astype(jnp.bfloat16)[:, :, None] * reduced_rank_rows[:, None, :]).reshape(-1, ADAPTER_COUNT, 2, ADAPTER_RANK)
    deltas = []
    for adapter_membership in range(2):
        part_rank = broadcast_rank_rows[:, :, adapter_membership].reshape(-1, ADAPTER_COUNT * ADAPTER_RANK)
        up_weight_flat = adapter_up_weight[:, adapter_membership].reshape(ADAPTER_COUNT * ADAPTER_RANK, combined_width)
        rounded = jnp.dot(part_rank, up_weight_flat, preferred_element_type=jnp.float32).astype(jnp.bfloat16)
        deltas.append(lax.optimization_barrier(rounded).astype(jnp.float32))
    queries = (projected[:, 0] + deltas[0]).astype(jnp.bfloat16)
    keys_new = projected[:, 1].astype(jnp.bfloat16)
    values_new = (projected[:, 2] + deltas[1]).astype(jnp.bfloat16)
    grid_q = queries.reshape(N_REQ, rows_dev, HEADS, HEAD_DIM)
    grid_k = keys_new.reshape(N_REQ, rows_dev, HEADS, HEAD_DIM)
    grid_v = values_new.reshape(N_REQ, rows_dev, HEADS, HEAD_DIM)
    prompt_q = grid_q[:, :prompt_rows].reshape(N_REQ * PSLOTS, PLEN, HEADS, HEAD_DIM)
    prompt_k = grid_k[:, :prompt_rows].reshape(N_REQ * PSLOTS, PLEN, HEADS, HEAD_DIM)
    prompt_v = grid_v[:, :prompt_rows].reshape(N_REQ * PSLOTS, PLEN, HEADS, HEAD_DIM)
    causal = jnp.arange(PLEN)[None, :] <= jnp.arange(PLEN)[:, None]

    def one_prompt(item):
        query_blk, key_blk, value_blk, length = item
        scores = jnp.einsum('ihd,jhd->hij', query_blk.astype(jnp.float32), key_blk.astype(jnp.float32)) * score_scale
        scores = jnp.where(causal[None], scores, -1e+30)
        highest = lax.optimization_barrier(jnp.max(scores, axis=2, keepdims=True))
        weights = jnp.where(causal[None], jnp.exp(scores - highest), 0.0)
        weights = (weights / lax.optimization_barrier(jnp.sum(weights, axis=2, keepdims=True))).astype(jnp.bfloat16)
        result = jnp.einsum('hij,jhd->ihd', weights.astype(jnp.float32), value_blk.astype(jnp.float32))
        active = jnp.arange(PLEN) < length
        return jnp.where(active[:, None, None], result, 0.0).astype(jnp.bfloat16)
    prompt_out = lax.map(one_prompt, (prompt_q, prompt_k, prompt_v, prompt_length_list))
    prompt_out = prompt_out.reshape(N_REQ, prompt_rows, combined_width)
    decode_q = grid_q[:, prompt_rows:].reshape(N_REQ * DEC_DEV, HEADS, HEAD_DIM)
    decode_k = grid_k[:, prompt_rows:].reshape(N_REQ * DEC_DEV, HEADS, HEAD_DIM)
    decode_v = grid_v[:, prompt_rows:].reshape(N_REQ * DEC_DEV, HEADS, HEAD_DIM)

    def one_decode(item):
        query_row, key_row, value_row, stored, length = item
        keys_old = stored[:, 0].reshape(CACHE, HEADS, HEAD_DIM).astype(jnp.float32)
        values_old = stored[:, 1].reshape(CACHE, HEADS, HEAD_DIM).astype(jnp.float32)
        query_row = query_row.astype(jnp.float32)
        row_scores = jnp.einsum('hd,thd->ht', query_row, keys_old) * score_scale
        live_cache = jnp.arange(CACHE)[None, :] < length
        row_scores = jnp.where(live_cache, row_scores, -1e+30)
        self_score = lax.optimization_barrier(jnp.sum(query_row * key_row.astype(jnp.float32), axis=1)) * score_scale
        row_top = jnp.maximum(lax.optimization_barrier(jnp.max(row_scores, axis=1)), self_score)
        row_weights = jnp.where(live_cache, jnp.exp(row_scores - row_top[:, None]), 0.0)
        self_weight = jnp.exp(self_score - row_top)
        totals = lax.optimization_barrier(jnp.sum(row_weights, axis=1)) + self_weight
        row_weights = (row_weights / totals[:, None]).astype(jnp.bfloat16)
        self_weight = (self_weight / totals).astype(jnp.bfloat16)
        result = jnp.einsum('ht,thd->hd', row_weights.astype(jnp.float32), values_old)
        result = result + self_weight.astype(jnp.float32)[:, None] * value_row.astype(jnp.float32)
        return result.astype(jnp.bfloat16)
    decode_out = lax.map(one_decode, (decode_q, decode_k, decode_v, cache, cache_length_list))
    decode_out = decode_out.reshape(N_REQ, DEC_DEV, combined_width)
    attended = jnp.concatenate([prompt_out, decode_out], axis=1).reshape(N_REQ * rows_dev, combined_width)
    mixed = jnp.dot(attended, output_weight, preferred_element_type=jnp.float32)
    return (tokens.astype(jnp.float32) + mixed + output_bias[None]).astype(jnp.bfloat16)
```

```python
import functools

import jax
import jax.numpy as jnp
from jax import lax
from jax.experimental import pallas as pl
from jax.experimental.pallas import tpu as pltpu
from jax.sharding import PartitionSpec as P

HEAD_DIM = 128
ADAPTER_RANK = 16
BF = jnp.bfloat16
F32 = jnp.float32
MIB = 1 << 20

NZ, NM = 4, 4
SLOTS, PLEN, DEC = 3, 32, 2
QROWS = 24
BLK = 32
CHUNK = 128
DCH = 16


def swap_req(x, bits):
    return lax.ppermute(x, "req", [(i, i ^ bits) for i in range(2 * NZ)])


def swap_mp(x, bits):
    return lax.ppermute(x, "mp", [(i, i ^ bits) for i in range(NM)])


def move_z(x, hops):
    return lax.ppermute(x, "req", [(a * 2 + c, b * 2 + c) for a, b in hops for c in range(2)])


RIGHT = [[(0, 1), (1, 2), (2, 3)], [(1, 2), (2, 3)], [(2, 3)]]
LEFT = [[(3, 2), (2, 1), (1, 0)], [(2, 1), (1, 0)], [(1, 0)]]


def gather_z(x):
    right, left = [x], [x]
    for s in range(NZ - 1):
        right.append(move_z(right[-1], RIGHT[s]))
        left.append(move_z(left[-1], LEFT[s]))
    return [x] + [right[s] + left[NZ - s] for s in range(1, NZ)]


def norm_kernel(place_ref, own_ref, r1_ref, r2_ref, r3_ref, gain_ref, shift_ref, table_ref, o0, o1, o2, o3, held):
    z, m = place_ref[0], place_ref[1]
    for k, ref in enumerate((own_ref, r1_ref, r2_ref, r3_ref)):
        held[k] = ref[...].astype(F32)
    width = NM * held.shape[2]
    mean = sum(jnp.sum(held[k], axis=1, keepdims=True) for k in range(NM)) / width
    var = sum(jnp.sum((held[k] - mean) ** 2, axis=1, keepdims=True) for k in range(NM)) / width
    rstd = lax.rsqrt(var + 1e-05)
    last = lax.broadcasted_iota(jnp.int32, held.shape[1:], 0) == BLK - 1
    for k, out in enumerate((o0, o1, o2, o3)):
        block = jnp.bitwise_xor(z, k)
        x = held[jnp.bitwise_xor(block, m)]
        y = (x - mean) * rstd * gain_ref[block] + shift_ref[block]
        out[...] = jnp.where(last, table_ref[...], y).astype(BF)


def norm_rows(place, blocks, gain, shift, table):
    cols = blocks[0].shape[1]
    out = jax.ShapeDtypeStruct((BLK, cols), BF)
    vmem = pl.BlockSpec(memory_space=pltpu.VMEM)
    return pl.pallas_call(
        norm_kernel,
        out_shape=[out] * 4,
        in_specs=[pl.BlockSpec(memory_space=pltpu.SMEM)] + [vmem] * 7,
        out_specs=[vmem] * 4,
        scratch_shapes=[pltpu.VMEM((NM, BLK, cols), F32)],
        compiler_params=pltpu.CompilerParams(vmem_limit_bytes=24 * MIB),
        name="norm_rows",
    )(place, *blocks, gain, shift, table)


def prompt_kernel(q_ref, ka_ref, kb_ref, va_ref, vb_ref, cr_ref, cc_ref, o_ref):
    rows = cr_ref[...]
    cols = cc_ref[...]
    allowed = ((rows >> 5) == (cols >> 5)) & (cols <= rows)
    keys = jnp.concatenate([ka_ref[...], kb_ref[...]], axis=0)
    values = jnp.concatenate([va_ref[...], vb_ref[...]], axis=0)
    for h in range(q_ref.shape[1] // HEAD_DIM):
        at = slice(h * HEAD_DIM, (h + 1) * HEAD_DIM)
        s = lax.dot_general(q_ref[:, at], keys[:, at], (((1,), (1,)), ((), ())), preferred_element_type=F32)
        s = jnp.where(allowed, s * HEAD_DIM**-0.5, -1e30)
        top = jnp.max(s, axis=1, keepdims=True)
        w = jnp.where(allowed, jnp.exp(s - top), 0.0)
        w = (w / jnp.sum(w, axis=1, keepdims=True)).astype(BF)
        o_ref[:, at] = jnp.dot(w, values[:, at], preferred_element_type=F32).astype(BF)


def prompt_attention(q, ka, kb, va, vb, code_rows, code_cols):
    vmem = pl.BlockSpec(memory_space=pltpu.VMEM)
    return pl.pallas_call(
        prompt_kernel,
        out_shape=jax.ShapeDtypeStruct(q.shape, BF),
        in_specs=[vmem] * 7,
        out_specs=vmem,
        compiler_params=pltpu.CompilerParams(vmem_limit_bytes=32 * MIB),
        name="prompt_attention",
    )(q, ka, kb, va, vb, code_rows, code_cols)


def decode_kernel(len_ref, q_ref, k_ref, v_ref, c_ref, o_ref, qbd, top, total, acc):
    d, t = pl.program_id(0), pl.program_id(1)
    span = c_ref.shape[1]
    live = len_ref[d]
    heads, feats = qbd.shape
    diag = lax.broadcasted_iota(jnp.int32, (heads, feats), 1) // HEAD_DIM == lax.broadcasted_iota(
        jnp.int32, (heads, feats), 0
    )

    @pl.when(t == 0)
    def _():
        q = jnp.where(diag, q_ref[0].astype(F32), 0.0)
        qbd[...] = q.astype(BF)
        own = jnp.sum(q * k_ref[0].astype(F32), axis=1, keepdims=True) * HEAD_DIM**-0.5
        top[...] = jnp.broadcast_to(own, top.shape)
        total[...] = jnp.ones_like(total)
        acc[...] = jnp.broadcast_to(v_ref[0].astype(F32), acc.shape)

    @pl.when(t * span < live)
    def _():
        x = c_ref[0].reshape(2 * span, feats)
        s = lax.dot_general(qbd[...], x, (((1,), (1,)), ((), ())), preferred_element_type=F32)
        column = lax.broadcasted_iota(jnp.int32, s.shape, 1)
        valid = (column % 2 == 0) & (t * span + column // 2 < live)
        s = jnp.where(valid, s * HEAD_DIM**-0.5, -1e30)
        before = top[:, :1]
        now = jnp.maximum(before, jnp.max(s, axis=1, keepdims=True))
        fade = jnp.exp(before - now)
        w = jnp.where(valid, jnp.exp(s - now), 0.0)
        total[...] = total[...] * fade + jnp.sum(w, axis=1, keepdims=True)
        top[...] = jnp.broadcast_to(now, top.shape)
        w = pltpu.roll(w, 1, 1).astype(BF)
        acc[...] = acc[...] * fade + jnp.dot(w, x, preferred_element_type=F32)

    @pl.when(t == pl.num_programs(1) - 1)
    def _():
        o = acc[...] / total[:, :1]
        o_ref[0] = jnp.sum(jnp.where(diag, o, 0.0), axis=0, keepdims=True).astype(BF)


def decode_attention(lengths, q, k, v, cache, span=256):
    count, positions, _, feats = cache.shape
    steps = positions // span
    row = pl.BlockSpec((1, 1, feats), lambda d, t, n: (d, 0, 0))
    heads = 16
    return pl.pallas_call(
        decode_kernel,
        grid_spec=pltpu.PrefetchScalarGridSpec(
            num_scalar_prefetch=1,
            grid=(count, steps),
            in_specs=[row, row, row]
            + [
                pl.BlockSpec(
                    (1, span, 2, feats),
                    lambda d, t, n: (d, jnp.minimum(t, (n[d] - 1) // span), 0, 0),
                )
            ],
            out_specs=row,
            scratch_shapes=[
                pltpu.VMEM((heads, feats), BF),
                pltpu.VMEM((heads, 128), F32),
                pltpu.VMEM((heads, 128), F32),
                pltpu.VMEM((heads, feats), F32),
            ],
        ),
        out_shape=jax.ShapeDtypeStruct((count, 1, feats), BF),
        compiler_params=pltpu.CompilerParams(vmem_limit_bytes=32 * MIB),
        cost_estimate=pl.CostEstimate(
            flops=4 * 256 * count * positions * feats, bytes_accessed=4 * count * positions * feats, transcendentals=0
        ),
        name="decode_attention",
    )(lengths, q, k, v, cache)


def out_kernel(place_ref, *refs):
    own, other, dec_ref, w_ref, pos_ref, o_ref, mixed = refs[:4], refs[4:8], *refs[8:]
    z = place_ref[0]
    half, width = own[0].shape
    for base, parts in ((0, own), (half, other)):
        total = None
        for s in range(NZ):
            block = jnp.bitwise_and(z - s, NZ - 1)
            w = w_ref[pl.ds(pl.multiple_of(block * width, width), width), :]
            term = jnp.dot(parts[s][...], w, preferred_element_type=F32)
            total = term if total is None else total + term
        mixed[pl.ds(base, half), :] = total.astype(BF)
    mixed[pl.ds(2 * half, dec_ref.shape[0]), :] = jnp.dot(
        dec_ref[...], w_ref[...], preferred_element_type=F32
    ).astype(BF)
    pos = pos_ref[...]
    pick = (pos == lax.broadcasted_iota(jnp.int32, (pos.shape[0], mixed.shape[0]), 1)).astype(BF)
    o_ref[...] = jnp.dot(pick, mixed[...], preferred_element_type=F32).astype(BF)


def out_project(place, own, other, dec, weight, pos):
    vmem = pl.BlockSpec(memory_space=pltpu.VMEM)
    rows = 2 * own[0].shape[0] + dec.shape[0]
    return pl.pallas_call(
        out_kernel,
        out_shape=jax.ShapeDtypeStruct((pos.shape[0], weight.shape[1]), BF),
        in_specs=[pl.BlockSpec(memory_space=pltpu.SMEM)] + [vmem] * 11,
        out_specs=vmem,
        scratch_shapes=[pltpu.VMEM((rows, weight.shape[1]), BF)],
        compiler_params=pltpu.CompilerParams(vmem_limit_bytes=40 * MIB),
        name="out_project",
    )(place, *own, *other, dec, weight, pos)


def quarter_of(index, size):
    return sum((index >= j * size).astype(jnp.int32) for j in range(1, NM))


def packed_device(
    tokens,
    layernorm_scale,
    layernorm_bias,
    query_key_value_weight,
    query_key_value_bias,
    adapter_down_weight,
    adapter_up_weight,
    adapter_index_table,
    prompt_length_list,
    cache,
    cache_length_list,
    output_weight,
    output_bias,
):
    i32 = jnp.int32
    r = lax.axis_index("req").astype(i32)
    m = lax.axis_index("mp").astype(i32)
    z, c = r >> 1, r & 1
    place = jnp.stack([z, m])
    rows_dev, cols = tokens.shape
    prompt_rows = SLOTS * PLEN
    feats = query_key_value_weight.shape[2]
    depth = query_key_value_weight.shape[1]
    per_z = feats // NZ
    own_adapters = adapter_down_weight.shape[0]

    down = jnp.transpose(adapter_down_weight, (0, 2, 1)).reshape(own_adapters * 2 * ADAPTER_RANK, cols)
    down_chip = jnp.concatenate([down, swap_req(down, 1)], axis=0)

    with jax.named_scope("deal"):
        lens = prompt_length_list
        starts = jnp.concatenate([jnp.zeros((1,), i32), jnp.cumsum(lens)[:-1].astype(i32)])
        size = (jnp.sum(lens) + 3) >> 2
        at = jnp.arange(PLEN, dtype=i32)[None, :]
        index = starts[:, None] + at
        quarter = quarter_of(index, size)
        target = jnp.where(at < lens[:, None], quarter * BLK + index - quarter * size, -1).reshape(-1)
        target = jnp.concatenate([target, z * BLK + QROWS + jnp.arange(DEC, dtype=i32)])
        pick = (jnp.arange(NM * BLK, dtype=i32)[:, None] == target[None, :]).astype(BF)
        dealt = jnp.dot(pick, tokens, preferred_element_type=F32).astype(BF).reshape(NM, BLK, cols)

        def block(k):
            return lax.dynamic_index_in_dim(dealt, m ^ k, 0, keepdims=False)

        blocks = [block(0)] + [swap_mp(block(k), k) for k in range(1, NM)]
    with jax.named_scope("norm_rows"):
        table = jnp.concatenate([lens, adapter_index_table[0]]).astype(F32)
        table = jnp.pad(table, (0, depth - table.shape[0]))
        table = jnp.tile(table, 2)[None, :]
        gain = layernorm_scale.reshape(NM, 1, cols)
        shift = layernorm_bias.reshape(NM, 1, cols)
        normed = norm_rows(place, blocks, gain, shift, table)
    with jax.named_scope("spread_z"):
        rows = jnp.concatenate([normed[0]] + [swap_req(normed[k], 2 * k) for k in range(1, NZ)], axis=0)
        mine = lax.dynamic_slice_in_dim(rows, c * depth, depth, 1)
        theirs = swap_req(lax.dynamic_slice_in_dim(rows, (1 - c) * depth, depth, 1), 1)
        both = jnp.concatenate([mine, theirs], axis=0)

    with jax.named_scope("tables"):
        tables = both.reshape(2 * NZ, BLK, depth)[:, BLK - 1, : SLOTS + SLOTS + DEC].astype(i32)
        order = jnp.arange(2 * NZ, dtype=i32)
        source = ((z ^ (order & 3)) << 1) + (c ^ (order >> 2))
        tables = jnp.sum(
            jnp.where(source[None, :, None] == order[:, None, None], tables[None], 0), axis=1
        )
        all_lens, all_adapters = tables[:, :SLOTS], tables[:, SLOTS:]
        live_count = jnp.sum(all_lens, axis=1)
        sizes = (live_count + 3) >> 2
        offsets = jnp.sum(jnp.where(order[None, :] < order[:, None], sizes[None, :], 0), axis=1)

        def by_source(values, src):
            return jnp.sum(jnp.where(src[:, None] == order[None, :], values[None, :], 0), axis=1)

    with jax.named_scope("pack"):
        src_size = by_source(sizes, source)
        src_live = by_source(live_count, source)
        src_off = by_source(offsets, source)
        t = jnp.arange(BLK, dtype=i32)[None, :]
        have = jnp.clip(src_live - m * src_size, 0, src_size)
        prompt_to = jnp.where(t < have[:, None], src_off[:, None] + t, -1)
        decode_to = jnp.where(
            (t >= QROWS) & (t < QROWS + DEC) & ((source >> 1) == m)[:, None],
            CHUNK + (source & 1)[:, None] * DEC + t - QROWS,
            -1,
        )
        to = jnp.where(t < QROWS, prompt_to, decode_to).reshape(-1)
        pick = (jnp.arange(CHUNK + DCH, dtype=i32)[:, None] == to[None, :]).astype(BF)
        chunk = jnp.dot(pick, both, preferred_element_type=F32).astype(BF)
    with jax.named_scope("gather_chunks"):
        chunks = [chunk] + [swap_mp(chunk, k) for k in range(1, NM)]
        low = jnp.concatenate([chunks[0][:CHUNK], chunks[1][:CHUNK]], axis=0)
        high = jnp.concatenate([chunks[2][:CHUNK], chunks[3][:CHUNK]], axis=0)
        x_own = jnp.where(c == 0, low, high)
        x_other = jnp.where(c == 0, high, low)
        dec_one = 2 * DEC
        x_dec = jnp.concatenate([v[CHUNK : CHUNK + dec_one] for v in chunks], axis=0)

    with jax.named_scope("places"):
        all_starts = jnp.concatenate(
            [jnp.zeros((2 * NZ, 1), i32), all_lens[:, :1], all_lens[:, :1] + all_lens[:, 1:2]], axis=1
        )
        index = (all_starts[:, :, None] + at[None]).reshape(2 * NZ, prompt_rows)
        alive = (at[None] < all_lens[:, :, None]).reshape(2 * NZ, prompt_rows)
        quarter = quarter_of(index, sizes[:, None])
        spot = (quarter ^ m) * CHUNK + offsets[:, None] + index - quarter * sizes[:, None]
        spot = jnp.where(alive, spot, -1)
        spot = jnp.where(alive, ((spot >> 8) ^ c) * 2 * CHUNK + (spot & (2 * CHUNK - 1)), -1)
        dec_ids = jnp.arange(DEC, dtype=i32)[None, :]
        dec_spot = 4 * CHUNK + ((order >> 1) ^ m)[:, None] * dec_one + (order & 1)[:, None] * DEC + dec_ids
        home_spot = jnp.concatenate([spot, dec_spot], axis=1)
        home_adapter = jnp.concatenate(
            [jnp.repeat(all_adapters[:, :SLOTS], PLEN, axis=1), all_adapters[:, SLOTS:]], axis=1
        )
        packed = NM * (CHUNK + dec_one)
        flat_spot = home_spot.reshape(-1)
        hit = jnp.arange(packed, dtype=i32)[:, None] == flat_spot[None, :]
        row_adapter = jnp.sum(jnp.where(hit, home_adapter.reshape(-1)[None, :] + 1, 0), axis=1) - 1
        prompt_id = order[:, None] * SLOTS + jnp.arange(rows_dev, dtype=i32)[None, :] // PLEN
        code = prompt_id * PLEN + jnp.arange(rows_dev, dtype=i32)[None, :] % PLEN
        row_code = jnp.sum(jnp.where(hit, code.reshape(-1)[None, :] + 1, 0), axis=1) - 1
        unused = jnp.arange(packed, dtype=i32) * PLEN + (1 << 16)
        row_code = jnp.where(row_code < 0, unused, row_code)[: 4 * CHUNK]

    with jax.named_scope("home_norm"):
        home = tokens.astype(F32)
        mean = jnp.mean(home, axis=1)
        spread = jnp.sum((home - mean[:, None]) ** 2, axis=1)
        stats = jnp.stack([mean, spread])
        stats = jnp.stack([stats] + [swap_mp(stats, k) for k in range(1, NM)])
        mean_all = jnp.mean(stats[:, 0], axis=0)
        var = (jnp.sum(stats[:, 1], axis=0) + cols * jnp.sum((stats[:, 0] - mean_all) ** 2, axis=0)) / (NM * cols)
        my_gain = lax.dynamic_slice_in_dim(layernorm_scale, m * cols, cols, 0)
        my_shift = lax.dynamic_slice_in_dim(layernorm_bias, m * cols, cols, 0)
        home = (home - mean_all[:, None]) * lax.rsqrt(var + 1e-05)[:, None]
        home = (home * my_gain + my_shift).astype(BF)
    with jax.named_scope("low_rank"):
        pieces = gather_z(home)
        piece_source = [(((z - s) & 3) << 1) + c for s in range(NZ)]
        chip_ids = jnp.concatenate(
            [r * own_adapters + jnp.arange(own_adapters, dtype=i32), (r ^ 1) * own_adapters + jnp.arange(own_adapters, dtype=i32)]
        )
        rank_parts = []
        for s in range(NZ):
            y = lax.dot_general(down_chip, pieces[s], (((1,), (1,)), ((), ())), preferred_element_type=F32)
            y = y.reshape(2 * own_adapters, 2 * ADAPTER_RANK, rows_dev)
            adapters = jnp.sum(jnp.where((order == piece_source[s])[:, None], home_adapter, 0), axis=0)
            rank_parts.append(jnp.sum(jnp.where((chip_ids[:, None] == adapters[None, :])[:, None, :], y, 0.0), axis=0))
        part = jnp.concatenate(rank_parts, axis=1)
        low_rank = part + sum(swap_mp(part, k) for k in range(1, NM))
        low_rank = low_rank.astype(BF)
        low_rank = jnp.concatenate([low_rank, swap_req(low_rank, 1)], axis=1)
        src = jnp.stack(piece_source + [s ^ 1 for s in piece_source])
        spots = jnp.sum(jnp.where((src[:, None] == order[None, :])[:, :, None], home_spot[None], 0), axis=1).reshape(-1)
        hit2 = (jnp.arange(packed, dtype=i32)[:, None] == spots[None, :]).astype(BF)
        packed_rank = lax.dot_general(
            hit2, low_rank, (((1,), (1,)), ((), ())), preferred_element_type=F32
        )
        mine_ids = r * own_adapters + jnp.arange(own_adapters, dtype=i32)
        owned = row_adapter[:, None] == mine_ids[None, :]

        def expand(v):
            return jnp.where(owned[:, :, None], v[:, None, :], 0.0).astype(BF).reshape(packed, own_adapters * ADAPTER_RANK)

        expanded = [expand(packed_rank[:, :ADAPTER_RANK]), None, expand(packed_rank[:, ADAPTER_RANK:])]
        ups = [adapter_up_weight[:, 0].reshape(-1, feats), None, adapter_up_weight[:, 1].reshape(-1, feats)]

    half = 2 * CHUNK

    def partial_sums(x, part, rows_at):
        y = jnp.dot(x, query_key_value_weight[part], preferred_element_type=F32)
        if expanded[part] is not None:
            y = y + jnp.dot(expanded[part][rows_at], ups[part], preferred_element_type=F32)
        return y

    def reduce_z(total):
        def piece(i):
            return lax.dynamic_slice_in_dim(total, jnp.clip(i, 0, NZ - 1) * per_z, per_z, 1)

        def add(own, got, when=None):
            got = got.astype(F32)
            return own + (got if when is None else jnp.where(when, got, 0.0))

        first = move_z(piece(jnp.where(z == 0, 3, 0)).astype(BF), [(0, 1), (3, 2)])
        right = move_z(add(piece(2 + z), first, z == 1).astype(BF), [(0, 1), (1, 2)])
        left = move_z(add(piece(z - 2), first, z == 2).astype(BF), [(3, 2), (2, 1)])
        right = move_z(add(piece(1 + z), right).astype(BF), [(0, 1), (1, 2), (2, 3)])
        left = move_z(add(piece(z - 1), left).astype(BF), [(3, 2), (2, 1), (1, 0)])
        return add(add(piece(z), right), left)

    def finish(total, part):
        bias = lax.dynamic_slice_in_dim(query_key_value_bias[part], z * per_z, per_z, 0)
        return (total + bias[None]).astype(BF)

    def project(part):
        sent = swap_req(partial_sums(x_other, part, slice(half, 2 * half)).astype(BF), 1)
        total = partial_sums(x_own, part, slice(0, half)) + sent.astype(F32)
        return finish(reduce_z(total), part)

    with jax.named_scope("decode_rows"):
        dec = jnp.stack([partial_sums(x_dec, part, slice(4 * CHUNK, None)) for part in range(3)], axis=1)
        dec = dec.reshape(NZ, 2, DEC, 3, feats)
        dec = jnp.stack([lax.dynamic_index_in_dim(dec, zz ^ m, 0, keepdims=False) for zz in range(NZ)])
        dec = lax.dynamic_index_in_dim(dec, c, 1, keepdims=False) + swap_req(
            lax.dynamic_index_in_dim(dec, 1 - c, 1, keepdims=False), 1
        )
        hi = z >> 1
        dec = lax.dynamic_slice_in_dim(dec, 2 * hi, 2, 0) + swap_req(
            lax.dynamic_slice_in_dim(dec, 2 * (1 - hi), 2, 0), 4
        )
        lo = z & 1
        dec = lax.dynamic_index_in_dim(dec, lo, 0, keepdims=False) + swap_req(
            lax.dynamic_index_in_dim(dec, 1 - lo, 0, keepdims=False), 2
        )
        dec = (dec + query_key_value_bias[None]).astype(BF)
    with jax.named_scope("decode_attention"):
        dec_out = decode_attention(cache_length_list, dec[:, 0:1], dec[:, 1:2], dec[:, 2:3], cache)
        dec_all = dec_out.reshape(DEC, feats)
        for bits in (1, 2, 4):
            dec_all = jnp.concatenate([dec_all, swap_req(dec_all, bits)], axis=0)

    with jax.named_scope("keys"):
        keys = project(1)
    with jax.named_scope("values"):
        values = project(2)
    with jax.named_scope("queries"):
        queries = project(0)
    with jax.named_scope("prompt_attention"):
        attended = prompt_attention(
            queries,
            keys,
            swap_req(keys, 1),
            values,
            swap_req(values, 1),
            row_code[:half, None],
            row_code[None, :],
        )
    with jax.named_scope("gather_attended"):
        own = gather_z(attended)
        other = [swap_req(v, 1) for v in own]
    with jax.named_scope("out_project"):
        where_to = home_spot[:, :prompt_rows].reshape(NZ, 2, 2, prompt_rows // 2)
        where_to = where_to.transpose(1, 2, 0, 3).reshape(NM, NZ * prompt_rows // 2)
        dec_to = 4 * CHUNK + (order[:, None] ^ r) * DEC + dec_ids
        dec_to = dec_to.reshape(NZ, 2, DEC).transpose(1, 2, 0).reshape(NM, NZ)
        tail = jnp.full((NM, 4), -1, i32)
        pos = jnp.concatenate([where_to, dec_to, tail], axis=1)
        quarter_rows = pos.shape[1]
        mixed = out_project(place, own, other, dec_all, output_weight, pos.reshape(-1, 1))
        mixed = mixed.reshape(NM, quarter_rows, -1)
    with jax.named_scope("sum_mp"):

        def share(k):
            return lax.dynamic_index_in_dim(mixed, m ^ k, 0, keepdims=False)

        total = share(0).astype(F32)
        for k in range(1, NM):
            total = total + swap_mp(share(k), k).astype(F32)
        total = total.astype(BF)
    with jax.named_scope("return_z"):
        n = prompt_rows // 2
        grid = jnp.concatenate(
            [
                total[: NZ * n].reshape(NZ, n, -1),
                jnp.pad(total[NZ * n : NZ * n + NZ].reshape(NZ, 1, -1), ((0, 0), (0, 7), (0, 0))),
            ],
            axis=1,
        )

        def for_z(k):
            return lax.dynamic_index_in_dim(grid, z ^ k, 0, keepdims=False)

        got = jnp.stack([for_z(0)] + [swap_req(for_z(k), 2 * k) for k in range(1, NZ)])
    with jax.named_scope("return_plane"):
        corner = 2 * c + (m & 1)
        parts = []
        for k in range(NM):
            hops = []
            for zz in range(NZ):
                for cc in range(2):
                    for mm in range(NM):
                        h, l = mm >> 1, mm & 1
                        hops.append(((zz * 2 + cc) * NM + mm, (zz * 2 + h) * NM + ((2 * cc + l) ^ k)))
            piece = lax.dynamic_index_in_dim(got, corner ^ k ^ z, 0, keepdims=False)
            parts.append(lax.ppermute(piece, ("req", "mp"), hops))
        parts = jnp.stack(parts)

        def corner_part(cc, l):
            return lax.dynamic_index_in_dim(parts, (2 * cc + l) ^ m, 0, keepdims=False)

        columns = []
        for cc in range(2):
            a, b = corner_part(cc, 0), corner_part(cc, 1)
            columns.append(jnp.concatenate([a[:n], b[:n], a[n : n + 1], b[n : n + 1]], axis=0))
        summed = jnp.concatenate(columns, axis=1).astype(F32)
        return (tokens.astype(F32) + summed + output_bias[None]).astype(BF)


def layer_norm(row_data, gain_vec, shift_vec):
    values = row_data.astype(jnp.float32)
    average = jnp.mean(values, axis=-1, keepdims=True)
    centred = values - average
    variance = jnp.mean(centred * centred, axis=-1, keepdims=True)
    scaled = centred * lax.rsqrt(variance + 1e-05)
    return (scaled * gain_vec + shift_vec).astype(jnp.bfloat16)


def on_device(
    tokens,
    layernorm_scale,
    layernorm_bias,
    query_key_value_weight,
    query_key_value_bias,
    adapter_down_weight,
    adapter_up_weight,
    adapter_index_table,
    prompt_length_list,
    cache,
    cache_length_list,
    output_weight,
    output_bias,
):
    rows_dev = tokens.shape[0]
    part_cols = tokens.shape[1]
    decode_count = cache.shape[0]
    slot_count = prompt_length_list.shape[0]
    prompt_rows = rows_dev - decode_count
    slot_len = prompt_rows // slot_count
    rank_size = ADAPTER_RANK
    head_count = query_key_value_weight.shape[2] // HEAD_DIM
    score_scale = HEAD_DIM ** (-0.5)
    gathered = lax.all_gather(tokens, "mp", axis=1, tiled=True)
    normed = layer_norm(gathered, layernorm_scale, layernorm_bias)
    column = lax.axis_index("mp")
    slice_m = lax.dynamic_slice_in_dim(normed, column * part_cols, part_cols, 1)
    spread = lax.all_to_all(normed, "req", split_axis=1, concat_axis=0, tiled=True)
    projected = lax.psum_scatter(
        jnp.einsum(
            "rd,cde->rce", spread, query_key_value_weight, preferred_element_type=jnp.float32
        ),
        "req",
        scatter_dimension=0,
        tiled=True,
    )
    projected = projected + query_key_value_bias[None]
    positions = jnp.arange(rows_dev)
    request_slot = jnp.where(
        positions < prompt_rows, positions // slot_len, slot_count + positions - prompt_rows
    )
    slot_match = request_slot[:, None] == jnp.arange(slot_count + decode_count)[None, :]
    row_adapter = jnp.sum(jnp.where(slot_match, adapter_index_table[0][None, :], 0), axis=1)
    adapter_on_device = adapter_down_weight.shape[0]
    owners = lax.axis_size("req")
    owner_row = row_adapter // adapter_on_device
    to_owner = owner_row[None, :] == jnp.arange(owners)[:, None]
    outgoing = jnp.where(to_owner[:, :, None], slice_m[None], jnp.zeros((), jnp.bfloat16))
    labels = jnp.where(to_owner, (row_adapter - owner_row * adapter_on_device)[None, :], -1)
    received_rows = lax.all_to_all(outgoing, "req", split_axis=0, concat_axis=0, tiled=True)
    arrived_labels = lax.all_to_all(labels, "req", split_axis=0, concat_axis=0, tiled=True)
    sources, items = arrived_labels.shape
    selection_mask = (
        arrived_labels[:, :, None] == jnp.arange(adapter_on_device)[None, None, :]
    ).astype(jnp.float32)
    adapter_wise_sums = jnp.einsum(
        "yju,ouv->yjov", received_rows, adapter_down_weight, preferred_element_type=jnp.float32
    )
    reduced_rank_rows = jnp.einsum("ogf,ogft->ogt", selection_mask, adapter_wise_sums)
    reduced_rank_rows = lax.psum(reduced_rank_rows, "mp").astype(jnp.bfloat16)
    broadcast_rank_rows = selection_mask.astype(jnp.bfloat16)[
        :, :, :, None, None
    ] * reduced_rank_rows.reshape(sources, items, 1, 2, rank_size)
    corrections = jnp.einsum(
        "pqwgd,wgdx->pqgx",
        broadcast_rank_rows,
        adapter_up_weight,
        preferred_element_type=jnp.float32,
    ).astype(jnp.bfloat16)
    returned = lax.all_to_all(corrections, "req", split_axis=0, concat_axis=0, tiled=True)
    adapter_delta = jnp.sum(returned.astype(jnp.float32), axis=0)
    queries = (projected[:, 0] + adapter_delta[:, 0]).astype(jnp.bfloat16)
    keys_new = projected[:, 1].astype(jnp.bfloat16)
    values_new = (projected[:, 2] + adapter_delta[:, 1]).astype(jnp.bfloat16)
    prompt_q = queries[:prompt_rows].reshape(slot_count, slot_len, head_count, HEAD_DIM)
    prompt_k = keys_new[:prompt_rows].reshape(slot_count, slot_len, head_count, HEAD_DIM)
    prompt_v = values_new[:prompt_rows].reshape(slot_count, slot_len, head_count, HEAD_DIM)
    scores = (
        jnp.einsum("sihd,sjhd->shij", prompt_q, prompt_k, preferred_element_type=jnp.float32)
        * score_scale
    )
    causal = jnp.arange(slot_len)[None, :] <= jnp.arange(slot_len)[:, None]
    scores = jnp.where(causal[None, None], scores, -1e30)
    highest = jnp.max(scores, axis=3, keepdims=True)
    weights = jnp.where(causal[None, None], jnp.exp(scores - highest), 0.0)
    weights = (weights / jnp.sum(weights, axis=3, keepdims=True)).astype(jnp.bfloat16)
    prompt_out = jnp.einsum(
        "shij,sjhd->sihd", weights, prompt_v, preferred_element_type=jnp.float32
    )
    active = jnp.arange(slot_len)[None, :] < prompt_length_list[:, None]
    prompt_out = (
        jnp.where(active[:, :, None, None], prompt_out, 0.0)
        .astype(jnp.bfloat16)
        .reshape(prompt_rows, -1)
    )
    cache_len = cache.shape[1]
    decode_q = queries[prompt_rows:].reshape(decode_count, head_count, HEAD_DIM)
    decode_k = keys_new[prompt_rows:].reshape(decode_count, head_count, HEAD_DIM)
    decode_v = values_new[prompt_rows:].reshape(decode_count, head_count, HEAD_DIM)
    keys_old = cache[:, :, 0].reshape(decode_count, cache_len, head_count, HEAD_DIM)
    values_old = cache[:, :, 1].reshape(decode_count, cache_len, head_count, HEAD_DIM)
    cache_scores = (
        jnp.einsum("dhe,dthe->dht", decode_q, keys_old, preferred_element_type=jnp.float32)
        * score_scale
    )
    live_cache = jnp.arange(cache_len)[None, None, :] < cache_length_list[:, None, None]
    cache_scores = jnp.where(live_cache, cache_scores, -1e30)
    self_score = (
        jnp.einsum("dhe,dhe->dh", decode_q, decode_k, preferred_element_type=jnp.float32)
        * score_scale
    )
    row_top = jnp.maximum(jnp.max(cache_scores, axis=2), self_score)
    cache_weights = jnp.where(live_cache, jnp.exp(cache_scores - row_top[:, :, None]), 0.0)
    self_weight = jnp.exp(self_score - row_top)
    totals = jnp.sum(cache_weights, axis=2) + self_weight
    cache_weights = (cache_weights / totals[:, :, None]).astype(jnp.bfloat16)
    self_weight = (self_weight / totals).astype(jnp.bfloat16)
    decode_out = jnp.einsum(
        "dht,dthe->dhe", cache_weights, values_old, preferred_element_type=jnp.float32
    )
    decode_out = decode_out + self_weight.astype(jnp.float32)[:, :, None] * decode_v.astype(
        jnp.float32
    )
    decode_out = decode_out.astype(jnp.bfloat16).reshape(decode_count, -1)
    attended = jnp.concatenate([prompt_out, decode_out], axis=0)
    mixed = jnp.dot(
        attended,
        lax.all_gather(output_weight, "req", axis=1, tiled=True),
        preferred_element_type=jnp.float32,
    )
    summed = lax.psum_scatter(
        mixed.astype(jnp.bfloat16), "mp", scatter_dimension=1, tiled=True
    ).astype(jnp.float32)
    return (tokens.astype(jnp.float32) + summed + output_bias[None]).astype(jnp.bfloat16)


def solution(mesh):
    placed = (
        P("req", "mp"),
        P(),
        P(),
        P(None, "req", "mp"),
        P(None, "mp"),
        P("req", "mp", None),
        P("req", None, None, "mp"),
        P("req", None),
        P("req"),
        P("req", None, None, "mp"),
        P("req"),
        P("mp", "req"),
        P("mp"),
    )
    quick = mesh.shape["req"] == 2 * NZ and mesh.shape["mp"] == NM
    return jax.shard_map(
        packed_device if quick else on_device, mesh=mesh, in_specs=placed, out_specs=P("req", "mp"), check_vma=False
    )
```

```python
import functools

import jax
import jax.numpy as jnp
from jax import lax
from jax.experimental import pallas as pl
from jax.experimental.pallas import tpu as pltpu
from jax.sharding import PartitionSpec as P

HEAD_DIM = 128
ADAPTER_RANK = 16
BF = jnp.bfloat16
F32 = jnp.float32
MIB = 1 << 20

NZ, NM = 4, 4
SLOTS, PLEN, DEC = 3, 32, 2
QROWS = 24
STAT_ROW = 26
BLK = 32
CHUNK = 128
DCH = 16
PACKED = NM * CHUNK + 2 * NZ * DEC
LANES = 128
DECODE_ROWS = 16
SMALL = pl.CostEstimate(flops=1, bytes_accessed=1, transcendentals=0)
VMEM = pl.BlockSpec(memory_space=pltpu.VMEM)
SMEM = pl.BlockSpec(memory_space=pltpu.SMEM)
ANY = pl.BlockSpec(memory_space=pl.ANY)


def swap_req(x, bits):
    return lax.ppermute(x, "req", [(i, i ^ bits) for i in range(2 * NZ)])


def swap_mp(x, bits):
    return lax.ppermute(x, "mp", [(i, i ^ bits) for i in range(NM)])


def gather_z(x):
    far, near = swap_req(x, 4), swap_req(x, 2)
    return [x, near, far, swap_req(far, 2)]


def gather_mp(x):
    one, two = swap_mp(x, 1), swap_mp(x, 2)
    return [x, one, two, swap_mp(one, 2)]


def limit(mib):
    return pltpu.CompilerParams(vmem_limit_bytes=mib * MIB)


def iota(shape, axis):
    return lax.broadcasted_iota(jnp.int32, shape, axis)


def three(x):
    a = x.astype(BF)
    rest = x - a.astype(F32)
    b = rest.astype(BF)
    return [a.astype(F32), b.astype(F32), (rest - b.astype(F32)).astype(BF).astype(F32)]


class Source:
    def __init__(self, s_ref, t_ref, j):
        z, core = s_ref[3], s_ref[6]
        self.z = jnp.bitwise_xor(z, j % NZ)
        self.core = jnp.bitwise_xor(core, j // NZ)
        self.index = self.z * 2 + self.core
        self.lens = [t_ref[j, i] for i in range(SLOTS)]
        self.adapters = [t_ref[j, SLOTS + i] for i in range(SLOTS + DEC)]
        self.live = self.lens[0] + self.lens[1] + self.lens[2]
        self.size = (self.live + 3) >> 2


def sources(s_ref, t_ref):
    found = [Source(s_ref, t_ref, j) for j in range(2 * NZ)]
    for a in found:
        a.offset = sum(jnp.where(b.index < a.index, b.size, 0) for b in found)
    return found


def by_slot(h, values):
    out = jnp.full_like(h, -1)
    for j in range(SLOTS):
        out = jnp.where((h >> 5) == j, values[j], out)
    return out


def chunk_places(found, other, t, seg, m):
    out = jnp.full_like(t, -1)
    for k in range(NZ):
        a = found[other * NZ + k]
        have = jnp.clip(a.live - m * a.size, 0, a.size)
        prompt = jnp.where(t < have, a.offset + t, -1)
        decode = jnp.where((t < QROWS + DEC) & (a.z == m), CHUNK + a.core * DEC + t - QROWS, -1)
        out = jnp.where(seg == k, jnp.where(t < QROWS, prompt, decode), out)
    return out


def packed_places(a, j, h, m, core):
    i = h & (PLEN - 1)
    starts = [0, a.lens[0], a.lens[0] + a.lens[1]]
    index = by_slot(h, starts) + i
    quarter = sum((index >= q * a.size).astype(jnp.int32) for q in range(1, NM))
    spot = jnp.bitwise_xor(quarter, m) * CHUNK + a.offset + index - quarter * a.size
    half = 2 * CHUNK
    spot = jnp.bitwise_xor(spot >> 8, core) * half + (spot & (half - 1))
    prompt = jnp.where(i < by_slot(h, a.lens), spot, -1)
    first = SLOTS * PLEN
    decode = jnp.where(h < first + DEC, NM * CHUNK + j * DEC + h - first, -1)
    return jnp.where(h < first, prompt, decode)


def home_adapters(a, h):
    out = by_slot(h, a.adapters)
    for j in range(DEC):
        out = jnp.where(h == SLOTS * PLEN + j, a.adapters[SLOTS + j], out)
    return out


def deal_kernel(s_ref, x_ref, *outs):
    len0, len1, len2, z, m = [s_ref[i] for i in range(5)]
    size = (len0 + len1 + len2 + 3) >> 2
    rows, cols = x_ref.shape
    prompt_rows = SLOTS * PLEN
    t, h = iota((BLK, rows), 0), iota((BLK, rows), 1)
    slot, i = h >> 5, h & (PLEN - 1)
    start = jnp.where(slot == 0, 0, jnp.where(slot == 1, len0, len0 + len1))
    length = jnp.where(slot == 0, len0, jnp.where(slot == 1, len1, len2))
    live = (i < length) & (h < prompt_rows) & (t < size)
    x = x_ref[...]
    wide = x.astype(F32)
    mean = jnp.sum(wide, axis=1, keepdims=True) / cols
    spread = jnp.sum((wide - mean) ** 2, axis=1, keepdims=True)
    lane = iota((rows, LANES), 1)
    stats = jnp.zeros((rows, LANES), F32)
    for j, term in enumerate(three(mean) + three(spread)):
        stats = jnp.where(lane == 2 + j, term, stats)
    same = (iota((rows, LANES), 0) == lane).astype(BF)
    turned = lax.dot_general(stats.astype(BF), same, (((0,), (0,)), ((), ())), preferred_element_type=F32)
    turned = jnp.concatenate([jnp.zeros((8, LANES), F32), turned[:8]], axis=0)
    for k, out in enumerate(outs):
        q = jnp.bitwise_xor(m, k)
        mine = live & (start + i - q * size == t)
        decode = (h >= prompt_rows) & (t == QROWS + h - prompt_rows) & (q == z)
        y = jnp.dot((mine | decode).astype(BF), x, preferred_element_type=F32)
        out[...] = y.astype(BF)
        out[16:32, :LANES] = (y[16:32, :LANES] + turned).astype(BF)


def deal(scalars, tokens):
    return pl.pallas_call(
        deal_kernel,
        out_shape=[jax.ShapeDtypeStruct((BLK, tokens.shape[1]), BF)] * NM,
        in_specs=[SMEM, VMEM],
        out_specs=[VMEM] * NM,
        compiler_params=limit(24),
        cost_estimate=SMALL,
        name="deal_rows",
    )(scalars, tokens)


def norm_kernel(s_ref, b0, b1, b2, b3, gain_ref, shift_ref, table_ref, _, __, o0, o1, o2, o3, held):
    z, m = s_ref[3], s_ref[4]
    cols = b0.shape[1]
    for k, ref in enumerate((b0, b1, b2, b3)):
        held[k] = ref[...].astype(F32)
    width = NM * cols
    means, spreads = [], []
    for k in range(NM):
        part = held[k, 24:32, :LANES]
        means.append(part[2:3] + part[3:4] + part[4:5])
        spreads.append(part[5:6] + part[6:7] + part[7:8])
    mean = sum(means) / NM
    var = (sum(spreads) + cols * sum((v - mean) ** 2 for v in means)) / width
    row = iota((BLK, LANES), 0)
    extra = []
    for value in (mean, lax.rsqrt(var + 1e-05)):
        block = jnp.zeros((BLK, LANES), F32)
        for j, term in enumerate(three(value)):
            block = jnp.where(row == STAT_ROW + j, term, block)
        extra.append(block)
    extra = jnp.concatenate(extra, axis=1)
    extra = jnp.where(iota(extra.shape, 0) == BLK - 1, table_ref[:, : 2 * LANES], extra)
    mean = sum(jnp.sum(held[k], axis=1, keepdims=True) for k in range(NM)) / width
    var = sum(jnp.sum((held[k] - mean) ** 2, axis=1, keepdims=True) for k in range(NM)) / width
    rstd = lax.rsqrt(var + 1e-05)
    last = iota((BLK, cols), 0) == BLK - 1
    stats = iota((BLK, 2 * LANES), 0) >= STAT_ROW
    for k, out in enumerate((o0, o1, o2, o3)):
        block = jnp.bitwise_xor(z, k)
        x = held[jnp.bitwise_xor(block, m)]
        y = (x - mean) * rstd * gain_ref[block] + shift_ref[block]
        y = jnp.where(last, table_ref[...], y)
        out[...] = y.astype(BF)
        out[:, : 2 * LANES] = jnp.where(stats, extra, y[:, : 2 * LANES]).astype(BF)


def norm_rows(scalars, blocks, gain, shift, table, near, far):
    return pl.pallas_call(
        norm_kernel,
        out_shape=[jax.ShapeDtypeStruct(blocks[0].shape, BF)] * NZ,
        in_specs=[SMEM] + [VMEM] * 7 + [ANY] * 2,
        out_specs=[VMEM] * NZ,
        scratch_shapes=[pltpu.VMEM((NM,) + blocks[0].shape, F32)],
        compiler_params=limit(32),
        cost_estimate=SMALL,
        name="norm_rows",
    )(scalars, *blocks, gain, shift, table, near, far)


def pack_kernel(s_ref, t_ref, a_ref, b_ref, o_ref):
    found = sources(s_ref, t_ref)
    half = a_ref.shape[0]
    lane = iota((1, half), 1)
    total = None
    for other, ref in enumerate((a_ref, b_ref)):
        to = chunk_places(found, other, lane & (BLK - 1), lane // BLK, s_ref[4])
        pick = (iota((o_ref.shape[0], half), 0) == to).astype(BF)
        term = jnp.dot(pick, ref[...], preferred_element_type=F32)
        total = term if total is None else total + term
    o_ref[...] = total.astype(BF)


def pack_rows(scalars, tables, mine, theirs):
    return pl.pallas_call(
        pack_kernel,
        out_shape=jax.ShapeDtypeStruct((CHUNK + DCH, mine.shape[1]), BF),
        in_specs=[SMEM] * 2 + [VMEM] * 2,
        out_specs=VMEM,
        compiler_params=limit(16),
        cost_estimate=SMALL,
        name="pack_rows",
    )(scalars, tables, mine, theirs)


def code_kernel(s_ref, t_ref, col_ref, row_ref):
    found = sources(s_ref, t_ref)
    m, core = s_ref[4], s_ref[6]
    n = NM * CHUNK
    lane, sub = iota((1, LANES), 1), iota((LANES, 1), 0)
    down, across = iota((n, LANES), 0), iota((LANES, n), 1)
    cols, rows = jnp.zeros((n, 1), jnp.int32), jnp.zeros((1, n), jnp.int32)
    for j, a in enumerate(found):
        first = a.index * SLOTS * PLEN + 1
        hit = down == packed_places(a, j, lane, m, core)
        cols = cols + jnp.sum(jnp.where(hit, first + lane, 0), axis=1, keepdims=True)
        hit = across == packed_places(a, j, sub, m, core)
        rows = rows + jnp.sum(jnp.where(hit, first + sub, 0), axis=0, keepdims=True)
    unused = (1 << 16) + PLEN * iota((n, 1), 0)
    col_ref[...] = jnp.where(cols > 0, cols - 1, unused)
    unused = (1 << 16) + PLEN * iota((1, n), 1)
    row_ref[...] = jnp.where(rows > 0, rows - 1, unused)


def packed_codes(scalars, tables):
    n = NM * CHUNK
    return pl.pallas_call(
        code_kernel,
        out_shape=[jax.ShapeDtypeStruct((n, 1), jnp.int32), jax.ShapeDtypeStruct((1, n), jnp.int32)],
        in_specs=[SMEM] * 2,
        out_specs=[VMEM] * 2,
        compiler_params=limit(16),
        cost_estimate=SMALL,
        name="packed_codes",
    )(scalars, tables)


def rank_kernel(s_ref, table_ref, da_ref, db_ref, x0, x1, x2, x3, t0, t1, t2, t3, gain_ref, shift_ref, o_ref):
    m, r = s_ref[4], s_ref[5]
    width = 2 * ADAPTER_RANK
    count = da_ref.shape[0] // width
    rows = x0.shape[0]
    same = (iota((rows, LANES), 0) == iota((rows, LANES), 1)).astype(BF)
    o_ref[...] = jnp.zeros_like(o_ref)
    for k, (x, stats) in enumerate(zip((x0, x1, x2, x3), (t0, t1, t2, t3))):

        def column(at):
            turned = lax.dot_general(
                same, stats[16:32, at], (((1,), (1,)), ((), ())), preferred_element_type=F32
            )
            j = STAT_ROW - 16
            return turned[:, j : j + 1] + turned[:, j + 1 : j + 2] + turned[:, j + 2 : j + 3]

        mean, rstd = column(slice(0, LANES)), column(slice(LANES, 2 * LANES))
        normed = ((x[...].astype(F32) - mean) * rstd * gain_ref[m] + shift_ref[m]).astype(BF)
        ids = home_adapters(Source(s_ref, table_ref, k), iota((1, rows), 1))
        total = jnp.zeros((width, rows), F32)
        for core, d in enumerate((da_ref, db_ref)):
            y = lax.dot_general(d[...], normed, (((1,), (1,)), ((), ())), preferred_element_type=F32)
            first = jnp.bitwise_xor(r, core) * count
            for a in range(count):
                total = total + jnp.where(ids == first + a, y[a * width : (a + 1) * width], 0.0)
        o_ref[:, k * LANES : k * LANES + rows] = total


def low_rank_rows(scalars, tables, down, down_other, pieces, stats, gain, shift):
    return pl.pallas_call(
        rank_kernel,
        out_shape=jax.ShapeDtypeStruct((2 * ADAPTER_RANK, NZ * LANES), F32),
        in_specs=[SMEM] * 2 + [VMEM] * 12,
        out_specs=VMEM,
        compiler_params=limit(32),
        cost_estimate=SMALL,
        name="low_rank_rows",
    )(scalars, tables, down, down_other, *pieces, *stats, gain, shift)


def expand_kernel(s_ref, t_ref, low_ref, low_other_ref, _, o_ref, *, count):
    m, r, core = s_ref[4], s_ref[5], s_ref[6]
    found = sources(s_ref, t_ref)
    width = count * ADAPTER_RANK
    repeat = []
    for t in range(2):
        shape = (width, 2 * ADAPTER_RANK)
        repeat.append((iota(shape, 1) == t * ADAPTER_RANK + iota(shape, 0) % ADAPTER_RANK).astype(BF))
    repeat = jnp.concatenate(repeat, axis=0)
    adapter = r * count + (iota((2 * width, LANES), 0) % width) // ADAPTER_RANK
    lane = iota((1, LANES), 1)
    total = jnp.zeros((PACKED, 2 * width), F32)
    for j, a in enumerate(found):
        ref = low_other_ref if j >= NZ else low_ref
        k = j % NZ
        low = jnp.dot(repeat, ref[:, k * LANES : (k + 1) * LANES], preferred_element_type=F32)
        low = jnp.where(adapter == home_adapters(a, lane), low, 0.0).astype(BF)
        hit = (iota((PACKED, LANES), 0) == packed_places(a, j, lane, m, core)).astype(BF)
        total = total + lax.dot_general(hit, low, (((1,), (1,)), ((), ())), preferred_element_type=F32)
    o_ref[0] = total[:, :width].astype(BF)
    o_ref[1] = total[:, width:].astype(BF)


def expand_rows(scalars, tables, low, low_other, count, after):
    return pl.pallas_call(
        functools.partial(expand_kernel, count=count),
        out_shape=jax.ShapeDtypeStruct((2, PACKED, count * ADAPTER_RANK), BF),
        in_specs=[SMEM] * 2 + [VMEM] * 2 + [ANY],
        out_specs=VMEM,
        compiler_params=limit(32),
        cost_estimate=SMALL,
        name="expand_rows",
    )(scalars, tables, low, low_other, after)


def emit_sums(y, own_ref, other_ref, dec_ref):
    half = 2 * CHUNK
    own_ref[...] = y[:half]
    other_ref[...] = y[half : 2 * half].astype(BF)
    dec_ref[...] = y[2 * half :]


def first_project_kernel(s_ref, c0, c1, c2, c3, w_ref, _, own_ref, other_ref, dec_ref, x):
    z, m, core = s_ref[3], s_ref[4], s_ref[6]

    @pl.when(pl.program_id(0) == 0)
    def _():
        chunks = (c0, c1, c2, c3)
        for k, chunk in enumerate(chunks):
            base = jnp.bitwise_xor(core, k >> 1) * 2 * CHUNK + (k & 1) * CHUNK
            x[pl.ds(pl.multiple_of(base, CHUNK), CHUNK), :] = chunk[:CHUNK, :]
        n, at = iota((2 * NZ * DEC, NM * DCH), 0), iota((2 * NZ * DEC, NM * DCH), 1)
        chip = jnp.bitwise_xor(z, (n >> 1) & 3)
        want = jnp.bitwise_xor(chip, m) * DCH + jnp.bitwise_xor(core, n >> 3) * DEC + (n & 1)
        rows = jnp.concatenate([chunk[CHUNK:, :] for chunk in chunks], axis=0)
        x[NM * CHUNK :, :] = jnp.dot((want == at).astype(BF), rows, preferred_element_type=F32).astype(BF)

    emit_sums(jnp.dot(x[...], w_ref[0], preferred_element_type=F32), own_ref, other_ref, dec_ref)


def project_rows(scalars, chunks, weight, part, after):
    _, depth, feats = weight.shape
    tile = feats // 2
    half = 2 * CHUNK
    whole = [pl.BlockSpec(v.shape, lambda j: (0, 0)) for v in chunks]
    out_shape = [
        jax.ShapeDtypeStruct((half, feats), F32),
        jax.ShapeDtypeStruct((half, feats), BF),
        jax.ShapeDtypeStruct((PACKED - 2 * half, feats), F32),
        jax.ShapeDtypeStruct((PACKED, depth), BF),
    ]
    out_specs = [pl.BlockSpec((v.shape[0], tile), lambda j: (0, j)) for v in out_shape[:3]]
    out_specs.append(pl.BlockSpec((PACKED, depth), lambda j: (0, 0)))
    return pl.pallas_call(
        first_project_kernel,
        grid=(feats // tile,),
        out_shape=out_shape,
        in_specs=[SMEM] + whole + [pl.BlockSpec((1, depth, tile), lambda j: (part, 0, j)), ANY],
        out_specs=out_specs,
        compiler_params=limit(56),
        cost_estimate=SMALL,
        name="project_keys",
    )(scalars, *chunks, weight, after)


def adapted_kernel(x_ref, w_ref, e_ref, u_ref, _, *outs):
    y = jnp.dot(x_ref[...], w_ref[0], preferred_element_type=F32)
    up = u_ref[...].reshape(-1, u_ref.shape[-1])
    y = y + jnp.dot(e_ref[0], up, preferred_element_type=F32)
    emit_sums(y, *outs)


def project_adapted(rows, weight, part, expanded, up, after):
    _, depth, feats = weight.shape
    tile = feats // 2
    half = 2 * CHUNK
    which = part // 2
    out_shape = [
        jax.ShapeDtypeStruct((half, feats), F32),
        jax.ShapeDtypeStruct((half, feats), BF),
        jax.ShapeDtypeStruct((PACKED - 2 * half, feats), F32),
    ]
    return pl.pallas_call(
        adapted_kernel,
        grid=(2,),
        out_shape=out_shape,
        in_specs=[
            pl.BlockSpec(rows.shape, lambda j: (0, 0)),
            pl.BlockSpec((1, depth, tile), lambda j: (part, 0, j)),
            pl.BlockSpec((1,) + expanded.shape[1:], lambda j: (which, 0, 0)),
            pl.BlockSpec((up.shape[0], 1, up.shape[2], tile), lambda j: (0, which, 0, j)),
            ANY,
        ],
        out_specs=[pl.BlockSpec((v.shape[0], tile), lambda j: (0, j)) for v in out_shape],
        compiler_params=limit(56),
        cost_estimate=SMALL,
        name="project_adapted",
    )(rows, weight, expanded, up, after)


def split_kernel(q_ref, k_ref, v_ref, _, keep_ref, send_ref):
    half = keep_ref.shape[0]
    feats = q_ref.shape[1]
    for j, ref in enumerate((q_ref, k_ref, v_ref)):
        at = slice(j * feats, (j + 1) * feats)
        keep_ref[:, at] = ref[:half, :]
        send_ref[:, at] = ref[half:, :]


def split_decode(parts, after):
    rows, feats = parts[0].shape
    out = jax.ShapeDtypeStruct((rows // 2, 3 * feats), F32)
    return pl.pallas_call(
        split_kernel,
        out_shape=[out, out],
        in_specs=[VMEM] * 3 + [ANY],
        out_specs=[VMEM] * 2,
        compiler_params=limit(16),
        cost_estimate=SMALL,
        name="split_decode",
    )(*parts, after)


def halve_kernel(s_ref, *refs, bit, groups):
    *ins, _, send_ref, keep_ref = refs
    count = len(ins) // 2
    side = (s_ref[3] >> bit) & 1
    to = 0
    for total_ref, got_ref in zip(ins[:count], ins[count:]):
        width = total_ref.shape[1] // groups // 2

        for g in range(groups):

            def part(which):
                at = pl.ds(pl.multiple_of((2 * g + which) * width, LANES), width)
                return total_ref[:, at] + got_ref[:, at].astype(F32)

            send_ref[:, to : to + width] = part(1 - side).astype(BF)
            keep_ref[:, to : to + width] = part(side)
            to += width


def halve(scalars, totals, gots, bit, after, groups=1):
    rows = totals[0].shape[0]
    feats = sum(v.shape[1] for v in totals) // 2
    return pl.pallas_call(
        functools.partial(halve_kernel, bit=bit, groups=groups),
        out_shape=[jax.ShapeDtypeStruct((rows, feats), BF), jax.ShapeDtypeStruct((rows, feats), F32)],
        in_specs=[SMEM] + [VMEM] * (2 * len(totals)) + [ANY],
        out_specs=[VMEM, VMEM],
        compiler_params=limit(16),
        cost_estimate=SMALL,
        name="halve_sums",
    )(scalars, *totals, *gots, after)


def finish_kernel(s_ref, total_ref, got_ref, bias_ref, _, *outs, parts):
    for j, (part, out) in enumerate(zip(parts, outs)):
        width = out.shape[1]
        at = pl.ds(pl.multiple_of(place_of(s_ref[3]) * width, LANES), width)
        mine = slice(j * width, (j + 1) * width)
        total = total_ref[:, mine] + got_ref[:, mine].astype(F32) + bias_ref[part : part + 1, at]
        out[...] = total.astype(BF)


def finish(scalars, total, got, bias, parts, after):
    rows, feats = total.shape
    return pl.pallas_call(
        functools.partial(finish_kernel, parts=parts),
        out_shape=[jax.ShapeDtypeStruct((rows, feats // len(parts)), BF)] * len(parts),
        in_specs=[SMEM, VMEM, VMEM, VMEM, ANY],
        out_specs=[VMEM] * len(parts),
        compiler_params=limit(16),
        cost_estimate=SMALL,
        name="finish_sums",
    )(scalars, total, got, bias, after)


def prompt_kernel(q_ref, ka_ref, kb_ref, va_ref, vb_ref, cr_ref, cc_ref, d0_ref, d1_ref, o_ref):
    rows = cr_ref[...]
    cols = cc_ref[...]
    allowed = ((rows >> 5) == (cols >> 5)) & (cols <= rows)
    keys = jnp.concatenate([ka_ref[...], kb_ref[...]], axis=0)
    values = jnp.concatenate([va_ref[...], vb_ref[...]], axis=0)
    for h in range(q_ref.shape[1] // HEAD_DIM):
        at = slice(h * HEAD_DIM, (h + 1) * HEAD_DIM)
        s = lax.dot_general(q_ref[:, at], keys[:, at], (((1,), (1,)), ((), ())), preferred_element_type=F32)
        s = jnp.where(allowed, s * HEAD_DIM**-0.5, -1e30)
        top = jnp.max(s, axis=1, keepdims=True)
        w = jnp.where(allowed, jnp.exp(s - top), 0.0)
        w = (w / jnp.sum(w, axis=1, keepdims=True)).astype(BF)
        o_ref[: q_ref.shape[0], at] = jnp.dot(w, values[:, at], preferred_element_type=F32).astype(BF)
    width = q_ref.shape[1]
    n = iota((DECODE_ROWS, width), 0)
    tail = jnp.zeros((DECODE_ROWS, width), F32)
    for b in range(NZ):
        for j, ref in enumerate((d0_ref, d1_ref)):
            tail = jnp.where(n == b * DEC + j, ref[:, b * width : (b + 1) * width].astype(F32), tail)
    o_ref[q_ref.shape[0] :, :] = tail.astype(BF)


def prompt_attention(q, ka, kb, va, vb, code_rows, code_cols, dec):
    return pl.pallas_call(
        prompt_kernel,
        out_shape=jax.ShapeDtypeStruct((q.shape[0] + DECODE_ROWS, q.shape[1]), BF),
        in_specs=[VMEM] * 9,
        out_specs=VMEM,
        compiler_params=limit(32),
        cost_estimate=SMALL,
        name="prompt_attention",
    )(q, ka, kb, va, vb, code_rows, code_cols, *dec)


def decode_kernel(len_ref, q_ref, k_ref, v_ref, c_ref, _, o_ref, qbd, top, total, acc):
    t = pl.program_id(0)
    span = c_ref.shape[1]
    live = len_ref[0]
    heads, feats = qbd.shape
    diag = lax.broadcasted_iota(jnp.int32, (heads, feats), 1) // HEAD_DIM == lax.broadcasted_iota(
        jnp.int32, (heads, feats), 0
    )

    @pl.when(t == 0)
    def _():
        q = jnp.where(diag, q_ref[0].astype(F32), 0.0)
        qbd[...] = q.astype(BF)
        own = jnp.sum(q * k_ref[0].astype(F32), axis=1, keepdims=True) * HEAD_DIM**-0.5
        top[...] = jnp.broadcast_to(own, top.shape)
        total[...] = jnp.ones_like(total)
        acc[...] = jnp.broadcast_to(v_ref[0].astype(F32), acc.shape)

    @pl.when(t * span < live)
    def _():
        x = c_ref[0].reshape(2 * span, feats)
        s = lax.dot_general(qbd[...], x, (((1,), (1,)), ((), ())), preferred_element_type=F32)
        column = lax.broadcasted_iota(jnp.int32, s.shape, 1)
        valid = (column % 2 == 0) & (t * span + column // 2 < live)
        s = jnp.where(valid, s * HEAD_DIM**-0.5, -1e30)
        before = top[:, :1]
        now = jnp.maximum(before, jnp.max(s, axis=1, keepdims=True))
        fade = jnp.exp(before - now)
        w = jnp.where(valid, jnp.exp(s - now), 0.0)
        total[...] = total[...] * fade + jnp.sum(w, axis=1, keepdims=True)
        top[...] = jnp.broadcast_to(now, top.shape)
        w = pltpu.roll(w, 1, 1).astype(BF)
        acc[...] = acc[...] * fade + jnp.dot(w, x, preferred_element_type=F32)

    @pl.when(t == pl.num_programs(0) - 1)
    def _():
        o = acc[...] / total[:, :1]
        o_ref[0] = jnp.sum(jnp.where(diag, o, 0.0), axis=0, keepdims=True).astype(BF)


def decode_attention(length, q, k, v, cache, which, after, span=256):
    _, positions, _, feats = cache.shape
    row = pl.BlockSpec((1, 1, feats), lambda t, n: (0, 0, 0))
    heads = 16
    return pl.pallas_call(
        decode_kernel,
        grid_spec=pltpu.PrefetchScalarGridSpec(
            num_scalar_prefetch=1,
            grid=(positions // span,),
            in_specs=[row, row, row]
            + [pl.BlockSpec((1, span, 2, feats), lambda t, n: (which, jnp.minimum(t, (n[0] - 1) // span), 0, 0)), ANY],
            out_specs=row,
            scratch_shapes=[
                pltpu.VMEM((heads, feats), BF),
                pltpu.VMEM((heads, LANES), F32),
                pltpu.VMEM((heads, LANES), F32),
                pltpu.VMEM((heads, feats), F32),
            ],
        ),
        out_shape=jax.ShapeDtypeStruct((1, 1, feats), BF),
        compiler_params=limit(32),
        cost_estimate=SMALL,
        name="decode_attention",
    )(length, q, k, v, cache, after)


def out_kernel(place_ref, *refs):
    own, other, w_ref, outs, mixed = refs[:4], refs[4:8], refs[8], refs[9:13], refs[13]
    z, m, core = place_ref[3], place_ref[4], place_ref[6]
    width = own[0].shape[1]
    half = own[0].shape[0] - DECODE_ROWS
    total = None
    for k in range(NZ):
        block = place_of(jnp.bitwise_xor(z, k))
        w = w_ref[pl.ds(pl.multiple_of(block * width, width), width), :]
        rows = jnp.concatenate([own[k][:half, :], other[k][:half, :]], axis=0)
        term = jnp.dot(rows, w, preferred_element_type=F32)
        total = term if total is None else total + term
    mixed[...] = total.astype(BF)
    tails = jnp.concatenate([v[half:, :] for v in own + other], axis=0)
    count = 2 * NZ * DEC
    n, at = iota((count, tails.shape[0]), 0), iota((count, tails.shape[0]), 1)
    total = None
    for b in range(NZ):
        pick = (at == (n // DEC) * DECODE_ROWS + b * DEC + n % DEC).astype(BF)
        rows = jnp.dot(pick, tails, preferred_element_type=F32).astype(BF)
        term = jnp.dot(rows, w_ref[b * width : (b + 1) * width, :], preferred_element_type=F32)
        total = term if total is None else total + term
    decode = total.astype(BF)
    n, at = iota((DCH, count), 0), iota((DCH, count), 1)
    for k, out in enumerate(outs):
        base = jnp.bitwise_xor(core, k >> 1) * 2 * CHUNK + (k & 1) * CHUNK
        out[:CHUNK, :] = mixed[pl.ds(pl.multiple_of(base, CHUNK), CHUNK), :]
        far = jnp.bitwise_xor(jnp.bitwise_xor(m, k), z)
        want = (jnp.bitwise_xor(core, n >> 1) * NZ + far) * DEC + (n & 1)
        pick = ((at == want) & (n < 2 * DEC)).astype(BF)
        out[CHUNK:, :] = jnp.dot(pick, decode, preferred_element_type=F32).astype(BF)


def out_project(scalars, own, other, weight):
    feats = weight.shape[1]
    return pl.pallas_call(
        out_kernel,
        out_shape=[jax.ShapeDtypeStruct((CHUNK + DCH, feats), BF)] * NM,
        in_specs=[SMEM] + [VMEM] * 9,
        out_specs=[VMEM] * NM,
        scratch_shapes=[pltpu.VMEM((NM * CHUNK, feats), BF)],
        compiler_params=limit(40),
        cost_estimate=SMALL,
        name="out_project",
    )(scalars, *own, *other, weight)


def unpack_kernel(s_ref, t_ref, c0, c1, c2, c3, *outs):
    total = sum(c[...].astype(F32) for c in (c0, c1, c2, c3)).astype(BF)
    found = sources(s_ref, t_ref)
    n = iota((NZ * BLK, 1), 0)
    for other in range(2):
        to = chunk_places(found, other, n & (BLK - 1), n // BLK, s_ref[4])
        pick = (iota((NZ * BLK, total.shape[0]), 1) == to).astype(BF)
        rows = jnp.dot(pick, total, preferred_element_type=F32).astype(BF)
        for k, out in enumerate(outs):
            out[other * BLK : (other + 1) * BLK, :] = rows[k * BLK : (k + 1) * BLK]


def unpack_rows(scalars, tables, chunks):
    feats = chunks[0].shape[1]
    return pl.pallas_call(
        unpack_kernel,
        out_shape=[jax.ShapeDtypeStruct((2 * BLK, feats), BF)] * NZ,
        in_specs=[SMEM] * 2 + [VMEM] * 4,
        out_specs=[VMEM] * NZ,
        compiler_params=limit(16),
        cost_estimate=SMALL,
        name="unpack_rows",
    )(scalars, tables, *chunks)


def join_kernel(s_ref, a0, a1, a2, a3, other_ref, o0, o1, o2, o3, held):
    z, m, core = s_ref[3], s_ref[4], s_ref[6]
    width = a0.shape[1]
    mine = pl.ds(pl.multiple_of(core * width, LANES), width)
    theirs = pl.ds(pl.multiple_of((1 - core) * width, LANES), width)
    for k, ref in enumerate((a0, a1, a2, a3)):
        held[k, :, mine] = ref[:BLK, :]
        held[k, :, theirs] = other_ref[k * BLK : (k + 1) * BLK, :]
    for k, out in enumerate((o0, o1, o2, o3)):
        out[...] = held[jnp.bitwise_xor(jnp.bitwise_xor(z, m), k)]


def join_halves(scalars, parts, other):
    shape = (BLK, 2 * parts[0].shape[1])
    return pl.pallas_call(
        join_kernel,
        out_shape=[jax.ShapeDtypeStruct(shape, BF)] * NM,
        in_specs=[SMEM] + [VMEM] * 5,
        out_specs=[VMEM] * NM,
        scratch_shapes=[pltpu.VMEM((NZ,) + shape, BF)],
        compiler_params=limit(16),
        cost_estimate=SMALL,
        name="join_halves",
    )(scalars, *parts, other)


def home_kernel(s_ref, x_ref, bias_ref, b0, b1, b2, b3, o_ref):
    len0, len1, len2, z, m = [s_ref[i] for i in range(5)]
    size = (len0 + len1 + len2 + 3) >> 2
    rows = x_ref.shape[0]
    prompt_rows = SLOTS * PLEN
    t, h = iota((rows, BLK), 1), iota((rows, BLK), 0)
    slot, i = h >> 5, h & (PLEN - 1)
    start = jnp.where(slot == 0, 0, jnp.where(slot == 1, len0, len0 + len1))
    length = jnp.where(slot == 0, len0, jnp.where(slot == 1, len1, len2))
    live = (i < length) & (h < prompt_rows) & (t < size)
    total = x_ref[...].astype(F32) + bias_ref[...]
    for k, ref in enumerate((b0, b1, b2, b3)):
        q = jnp.bitwise_xor(m, k)
        mine = live & (start + i - q * size == t)
        decode = (h >= prompt_rows) & (t == QROWS + h - prompt_rows) & (q == z)
        total = total + jnp.dot((mine | decode).astype(BF), ref[...], preferred_element_type=F32)
    o_ref[...] = total.astype(BF)


def add_home(scalars, tokens, bias, blocks):
    return pl.pallas_call(
        home_kernel,
        out_shape=jax.ShapeDtypeStruct(tokens.shape, BF),
        in_specs=[SMEM] + [VMEM] * 6,
        out_specs=VMEM,
        compiler_params=limit(24),
        cost_estimate=SMALL,
        name="add_home",
    )(scalars, tokens, bias, *blocks)


def place_of(z):
    return (z & 1) * 2 + (z >> 1)


def packed_device(
    tokens,
    layernorm_scale,
    layernorm_bias,
    query_key_value_weight,
    query_key_value_bias,
    adapter_down_weight,
    adapter_up_weight,
    adapter_index_table,
    prompt_length_list,
    cache,
    cache_length_list,
    output_weight,
    output_bias,
):
    i32 = jnp.int32
    r = lax.axis_index("req").astype(i32)
    m = lax.axis_index("mp").astype(i32)
    z, c = r >> 1, r & 1
    rows_dev, cols = tokens.shape
    prompt_rows = SLOTS * PLEN
    feats = query_key_value_weight.shape[2]
    depth = query_key_value_weight.shape[1]
    per_z = feats // NZ
    own_adapters = adapter_down_weight.shape[0]
    half = 2 * CHUNK
    order = jnp.arange(2 * NZ, dtype=i32)
    source = ((z ^ (order & 3)) << 1) + (c ^ (order >> 2))
    lens = prompt_length_list
    scalars = jnp.concatenate([lens, jnp.stack([z, m, r, c])])

    down = jnp.transpose(adapter_down_weight, (0, 2, 1)).reshape(own_adapters * 2 * ADAPTER_RANK, cols)
    down_other = swap_req(down, 1)

    with jax.named_scope("gather_home"):
        pieces = gather_z(tokens)

    with jax.named_scope("deal"):
        dealt = deal(scalars, tokens)
        blocks = [dealt[0]] + [swap_mp(dealt[k], k) for k in range(1, NM)]
    with jax.named_scope("norm_rows"):
        table = jnp.concatenate([lens, adapter_index_table[0]]).astype(F32)
        table = jnp.pad(table, (0, depth - table.shape[0]))
        table = jnp.tile(table, 2)[None, :]
        gain = layernorm_scale.reshape(NM, 1, cols)
        shift = layernorm_bias.reshape(NM, 1, cols)
        normed = norm_rows(scalars, blocks, gain, shift, table, pieces[1], pieces[2])
    with jax.named_scope("spread_z"):
        spread = [normed[0]] + [swap_req(normed[k], 2 * k) for k in range(1, NZ)]
        rows = jnp.concatenate(spread, axis=0)
        mine = lax.dynamic_slice_in_dim(rows, c * depth, depth, 1)
        theirs = swap_req(lax.dynamic_slice_in_dim(rows, (1 - c) * depth, depth, 1), 1)

    with jax.named_scope("tables"):
        tables = jnp.concatenate(
            [v.reshape(NZ, BLK, depth)[:, BLK - 1, : SLOTS + SLOTS + DEC] for v in (mine, theirs)], axis=0
        ).astype(i32)
    with jax.named_scope("pack"):
        chunk = pack_rows(scalars, tables, mine, theirs)
    with jax.named_scope("gather_chunks"):
        chunks = gather_mp(chunk)

    with jax.named_scope("codes"):
        code_col, code_row = packed_codes(scalars, tables)

    with jax.named_scope("low_rank"):
        part = low_rank_rows(scalars, tables, down, down_other, pieces, spread, gain, shift)
        two = part + swap_mp(part, 1)
        low_rank = (two + swap_mp(two, 2)).astype(BF)
    with jax.named_scope("keys"):
        own_k, other_k, dec_k, x_rows = project_rows(scalars, chunks, query_key_value_weight, 1, part)
        send_k, keep_k = halve(scalars, [own_k], [swap_req(other_k, 1)], 0, other_k)
        got_k = swap_req(send_k, 2)
    with jax.named_scope("low_rank"):
        expanded = expand_rows(scalars, tables, low_rank, swap_req(low_rank, 1), own_adapters, send_k)
    with jax.named_scope("values"):
        own_v, other_v, dec_v = project_adapted(x_rows, query_key_value_weight, 2, expanded, adapter_up_weight, send_k)
        core_v = swap_req(other_v, 1)
    with jax.named_scope("keys"):
        send_k, keep_k = halve(scalars, [keep_k], [got_k], 1, other_v)
        got_k = swap_req(send_k, 4)
    with jax.named_scope("queries"):
        own_q, other_q, dec_q = project_adapted(x_rows, query_key_value_weight, 0, expanded, adapter_up_weight, send_k)
        core_q = swap_req(other_q, 1)
    with jax.named_scope("keys"):
        (keys,) = finish(scalars, keep_k, got_k, query_key_value_bias, (1,), keep_k)
        keys_other = swap_req(keys, 1)
    with jax.named_scope("values_queries"):
        send, keep = halve(scalars, [own_v, own_q], [core_v, core_q], 0, keys)
        got = swap_req(send, 2)
    with jax.named_scope("decode_rows"):
        dec, dec_sent = split_decode((dec_q, dec_k, dec_v), send)
        dec = dec + swap_req(dec_sent, 1)
        for bits in (4, 2):
            count = dec.shape[0] // 2
            dec = dec[:count] + swap_req(dec[count:], bits)
        dec = (dec.reshape(DEC, 3, feats) + query_key_value_bias[None]).astype(BF)

    def decode_one(j, after):
        return decode_attention(
            cache_length_list[j : j + 1], dec[j : j + 1, 0:1], dec[j : j + 1, 1:2], dec[j : j + 1, 2:3], cache, j, after
        ).reshape(1, feats)

    with jax.named_scope("decode_attention"):
        dec_first = decode_one(0, send)
    with jax.named_scope("values_queries"):
        send, keep = halve(scalars, [keep], [got], 1, dec_first, groups=2)
        got = swap_req(send, 4)
    with jax.named_scope("decode_attention"):
        dec_second = decode_one(1, send)
    with jax.named_scope("values_queries"):
        values, queries = finish(scalars, keep, got, query_key_value_bias, (2, 0), dec_second)
        values_other = swap_req(values, 1)
    with jax.named_scope("prompt_attention"):
        attended = prompt_attention(
            queries,
            keys,
            keys_other,
            values,
            values_other,
            code_col[: 2 * CHUNK],
            code_row,
            (dec_first, dec_second),
        )
    with jax.named_scope("gather_attended"):
        own = gather_z(attended)
        other = [swap_req(v, 1) for v in own]
    with jax.named_scope("out_project"):
        mixed = out_project(scalars, own, other, output_weight)
    with jax.named_scope("sum_mp"):
        shares = [mixed[0]] + [swap_mp(mixed[k], k) for k in range(1, NM)]
    with jax.named_scope("return_z"):
        back = unpack_rows(scalars, tables, shares)
        back = [back[0]] + [swap_req(back[k], 2 * k) for k in range(1, NZ)]
        back_other = swap_req(jnp.concatenate([v[BLK:] for v in back], axis=0), 1)
    with jax.named_scope("return_plane"):
        joined = join_halves(scalars, back, back_other)
        joined = [joined[0]] + [swap_mp(joined[k], k) for k in range(1, NM)]
        return add_home(scalars, tokens, output_bias[None], joined)


def layer_norm(row_data, gain_vec, shift_vec):
    values = row_data.astype(jnp.float32)
    average = jnp.mean(values, axis=-1, keepdims=True)
    centred = values - average
    variance = jnp.mean(centred * centred, axis=-1, keepdims=True)
    scaled = centred * lax.rsqrt(variance + 1e-05)
    return (scaled * gain_vec + shift_vec).astype(jnp.bfloat16)


def on_device(
    tokens,
    layernorm_scale,
    layernorm_bias,
    query_key_value_weight,
    query_key_value_bias,
    adapter_down_weight,
    adapter_up_weight,
    adapter_index_table,
    prompt_length_list,
    cache,
    cache_length_list,
    output_weight,
    output_bias,
):
    rows_dev = tokens.shape[0]
    part_cols = tokens.shape[1]
    decode_count = cache.shape[0]
    slot_count = prompt_length_list.shape[0]
    prompt_rows = rows_dev - decode_count
    slot_len = prompt_rows // slot_count
    rank_size = ADAPTER_RANK
    head_count = query_key_value_weight.shape[2] // HEAD_DIM
    score_scale = HEAD_DIM ** (-0.5)
    gathered = lax.all_gather(tokens, "mp", axis=1, tiled=True)
    normed = layer_norm(gathered, layernorm_scale, layernorm_bias)
    column = lax.axis_index("mp")
    slice_m = lax.dynamic_slice_in_dim(normed, column * part_cols, part_cols, 1)
    spread = lax.all_to_all(normed, "req", split_axis=1, concat_axis=0, tiled=True)
    projected = lax.psum_scatter(
        jnp.einsum(
            "rd,cde->rce", spread, query_key_value_weight, preferred_element_type=jnp.float32
        ),
        "req",
        scatter_dimension=0,
        tiled=True,
    )
    projected = projected + query_key_value_bias[None]
    positions = jnp.arange(rows_dev)
    request_slot = jnp.where(
        positions < prompt_rows, positions // slot_len, slot_count + positions - prompt_rows
    )
    slot_match = request_slot[:, None] == jnp.arange(slot_count + decode_count)[None, :]
    row_adapter = jnp.sum(jnp.where(slot_match, adapter_index_table[0][None, :], 0), axis=1)
    adapter_on_device = adapter_down_weight.shape[0]
    owners = lax.axis_size("req")
    owner_row = row_adapter // adapter_on_device
    to_owner = owner_row[None, :] == jnp.arange(owners)[:, None]
    outgoing = jnp.where(to_owner[:, :, None], slice_m[None], jnp.zeros((), jnp.bfloat16))
    labels = jnp.where(to_owner, (row_adapter - owner_row * adapter_on_device)[None, :], -1)
    received_rows = lax.all_to_all(outgoing, "req", split_axis=0, concat_axis=0, tiled=True)
    arrived_labels = lax.all_to_all(labels, "req", split_axis=0, concat_axis=0, tiled=True)
    sources, items = arrived_labels.shape
    selection_mask = (
        arrived_labels[:, :, None] == jnp.arange(adapter_on_device)[None, None, :]
    ).astype(jnp.float32)
    adapter_wise_sums = jnp.einsum(
        "yju,ouv->yjov", received_rows, adapter_down_weight, preferred_element_type=jnp.float32
    )
    reduced_rank_rows = jnp.einsum("ogf,ogft->ogt", selection_mask, adapter_wise_sums)
    reduced_rank_rows = lax.psum(reduced_rank_rows, "mp").astype(jnp.bfloat16)
    broadcast_rank_rows = selection_mask.astype(jnp.bfloat16)[
        :, :, :, None, None
    ] * reduced_rank_rows.reshape(sources, items, 1, 2, rank_size)
    corrections = jnp.einsum(
        "pqwgd,wgdx->pqgx",
        broadcast_rank_rows,
        adapter_up_weight,
        preferred_element_type=jnp.float32,
    ).astype(jnp.bfloat16)
    returned = lax.all_to_all(corrections, "req", split_axis=0, concat_axis=0, tiled=True)
    adapter_delta = jnp.sum(returned.astype(jnp.float32), axis=0)
    queries = (projected[:, 0] + adapter_delta[:, 0]).astype(jnp.bfloat16)
    keys_new = projected[:, 1].astype(jnp.bfloat16)
    values_new = (projected[:, 2] + adapter_delta[:, 1]).astype(jnp.bfloat16)
    prompt_q = queries[:prompt_rows].reshape(slot_count, slot_len, head_count, HEAD_DIM)
    prompt_k = keys_new[:prompt_rows].reshape(slot_count, slot_len, head_count, HEAD_DIM)
    prompt_v = values_new[:prompt_rows].reshape(slot_count, slot_len, head_count, HEAD_DIM)
    scores = (
        jnp.einsum("sihd,sjhd->shij", prompt_q, prompt_k, preferred_element_type=jnp.float32)
        * score_scale
    )
    causal = jnp.arange(slot_len)[None, :] <= jnp.arange(slot_len)[:, None]
    scores = jnp.where(causal[None, None], scores, -1e30)
    highest = jnp.max(scores, axis=3, keepdims=True)
    weights = jnp.where(causal[None, None], jnp.exp(scores - highest), 0.0)
    weights = (weights / jnp.sum(weights, axis=3, keepdims=True)).astype(jnp.bfloat16)
    prompt_out = jnp.einsum(
        "shij,sjhd->sihd", weights, prompt_v, preferred_element_type=jnp.float32
    )
    active = jnp.arange(slot_len)[None, :] < prompt_length_list[:, None]
    prompt_out = (
        jnp.where(active[:, :, None, None], prompt_out, 0.0)
        .astype(jnp.bfloat16)
        .reshape(prompt_rows, -1)
    )
    cache_len = cache.shape[1]
    decode_q = queries[prompt_rows:].reshape(decode_count, head_count, HEAD_DIM)
    decode_k = keys_new[prompt_rows:].reshape(decode_count, head_count, HEAD_DIM)
    decode_v = values_new[prompt_rows:].reshape(decode_count, head_count, HEAD_DIM)
    keys_old = cache[:, :, 0].reshape(decode_count, cache_len, head_count, HEAD_DIM)
    values_old = cache[:, :, 1].reshape(decode_count, cache_len, head_count, HEAD_DIM)
    cache_scores = (
        jnp.einsum("dhe,dthe->dht", decode_q, keys_old, preferred_element_type=jnp.float32)
        * score_scale
    )
    live_cache = jnp.arange(cache_len)[None, None, :] < cache_length_list[:, None, None]
    cache_scores = jnp.where(live_cache, cache_scores, -1e30)
    self_score = (
        jnp.einsum("dhe,dhe->dh", decode_q, decode_k, preferred_element_type=jnp.float32)
        * score_scale
    )
    row_top = jnp.maximum(jnp.max(cache_scores, axis=2), self_score)
    cache_weights = jnp.where(live_cache, jnp.exp(cache_scores - row_top[:, :, None]), 0.0)
    self_weight = jnp.exp(self_score - row_top)
    totals = jnp.sum(cache_weights, axis=2) + self_weight
    cache_weights = (cache_weights / totals[:, :, None]).astype(jnp.bfloat16)
    self_weight = (self_weight / totals).astype(jnp.bfloat16)
    decode_out = jnp.einsum(
        "dht,dthe->dhe", cache_weights, values_old, preferred_element_type=jnp.float32
    )
    decode_out = decode_out + self_weight.astype(jnp.float32)[:, :, None] * decode_v.astype(
        jnp.float32
    )
    decode_out = decode_out.astype(jnp.bfloat16).reshape(decode_count, -1)
    attended = jnp.concatenate([prompt_out, decode_out], axis=0)
    mixed = jnp.dot(
        attended,
        lax.all_gather(output_weight, "req", axis=1, tiled=True),
        preferred_element_type=jnp.float32,
    )
    summed = lax.psum_scatter(
        mixed.astype(jnp.bfloat16), "mp", scatter_dimension=1, tiled=True
    ).astype(jnp.float32)
    return (tokens.astype(jnp.float32) + summed + output_bias[None]).astype(jnp.bfloat16)


def solution(mesh):
    placed = (
        P("req", "mp"),
        P(),
        P(),
        P(None, "req", "mp"),
        P(None, "mp"),
        P("req", "mp", None),
        P("req", None, None, "mp"),
        P("req", None),
        P("req"),
        P("req", None, None, "mp"),
        P("req"),
        P("mp", "req"),
        P("mp"),
    )
    quick = mesh.shape["req"] == 2 * NZ and mesh.shape["mp"] == NM
    return jax.shard_map(
        packed_device if quick else on_device, mesh=mesh, in_specs=placed, out_specs=P("req", "mp"), check_vma=False
    )
```

```python
import functools

import jax
import jax.numpy as jnp
from jax import lax
from jax.experimental import pallas as pl
from jax.experimental.pallas import tpu as pltpu
from jax.sharding import PartitionSpec as P

HEAD_DIM = 128
ADAPTER_RANK = 16
BF = jnp.bfloat16
F32 = jnp.float32
MIB = 1 << 20

NZ, NM = 4, 4
SLOTS, PLEN, DEC = 3, 32, 2
QROWS = 24
STAT_ROW = 26
BLK = 32
CHUNK = 128
DCH = 16
PACKED = NM * CHUNK + 2 * NZ * DEC
LANES = 128
DECODE_ROWS = 16
SMALL = pl.CostEstimate(flops=1, bytes_accessed=1, transcendentals=0)
VMEM = pl.BlockSpec(memory_space=pltpu.VMEM)
SMEM = pl.BlockSpec(memory_space=pltpu.SMEM)
ANY = pl.BlockSpec(memory_space=pl.ANY)


def swap_req(x, bits):
    return lax.ppermute(x, "req", [(i, i ^ bits) for i in range(2 * NZ)])


def swap_mp(x, bits):
    return lax.ppermute(x, "mp", [(i, i ^ bits) for i in range(NM)])


def gather_z(x):
    far, near = swap_req(x, 4), swap_req(x, 2)
    return [x, near, far, swap_req(far, 2)]


def gather_mp(x):
    one, two = swap_mp(x, 1), swap_mp(x, 2)
    return [x, one, two, swap_mp(one, 2)]


def limit(mib):
    return pltpu.CompilerParams(vmem_limit_bytes=mib * MIB)


def iota(shape, axis):
    return lax.broadcasted_iota(jnp.int32, shape, axis)


def three(x):
    a = x.astype(BF)
    rest = x - a.astype(F32)
    b = rest.astype(BF)
    return [a.astype(F32), b.astype(F32), (rest - b.astype(F32)).astype(BF).astype(F32)]


class Source:
    def __init__(self, s_ref, t_ref, j):
        z, core = s_ref[3], s_ref[6]
        self.z = jnp.bitwise_xor(z, j % NZ)
        self.core = jnp.bitwise_xor(core, j // NZ)
        self.index = self.z * 2 + self.core
        self.lens = [t_ref[j, i] for i in range(SLOTS)]
        self.adapters = [t_ref[j, SLOTS + i] for i in range(SLOTS + DEC)]
        self.live = self.lens[0] + self.lens[1] + self.lens[2]
        self.size = (self.live + 3) >> 2


def sources(s_ref, t_ref):
    found = [Source(s_ref, t_ref, j) for j in range(2 * NZ)]
    for a in found:
        a.offset = sum(jnp.where(b.index < a.index, b.size, 0) for b in found)
    return found


def by_slot(h, values):
    out = jnp.full_like(h, -1)
    for j in range(SLOTS):
        out = jnp.where((h >> 5) == j, values[j], out)
    return out


def chunk_places(found, other, t, seg, m):
    out = jnp.full_like(t, -1)
    for k in range(NZ):
        a = found[other * NZ + k]
        have = jnp.clip(a.live - m * a.size, 0, a.size)
        prompt = jnp.where(t < have, a.offset + t, -1)
        decode = jnp.where((t < QROWS + DEC) & (a.z == m), CHUNK + a.core * DEC + t - QROWS, -1)
        out = jnp.where(seg == k, jnp.where(t < QROWS, prompt, decode), out)
    return out


def packed_places(a, j, h, m, core):
    i = h & (PLEN - 1)
    starts = [0, a.lens[0], a.lens[0] + a.lens[1]]
    index = by_slot(h, starts) + i
    quarter = sum((index >= q * a.size).astype(jnp.int32) for q in range(1, NM))
    spot = jnp.bitwise_xor(quarter, m) * CHUNK + a.offset + index - quarter * a.size
    half = 2 * CHUNK
    spot = jnp.bitwise_xor(spot >> 8, core) * half + (spot & (half - 1))
    prompt = jnp.where(i < by_slot(h, a.lens), spot, -1)
    first = SLOTS * PLEN
    base = NM * CHUNK + (j // NZ * NZ + turned_bits(j % NZ)) * DEC - first
    decode = jnp.where(h < first + DEC, base + h, -1)
    return jnp.where(h < first, prompt, decode)


def home_adapters(a, h):
    out = by_slot(h, a.adapters)
    for j in range(DEC):
        out = jnp.where(h == SLOTS * PLEN + j, a.adapters[SLOTS + j], out)
    return out


def deal_kernel(s_ref, x_ref, *outs):
    len0, len1, len2, z, m = [s_ref[i] for i in range(5)]
    size = (len0 + len1 + len2 + 3) >> 2
    rows, cols = x_ref.shape
    prompt_rows = SLOTS * PLEN
    t, h = iota((BLK, rows), 0), iota((BLK, rows), 1)
    slot, i = h >> 5, h & (PLEN - 1)
    start = jnp.where(slot == 0, 0, jnp.where(slot == 1, len0, len0 + len1))
    length = jnp.where(slot == 0, len0, jnp.where(slot == 1, len1, len2))
    live = (i < length) & (h < prompt_rows) & (t < size)
    x = x_ref[...]
    wide = x.astype(F32)
    mean = jnp.sum(wide, axis=1, keepdims=True) / cols
    spread = jnp.sum((wide - mean) ** 2, axis=1, keepdims=True)
    lane = iota((rows, LANES), 1)
    stats = jnp.zeros((rows, LANES), F32)
    for j, term in enumerate(three(mean) + three(spread)):
        stats = jnp.where(lane == 2 + j, term, stats)
    same = (iota((rows, LANES), 0) == lane).astype(BF)
    turned = lax.dot_general(stats.astype(BF), same, (((0,), (0,)), ((), ())), preferred_element_type=F32)
    turned = jnp.concatenate([jnp.zeros((8, LANES), F32), turned[:8]], axis=0)
    for k, out in enumerate(outs):
        q = jnp.bitwise_xor(m, k)
        mine = live & (start + i - q * size == t)
        decode = (h >= prompt_rows) & (t == QROWS + h - prompt_rows) & (q == z)
        y = jnp.dot((mine | decode).astype(BF), x, preferred_element_type=F32)
        out[...] = y.astype(BF)
        out[16:32, :LANES] = (y[16:32, :LANES] + turned).astype(BF)


def deal(scalars, tokens):
    return pl.pallas_call(
        deal_kernel,
        out_shape=[jax.ShapeDtypeStruct((BLK, tokens.shape[1]), BF)] * NM,
        in_specs=[SMEM, VMEM],
        out_specs=[VMEM] * NM,
        compiler_params=limit(24),
        cost_estimate=SMALL,
        name="deal_rows",
    )(scalars, tokens)


def norm_kernel(s_ref, b0, b1, b2, b3, affine_ref, table_ref, _, __, o0, o1, o2, o3, held):
    z, m = s_ref[3], s_ref[4]
    cols = b0.shape[1]
    for k, ref in enumerate((b0, b1, b2, b3)):
        held[k] = ref[...].astype(F32)
    width = NM * cols
    means, spreads = [], []
    for k in range(NM):
        part = held[k, 24:32, :LANES]
        means.append(part[2:3] + part[3:4] + part[4:5])
        spreads.append(part[5:6] + part[6:7] + part[7:8])
    mean = sum(means) / NM
    var = (sum(spreads) + cols * sum((v - mean) ** 2 for v in means)) / width
    row = iota((BLK, LANES), 0)
    extra = []
    for value in (mean, lax.rsqrt(var + 1e-05)):
        block = jnp.zeros((BLK, LANES), F32)
        for j, term in enumerate(three(value)):
            block = jnp.where(row == STAT_ROW + j, term, block)
        extra.append(block)
    extra = jnp.concatenate(extra, axis=1)
    extra = jnp.where(iota(extra.shape, 0) == BLK - 1, table_ref[:, : 2 * LANES], extra)
    mean = sum(jnp.sum(held[k], axis=1, keepdims=True) for k in range(NM)) / width
    var = sum(jnp.sum((held[k] - mean) ** 2, axis=1, keepdims=True) for k in range(NM)) / width
    rstd = lax.rsqrt(var + 1e-05)
    last = iota((BLK, cols), 0) == BLK - 1
    stats = iota((BLK, 2 * LANES), 0) >= STAT_ROW
    for k, out in enumerate((o0, o1, o2, o3)):
        block = jnp.bitwise_xor(z, k)
        x = held[jnp.bitwise_xor(block, m)]
        y = (x - mean) * rstd * affine_ref[block] + affine_ref[NM + block]
        y = jnp.where(last, table_ref[...], y)
        out[...] = y.astype(BF)
        out[:, : 2 * LANES] = jnp.where(stats, extra, y[:, : 2 * LANES]).astype(BF)


def norm_rows(scalars, blocks, affine, table, near, far):
    return pl.pallas_call(
        norm_kernel,
        out_shape=[jax.ShapeDtypeStruct(blocks[0].shape, BF)] * NZ,
        in_specs=[SMEM] + [VMEM] * 6 + [ANY] * 2,
        out_specs=[VMEM] * NZ,
        scratch_shapes=[pltpu.VMEM((NM,) + blocks[0].shape, F32)],
        compiler_params=limit(32),
        cost_estimate=SMALL,
        name="norm_rows",
    )(scalars, *blocks, affine, table, near, far)


def cores_kernel(s_ref, b0, b1, b2, b3, mine_ref, theirs_ref):
    core = s_ref[6]
    width = mine_ref.shape[1]
    for k, ref in enumerate((b0, b1, b2, b3)):
        rows = slice(k * BLK, (k + 1) * BLK)
        mine_ref[rows, :] = ref[:, pl.ds(pl.multiple_of(core * width, LANES), width)]
        theirs_ref[rows, :] = ref[:, pl.ds(pl.multiple_of((1 - core) * width, LANES), width)]


def split_cores(scalars, blocks):
    out = jax.ShapeDtypeStruct((NZ * BLK, blocks[0].shape[1] // 2), BF)
    return pl.pallas_call(
        cores_kernel,
        out_shape=[out, out],
        in_specs=[SMEM] + [VMEM] * NZ,
        out_specs=[VMEM] * 2,
        compiler_params=limit(16),
        cost_estimate=SMALL,
        name="split_cores",
    )(scalars, *blocks)


def pack_kernel(s_ref, t_ref, a_ref, b_ref, o_ref):
    found = sources(s_ref, t_ref)
    half = a_ref.shape[0]
    lane = iota((1, half), 1)
    total = None
    for other, ref in enumerate((a_ref, b_ref)):
        to = chunk_places(found, other, lane & (BLK - 1), lane // BLK, s_ref[4])
        pick = (iota((o_ref.shape[0], half), 0) == to).astype(BF)
        term = jnp.dot(pick, ref[...], preferred_element_type=F32)
        total = term if total is None else total + term
    o_ref[...] = total.astype(BF)


def pack_rows(scalars, tables, mine, theirs):
    return pl.pallas_call(
        pack_kernel,
        out_shape=jax.ShapeDtypeStruct((CHUNK + DCH, mine.shape[1]), BF),
        in_specs=[SMEM] * 2 + [VMEM] * 2,
        out_specs=VMEM,
        compiler_params=limit(16),
        cost_estimate=SMALL,
        name="pack_rows",
    )(scalars, tables, mine, theirs)


def copy_kernel(x_ref, _, o_ref):
    o_ref[...] = x_ref[...]


def copy_rows(x, after):
    return pl.pallas_call(
        copy_kernel,
        out_shape=jax.ShapeDtypeStruct(x.shape, x.dtype),
        in_specs=[VMEM, ANY],
        out_specs=VMEM,
        compiler_params=limit(16),
        cost_estimate=SMALL,
        name="copy_rows",
    )(x, after)


def code_kernel(s_ref, t_ref, _, col_ref, row_ref):
    found = sources(s_ref, t_ref)
    m, core = s_ref[4], s_ref[6]
    n = NM * CHUNK
    lane, sub = iota((1, LANES), 1), iota((LANES, 1), 0)
    down, across = iota((n, LANES), 0), iota((LANES, n), 1)
    cols, rows = jnp.zeros((n, 1), jnp.int32), jnp.zeros((1, n), jnp.int32)
    for j, a in enumerate(found):
        first = a.index * SLOTS * PLEN + 1
        hit = down == packed_places(a, j, lane, m, core)
        cols = cols + jnp.sum(jnp.where(hit, first + lane, 0), axis=1, keepdims=True)
        hit = across == packed_places(a, j, sub, m, core)
        rows = rows + jnp.sum(jnp.where(hit, first + sub, 0), axis=0, keepdims=True)
    unused = (1 << 16) + PLEN * iota((n, 1), 0)
    col_ref[...] = jnp.where(cols > 0, cols - 1, unused)
    unused = (1 << 16) + PLEN * iota((1, n), 1)
    row_ref[...] = jnp.where(rows > 0, rows - 1, unused)


def packed_codes(scalars, tables, after):
    n = NM * CHUNK
    return pl.pallas_call(
        code_kernel,
        out_shape=[jax.ShapeDtypeStruct((n, 1), jnp.int32), jax.ShapeDtypeStruct((1, n), jnp.int32)],
        in_specs=[SMEM] * 2 + [ANY],
        out_specs=[VMEM] * 2,
        compiler_params=limit(16),
        cost_estimate=SMALL,
        name="packed_codes",
    )(scalars, tables, after)


def rank_kernel(s_ref, table_ref, da_ref, db_ref, x0, x1, x2, x3, t0, t1, t2, t3, affine_ref, o_ref):
    m, r = s_ref[4], s_ref[5]
    width = 2 * ADAPTER_RANK
    count = da_ref.shape[0] // width
    rows = x0.shape[0]
    same = (iota((rows, LANES), 0) == iota((rows, LANES), 1)).astype(BF)
    o_ref[...] = jnp.zeros_like(o_ref)
    for k, (x, stats) in enumerate(zip((x0, x1, x2, x3), (t0, t1, t2, t3))):

        def column(at):
            turned = lax.dot_general(
                same, stats[16:32, at], (((1,), (1,)), ((), ())), preferred_element_type=F32
            )
            j = STAT_ROW - 16
            return turned[:, j : j + 1] + turned[:, j + 1 : j + 2] + turned[:, j + 2 : j + 3]

        mean, rstd = column(slice(0, LANES)), column(slice(LANES, 2 * LANES))
        normed = ((x[...].astype(F32) - mean) * rstd * affine_ref[m] + affine_ref[NM + m]).astype(BF)
        ids = home_adapters(Source(s_ref, table_ref, k), iota((1, rows), 1))
        total = jnp.zeros((width, rows), F32)
        for core, d in enumerate((da_ref, db_ref)):
            y = lax.dot_general(d[...], normed, (((1,), (1,)), ((), ())), preferred_element_type=F32)
            first = jnp.bitwise_xor(r, core) * count
            for a in range(count):
                total = total + jnp.where(ids == first + a, y[a * width : (a + 1) * width], 0.0)
        o_ref[:, k * LANES : k * LANES + rows] = total


def low_rank_rows(scalars, tables, down, down_other, pieces, stats, affine):
    return pl.pallas_call(
        rank_kernel,
        out_shape=jax.ShapeDtypeStruct((2 * ADAPTER_RANK, NZ * LANES), F32),
        in_specs=[SMEM] * 2 + [VMEM] * 11,
        out_specs=VMEM,
        compiler_params=limit(32),
        cost_estimate=SMALL,
        name="low_rank_rows",
    )(scalars, tables, down, down_other, *pieces, *stats, affine)


def expand_kernel(s_ref, t_ref, low_ref, low_other_ref, base_ref, up_ref, _, o_ref, keep_ref, send_ref, *, count):
    m, r, core = s_ref[4], s_ref[5], s_ref[6]
    found = sources(s_ref, t_ref)
    width = count * ADAPTER_RANK
    repeat = []
    for t in range(2):
        shape = (width, 2 * ADAPTER_RANK)
        repeat.append((iota(shape, 1) == t * ADAPTER_RANK + iota(shape, 0) % ADAPTER_RANK).astype(BF))
    repeat = jnp.concatenate(repeat, axis=0)
    adapter = r * count + (iota((2 * width, LANES), 0) % width) // ADAPTER_RANK
    lane = iota((1, LANES), 1)
    total = jnp.zeros((PACKED, 2 * width), F32)
    for j, a in enumerate(found):
        ref = low_other_ref if j >= NZ else low_ref
        k = j % NZ
        low = jnp.dot(repeat, ref[:, k * LANES : (k + 1) * LANES], preferred_element_type=F32)
        low = jnp.where(adapter == home_adapters(a, lane), low, 0.0).astype(BF)
        hit = (iota((PACKED, LANES), 0) == packed_places(a, j, lane, m, core)).astype(BF)
        total = total + lax.dot_general(hit, low, (((1,), (1,)), ((), ())), preferred_element_type=F32)
    feats = up_ref.shape[3]
    half = keep_ref.shape[0]
    keep_ref[...] = base_ref[:half, :]
    send_ref[...] = base_ref[half:, :]
    for t, first in ((0, 0), (1, 2 * feats)):
        rows = total[:, t * width : (t + 1) * width].astype(BF)
        o_ref[t] = rows
        up = up_ref[:, t].reshape(-1, feats)
        term = jnp.dot(rows[NM * CHUNK :, :], up, preferred_element_type=F32)
        keep_ref[:, first : first + feats] += term[:half]
        send_ref[:, first : first + feats] += term[half:]


def expand_rows(scalars, tables, low, low_other, base, up, count, after):
    half = jax.ShapeDtypeStruct((base.shape[0] // 2, base.shape[1]), F32)
    return pl.pallas_call(
        functools.partial(expand_kernel, count=count),
        out_shape=[jax.ShapeDtypeStruct((2, PACKED, count * ADAPTER_RANK), BF), half, half],
        in_specs=[SMEM] * 2 + [VMEM] * 4 + [ANY],
        out_specs=[VMEM] * 3,
        compiler_params=limit(32),
        cost_estimate=SMALL,
        name="expand_rows",
    )(scalars, tables, low, low_other, base, up, after)


def emit_sums(y, own_ref, other_ref):
    half = 2 * CHUNK
    own_ref[...] = y[:half].astype(BF)
    other_ref[...] = y[half : 2 * half].astype(BF)


def first_project_kernel(s_ref, c0, c1, c2, c3, w_ref, _, own_ref, other_ref, x):
    z, m, core = s_ref[3], s_ref[4], s_ref[6]

    @pl.when(pl.program_id(0) == 0)
    def _():
        chunks = (c0, c1, c2, c3)
        for k, chunk in enumerate(chunks):
            base = jnp.bitwise_xor(core, k >> 1) * 2 * CHUNK + (k & 1) * CHUNK
            x[pl.ds(pl.multiple_of(base, CHUNK), CHUNK), :] = chunk[:CHUNK, :]
        n, at = iota((2 * NZ * DEC, NM * DCH), 0), iota((2 * NZ * DEC, NM * DCH), 1)
        chip = jnp.bitwise_xor(z, turned_bits((n >> 1) & 3))
        want = jnp.bitwise_xor(chip, m) * DCH + jnp.bitwise_xor(core, n >> 3) * DEC + (n & 1)
        rows = jnp.concatenate([chunk[CHUNK:, :] for chunk in chunks], axis=0)
        x[NM * CHUNK :, :] = jnp.dot((want == at).astype(BF), rows, preferred_element_type=F32).astype(BF)

    emit_sums(jnp.dot(x[: NM * CHUNK, :], w_ref[0], preferred_element_type=F32), own_ref, other_ref)


def project_rows(scalars, chunks, weight, part, after):
    _, depth, feats = weight.shape
    tile = feats // 2
    half = 2 * CHUNK
    whole = [pl.BlockSpec(v.shape, lambda j: (0, 0)) for v in chunks]
    out_shape = [
        jax.ShapeDtypeStruct((half, feats), BF),
        jax.ShapeDtypeStruct((half, feats), BF),
        jax.ShapeDtypeStruct((PACKED, depth), BF),
    ]
    out_specs = [pl.BlockSpec((v.shape[0], tile), lambda j: (0, j)) for v in out_shape[:2]]
    out_specs.append(pl.BlockSpec((PACKED, depth), lambda j: (0, 0)))
    return pl.pallas_call(
        first_project_kernel,
        grid=(feats // tile,),
        out_shape=out_shape,
        in_specs=[SMEM] + whole + [pl.BlockSpec((1, depth, tile), lambda j: (part, 0, j)), ANY],
        out_specs=out_specs,
        compiler_params=limit(56),
        cost_estimate=SMALL,
        name="project_keys",
    )(scalars, *chunks, weight, after)


def adapted_kernel(x_ref, w_ref, e_ref, u_ref, _, *outs):
    y = jnp.dot(x_ref[: NM * CHUNK, :], w_ref[0], preferred_element_type=F32)
    up = u_ref[...].reshape(-1, u_ref.shape[-1])
    y = y + jnp.dot(e_ref[0, : NM * CHUNK, :], up, preferred_element_type=F32)
    emit_sums(y, *outs)


def project_adapted(rows, weight, part, expanded, up, after):
    _, depth, feats = weight.shape
    tile = feats // 2
    half = 2 * CHUNK
    which = part // 2
    out_shape = [
        jax.ShapeDtypeStruct((half, feats), BF),
        jax.ShapeDtypeStruct((half, feats), BF),
    ]
    return pl.pallas_call(
        adapted_kernel,
        grid=(2,),
        out_shape=out_shape,
        in_specs=[
            pl.BlockSpec(rows.shape, lambda j: (0, 0)),
            pl.BlockSpec((1, depth, tile), lambda j: (part, 0, j)),
            pl.BlockSpec((1,) + expanded.shape[1:], lambda j: (which, 0, 0)),
            pl.BlockSpec((up.shape[0], 1, up.shape[2], tile), lambda j: (0, which, 0, j)),
            ANY,
        ],
        out_specs=[pl.BlockSpec((v.shape[0], tile), lambda j: (0, j)) for v in out_shape],
        compiler_params=limit(56),
        cost_estimate=SMALL,
        name="project_adapted",
    )(rows, weight, expanded, up, after)


def add_kernel(a_ref, b_ref, _, o_ref):
    o_ref[...] = (a_ref[: b_ref.shape[0], :] + b_ref[...]).astype(o_ref.dtype)


def add_rows(a, b, after, dtype=F32):
    return pl.pallas_call(
        add_kernel,
        out_shape=jax.ShapeDtypeStruct(b.shape, dtype),
        in_specs=[VMEM] * 2 + [ANY],
        out_specs=VMEM,
        compiler_params=limit(16),
        cost_estimate=SMALL,
        name="add_rows",
    )(a, b, after)


def decode_finish_kernel(a_ref, b_ref, bias_ref, _, q_ref, k_ref, v_ref):
    total = a_ref[: b_ref.shape[0], :] + b_ref[...]
    feats = bias_ref.shape[1]
    for j, out in enumerate((q_ref, k_ref, v_ref)):
        part = total[:, j * feats : (j + 1) * feats] + bias_ref[j : j + 1, :]
        for i in range(out.shape[0]):
            out[i] = part[i : i + 1].astype(BF)


def decode_finish(a, b, bias, after):
    out = jax.ShapeDtypeStruct((b.shape[0], 1, bias.shape[1]), BF)
    return pl.pallas_call(
        decode_finish_kernel,
        out_shape=[out] * 3,
        in_specs=[VMEM] * 3 + [ANY],
        out_specs=[VMEM] * 3,
        compiler_params=limit(16),
        cost_estimate=SMALL,
        name="decode_finish",
    )(a, b, bias, after)


def decode_base_kernel(x_ref, w_ref, _, o_ref):
    o_ref[...] = jnp.dot(x_ref[...], w_ref[0], preferred_element_type=F32)


def decode_base(rows, weight, after):
    parts, depth, feats = weight.shape
    count = PACKED - NM * CHUNK
    return pl.pallas_call(
        decode_base_kernel,
        grid=(parts,),
        out_shape=jax.ShapeDtypeStruct((count, parts * feats), F32),
        in_specs=[
            pl.BlockSpec((count, depth), lambda p: (NM * CHUNK // count, 0)),
            pl.BlockSpec((1, depth, feats), lambda p: (p, 0, 0)),
            ANY,
        ],
        out_specs=pl.BlockSpec((count, feats), lambda p: (0, p)),
        compiler_params=limit(56),
        cost_estimate=SMALL,
        name="decode_base",
    )(rows, weight, after)


def halve_kernel(s_ref, *refs, bit, groups):
    *ins, _, send_ref, keep_ref = refs
    count = len(ins) // 2
    side = (s_ref[3] >> bit) & 1
    to = 0
    for total_ref, got_ref in zip(ins[:count], ins[count:]):
        width = total_ref.shape[1] // groups // 2

        for g in range(groups):

            def part(which):
                at = pl.ds(pl.multiple_of((2 * g + which) * width, LANES), width)
                return total_ref[:, at].astype(F32) + got_ref[:, at].astype(F32)

            send_ref[:, to : to + width] = part(1 - side).astype(BF)
            keep_ref[:, to : to + width] = part(side)
            to += width


def halve(scalars, totals, gots, bit, after, groups=1):
    rows = totals[0].shape[0]
    feats = sum(v.shape[1] for v in totals) // 2
    return pl.pallas_call(
        functools.partial(halve_kernel, bit=bit, groups=groups),
        out_shape=[jax.ShapeDtypeStruct((rows, feats), BF), jax.ShapeDtypeStruct((rows, feats), F32)],
        in_specs=[SMEM] + [VMEM] * (2 * len(totals)) + [ANY],
        out_specs=[VMEM, VMEM],
        compiler_params=limit(24),
        cost_estimate=SMALL,
        name="halve_sums",
    )(scalars, *totals, *gots, after)


def finish_kernel(s_ref, total_ref, got_ref, bias_ref, _, *outs, parts):
    for j, (part, out) in enumerate(zip(parts, outs)):
        width = out.shape[1]
        at = pl.ds(pl.multiple_of(place_of(s_ref[3]) * width, LANES), width)
        mine = slice(j * width, (j + 1) * width)
        total = total_ref[:, mine] + got_ref[:, mine].astype(F32) + bias_ref[part : part + 1, at]
        out[...] = total.astype(BF)


def finish(scalars, total, got, bias, parts, after):
    rows, feats = total.shape
    return pl.pallas_call(
        functools.partial(finish_kernel, parts=parts),
        out_shape=[jax.ShapeDtypeStruct((rows, feats // len(parts)), BF)] * len(parts),
        in_specs=[SMEM, VMEM, VMEM, VMEM, ANY],
        out_specs=[VMEM] * len(parts),
        compiler_params=limit(16),
        cost_estimate=SMALL,
        name="finish_sums",
    )(scalars, total, got, bias, after)


def prompt_kernel(q_ref, ka_ref, kb_ref, va_ref, vb_ref, cr_ref, cc_ref, d_ref, o_ref):
    rows = cr_ref[...]
    cols = cc_ref[...]
    allowed = ((rows >> 5) == (cols >> 5)) & (cols <= rows)
    keys = jnp.concatenate([ka_ref[...], kb_ref[...]], axis=0)
    values = jnp.concatenate([va_ref[...], vb_ref[...]], axis=0)
    for h in range(q_ref.shape[1] // HEAD_DIM):
        at = slice(h * HEAD_DIM, (h + 1) * HEAD_DIM)
        s = lax.dot_general(q_ref[:, at], keys[:, at], (((1,), (1,)), ((), ())), preferred_element_type=F32)
        s = jnp.where(allowed, s * HEAD_DIM**-0.5, -1e30)
        top = jnp.max(s, axis=1, keepdims=True)
        w = jnp.where(allowed, jnp.exp(s - top), 0.0)
        w = (w / jnp.sum(w, axis=1, keepdims=True)).astype(BF)
        o_ref[: q_ref.shape[0], at] = jnp.dot(w, values[:, at], preferred_element_type=F32).astype(BF)
    width = q_ref.shape[1]
    n = iota((DECODE_ROWS, width), 0)
    tail = jnp.zeros((DECODE_ROWS, width), F32)
    for b in range(NZ):
        for j in range(DEC):
            tail = jnp.where(n == b * DEC + j, d_ref[j : j + 1, b * width : (b + 1) * width].astype(F32), tail)
    o_ref[q_ref.shape[0] :, :] = tail.astype(BF)


def prompt_attention(q, ka, kb, va, vb, code_rows, code_cols, dec):
    return pl.pallas_call(
        prompt_kernel,
        out_shape=jax.ShapeDtypeStruct((q.shape[0] + DECODE_ROWS, q.shape[1]), BF),
        in_specs=[VMEM] * 8,
        out_specs=VMEM,
        compiler_params=limit(32),
        cost_estimate=SMALL,
        name="prompt_attention",
    )(q, ka, kb, va, vb, code_rows, code_cols, dec)


def decode_kernel(len_ref, q_ref, k_ref, v_ref, c_ref, _, o_ref, qbd, top, total, acc):
    d, t = pl.program_id(0), pl.program_id(1)
    span = c_ref.shape[1]
    live = len_ref[d]
    heads, feats = qbd.shape
    diag = lax.broadcasted_iota(jnp.int32, (heads, feats), 1) // HEAD_DIM == lax.broadcasted_iota(
        jnp.int32, (heads, feats), 0
    )

    @pl.when(t == 0)
    def _():
        q = jnp.where(diag, q_ref[0].astype(F32), 0.0)
        qbd[...] = q.astype(BF)
        own = jnp.sum(q * k_ref[0].astype(F32), axis=1, keepdims=True) * HEAD_DIM**-0.5
        top[...] = jnp.broadcast_to(own, top.shape)
        total[...] = jnp.ones_like(total)
        acc[...] = jnp.broadcast_to(v_ref[0].astype(F32), acc.shape)

    @pl.when(t * span < live)
    def _():
        x = c_ref[0].reshape(2 * span, feats)
        s = lax.dot_general(qbd[...], x, (((1,), (1,)), ((), ())), preferred_element_type=F32)
        column = lax.broadcasted_iota(jnp.int32, s.shape, 1)
        valid = (column % 2 == 0) & (t * span + column // 2 < live)
        s = jnp.where(valid, s * HEAD_DIM**-0.5, -1e30)
        before = top[:, :1]
        now = jnp.maximum(before, jnp.max(s, axis=1, keepdims=True))
        fade = jnp.exp(before - now)
        w = jnp.where(valid, jnp.exp(s - now), 0.0)
        total[...] = total[...] * fade + jnp.sum(w, axis=1, keepdims=True)
        top[...] = jnp.broadcast_to(now, top.shape)
        w = pltpu.roll(w, 1, 1).astype(BF)
        acc[...] = acc[...] * fade + jnp.dot(w, x, preferred_element_type=F32)

    @pl.when(t == pl.num_programs(1) - 1)
    def _():
        o = acc[...] / total[:, :1]
        o_ref[0] = jnp.sum(jnp.where(diag, o, 0.0), axis=0, keepdims=True).astype(BF)


def decode_attention(lengths, q, k, v, cache, after, span=256):
    count, positions, _, feats = cache.shape
    row = pl.BlockSpec((1, 1, feats), lambda d, t, n: (d, 0, 0))
    heads = 16
    return pl.pallas_call(
        decode_kernel,
        grid_spec=pltpu.PrefetchScalarGridSpec(
            num_scalar_prefetch=1,
            grid=(count, positions // span),
            in_specs=[row, row, row]
            + [pl.BlockSpec((1, span, 2, feats), lambda d, t, n: (d, jnp.minimum(t, (n[d] - 1) // span), 0, 0)), ANY],
            out_specs=row,
            scratch_shapes=[
                pltpu.VMEM((heads, feats), BF),
                pltpu.VMEM((heads, LANES), F32),
                pltpu.VMEM((heads, LANES), F32),
                pltpu.VMEM((heads, feats), F32),
            ],
        ),
        out_shape=jax.ShapeDtypeStruct((count, 1, feats), BF),
        compiler_params=limit(32),
        cost_estimate=SMALL,
        name="decode_attention",
    )(lengths, q, k, v, cache, after)


def out_kernel(place_ref, *refs):
    own, other, w_ref, outs, mixed = refs[:4], refs[4:8], refs[8], refs[9:13], refs[13]
    z, m, core = place_ref[3], place_ref[4], place_ref[6]
    width = own[0].shape[1]
    half = own[0].shape[0] - DECODE_ROWS
    total = None
    for k in range(NZ):
        block = place_of(jnp.bitwise_xor(z, k))
        w = w_ref[pl.ds(pl.multiple_of(block * width, width), width), :]
        rows = jnp.concatenate([own[k][:half, :], other[k][:half, :]], axis=0)
        term = jnp.dot(rows, w, preferred_element_type=F32)
        total = term if total is None else total + term
    mixed[...] = total.astype(BF)
    tails = jnp.concatenate([v[half:, :] for v in own + other], axis=0)
    count = 2 * NZ * DEC
    n, at = iota((count, tails.shape[0]), 0), iota((count, tails.shape[0]), 1)
    total = None
    for b in range(NZ):
        pick = (at == (n // DEC) * DECODE_ROWS + b * DEC + n % DEC).astype(BF)
        rows = jnp.dot(pick, tails, preferred_element_type=F32).astype(BF)
        term = jnp.dot(rows, w_ref[b * width : (b + 1) * width, :], preferred_element_type=F32)
        total = term if total is None else total + term
    decode = total.astype(BF)
    n, at = iota((DCH, count), 0), iota((DCH, count), 1)
    for k, out in enumerate(outs):
        base = jnp.bitwise_xor(core, k >> 1) * 2 * CHUNK + (k & 1) * CHUNK
        out[:CHUNK, :] = mixed[pl.ds(pl.multiple_of(base, CHUNK), CHUNK), :]
        far = jnp.bitwise_xor(jnp.bitwise_xor(m, k), z)
        want = (jnp.bitwise_xor(core, n >> 1) * NZ + far) * DEC + (n & 1)
        pick = ((at == want) & (n < 2 * DEC)).astype(BF)
        out[CHUNK:, :] = jnp.dot(pick, decode, preferred_element_type=F32).astype(BF)


def out_project(scalars, own, other, weight):
    feats = weight.shape[1]
    return pl.pallas_call(
        out_kernel,
        out_shape=[jax.ShapeDtypeStruct((CHUNK + DCH, feats), BF)] * NM,
        in_specs=[SMEM] + [VMEM] * 9,
        out_specs=[VMEM] * NM,
        scratch_shapes=[pltpu.VMEM((NM * CHUNK, feats), BF)],
        compiler_params=limit(40),
        cost_estimate=SMALL,
        name="out_project",
    )(scalars, *own, *other, weight)


def unpack_kernel(s_ref, t_ref, c0, c1, c2, c3, *outs):
    total = sum(c[...].astype(F32) for c in (c0, c1, c2, c3)).astype(BF)
    found = sources(s_ref, t_ref)
    n = iota((NZ * BLK, 1), 0)
    for other in range(2):
        to = chunk_places(found, other, n & (BLK - 1), n // BLK, s_ref[4])
        pick = (iota((NZ * BLK, total.shape[0]), 1) == to).astype(BF)
        rows = jnp.dot(pick, total, preferred_element_type=F32).astype(BF)
        for k, out in enumerate(outs):
            out[other * BLK : (other + 1) * BLK, :] = rows[k * BLK : (k + 1) * BLK]


def unpack_rows(scalars, tables, chunks):
    feats = chunks[0].shape[1]
    return pl.pallas_call(
        unpack_kernel,
        out_shape=[jax.ShapeDtypeStruct((2 * BLK, feats), BF)] * NZ,
        in_specs=[SMEM] * 2 + [VMEM] * 4,
        out_specs=[VMEM] * NZ,
        compiler_params=limit(16),
        cost_estimate=SMALL,
        name="unpack_rows",
    )(scalars, tables, *chunks)


def join_kernel(s_ref, a0, a1, a2, a3, other_ref, o0, o1, o2, o3, held):
    z, m, core = s_ref[3], s_ref[4], s_ref[6]
    width = a0.shape[1]
    mine = pl.ds(pl.multiple_of(core * width, LANES), width)
    theirs = pl.ds(pl.multiple_of((1 - core) * width, LANES), width)
    for k, ref in enumerate((a0, a1, a2, a3)):
        held[k, :, mine] = ref[:BLK, :]
        held[k, :, theirs] = other_ref[k * BLK : (k + 1) * BLK, :]
    for k, out in enumerate((o0, o1, o2, o3)):
        out[...] = held[jnp.bitwise_xor(jnp.bitwise_xor(z, m), k)]


def join_halves(scalars, parts, other):
    shape = (BLK, 2 * parts[0].shape[1])
    return pl.pallas_call(
        join_kernel,
        out_shape=[jax.ShapeDtypeStruct(shape, BF)] * NM,
        in_specs=[SMEM] + [VMEM] * 5,
        out_specs=[VMEM] * NM,
        scratch_shapes=[pltpu.VMEM((NZ,) + shape, BF)],
        compiler_params=limit(16),
        cost_estimate=SMALL,
        name="join_halves",
    )(scalars, *parts, other)


def home_kernel(s_ref, x_ref, bias_ref, b0, b1, b2, b3, o_ref):
    len0, len1, len2, z, m = [s_ref[i] for i in range(5)]
    size = (len0 + len1 + len2 + 3) >> 2
    rows = x_ref.shape[0]
    prompt_rows = SLOTS * PLEN
    t, h = iota((rows, BLK), 1), iota((rows, BLK), 0)
    slot, i = h >> 5, h & (PLEN - 1)
    start = jnp.where(slot == 0, 0, jnp.where(slot == 1, len0, len0 + len1))
    length = jnp.where(slot == 0, len0, jnp.where(slot == 1, len1, len2))
    live = (i < length) & (h < prompt_rows) & (t < size)
    total = x_ref[...].astype(F32) + bias_ref[...]
    for k, ref in enumerate((b0, b1, b2, b3)):
        q = jnp.bitwise_xor(m, k)
        mine = live & (start + i - q * size == t)
        decode = (h >= prompt_rows) & (t == QROWS + h - prompt_rows) & (q == z)
        total = total + jnp.dot((mine | decode).astype(BF), ref[...], preferred_element_type=F32)
    o_ref[...] = total.astype(BF)


def add_home(scalars, tokens, bias, blocks):
    return pl.pallas_call(
        home_kernel,
        out_shape=jax.ShapeDtypeStruct(tokens.shape, BF),
        in_specs=[SMEM] + [VMEM] * 6,
        out_specs=VMEM,
        compiler_params=limit(24),
        cost_estimate=SMALL,
        name="add_home",
    )(scalars, tokens, bias, *blocks)


def turned_bits(k):
    return (k & 1) * 2 + (k >> 1)


def place_of(z):
    return turned_bits(z)


def packed_device(
    tokens,
    layernorm_scale,
    layernorm_bias,
    query_key_value_weight,
    query_key_value_bias,
    adapter_down_weight,
    adapter_up_weight,
    adapter_index_table,
    prompt_length_list,
    cache,
    cache_length_list,
    output_weight,
    output_bias,
):
    i32 = jnp.int32
    r = lax.axis_index("req").astype(i32)
    m = lax.axis_index("mp").astype(i32)
    z, c = r >> 1, r & 1
    rows_dev, cols = tokens.shape
    prompt_rows = SLOTS * PLEN
    feats = query_key_value_weight.shape[2]
    depth = query_key_value_weight.shape[1]
    per_z = feats // NZ
    own_adapters = adapter_down_weight.shape[0]
    half = 2 * CHUNK
    order = jnp.arange(2 * NZ, dtype=i32)
    source = ((z ^ (order & 3)) << 1) + (c ^ (order >> 2))
    lens = prompt_length_list
    scalars = jnp.concatenate([lens, jnp.stack([z, m, r, c])])

    down = jnp.transpose(adapter_down_weight, (0, 2, 1)).reshape(own_adapters * 2 * ADAPTER_RANK, cols)

    with jax.named_scope("deal"):
        dealt = deal(scalars, tokens)
    with jax.named_scope("gather_home"):
        pieces = gather_z(tokens)
    with jax.named_scope("deal"):
        blocks = [dealt[0]] + [swap_mp(dealt[k], k) for k in range(1, NM)]
    with jax.named_scope("norm_rows"):
        table = jnp.concatenate([lens, adapter_index_table[0]]).astype(F32)
        table = jnp.pad(table, (0, depth - table.shape[0]))
        table = jnp.tile(table, 2)[None, :]
        affine = jnp.stack([layernorm_scale, layernorm_bias]).reshape(2 * NM, 1, cols)
        normed = norm_rows(scalars, blocks, affine, table, pieces[1], pieces[2])
    with jax.named_scope("spread_z"):
        spread = [normed[0]] + [swap_req(normed[k], 2 * k) for k in range(1, NZ)]
        mine, theirs = split_cores(scalars, spread)
        theirs = swap_req(theirs, 1)

    with jax.named_scope("tables"):
        tables = jnp.concatenate(
            [v.reshape(NZ, BLK, depth)[:, BLK - 1, : SLOTS + SLOTS + DEC] for v in (mine, theirs)], axis=0
        ).astype(i32)
    with jax.named_scope("pack"):
        chunk = pack_rows(scalars, tables, mine, theirs)
    with jax.named_scope("gather_chunks"):
        chunks = gather_mp(chunk)

    with jax.named_scope("low_rank"):
        down_other = swap_req(copy_rows(down, chunk), 1)
        part = low_rank_rows(scalars, tables, down, down_other, pieces, spread, affine)
    with jax.named_scope("keys"):
        own_k, other_k, x_rows = project_rows(scalars, chunks, query_key_value_weight, 1, part)
        core_k = swap_req(other_k, 1)
    with jax.named_scope("decode_rows"):
        base = decode_base(x_rows, query_key_value_weight, other_k)
    with jax.named_scope("low_rank"):
        two = add_rows(part, swap_mp(part, 1), base)
    with jax.named_scope("keys"):
        send_k, keep_k = halve(scalars, [own_k], [core_k], 0, two)
        got_k = swap_req(send_k, 2)
    with jax.named_scope("low_rank"):
        code_col, code_row = packed_codes(scalars, tables, send_k)
        low_rank = add_rows(two, swap_mp(two, 2), code_row, BF)
        expanded, dec, dec_sent = expand_rows(
            scalars, tables, low_rank, swap_req(low_rank, 1), base, adapter_up_weight, own_adapters, base
        )
    with jax.named_scope("decode_rows"):
        dec_chip = add_rows(dec, swap_req(dec_sent, 1), expanded)
    with jax.named_scope("keys"):
        send_k, keep_k = halve(scalars, [keep_k], [got_k], 1, dec_chip)
        got_k = swap_req(send_k, 4)
    with jax.named_scope("values"):
        own_v, other_v = project_adapted(x_rows, query_key_value_weight, 2, expanded, adapter_up_weight, send_k)
        core_v = swap_req(other_v, 1)
    with jax.named_scope("decode_rows"):
        dec_pair = add_rows(dec_chip, swap_req(dec_chip[4:], 2), own_v)
    with jax.named_scope("keys"):
        (keys,) = finish(scalars, keep_k, got_k, query_key_value_bias, (1,), dec_pair)
        keys_other = swap_req(keys, 1)
    with jax.named_scope("queries"):
        own_q, other_q = project_adapted(x_rows, query_key_value_weight, 0, expanded, adapter_up_weight, keys)
        core_q = swap_req(other_q, 1)
    with jax.named_scope("decode_rows"):
        dec = decode_finish(dec_pair, swap_req(dec_pair[2:], 4), query_key_value_bias, own_q)
    with jax.named_scope("reduce_z"):
        send, keep = halve(scalars, [own_v, own_q], [core_v, core_q], 0, dec[0])
        got = swap_req(send, 2)
    with jax.named_scope("reduce_z"):
        send, keep = halve(scalars, [keep], [got], 1, send, groups=2)
        got = swap_req(send, 4)
    with jax.named_scope("decode_attention"):
        dec_out = decode_attention(cache_length_list, *dec, cache, send)
        dec_out = dec_out.reshape(DEC, feats)
    with jax.named_scope("reduce_z"):
        values, queries = finish(scalars, keep, got, query_key_value_bias, (2, 0), dec_out)
        values_other = swap_req(values, 1)
    with jax.named_scope("prompt_attention"):
        attended = prompt_attention(
            queries,
            keys,
            keys_other,
            values,
            values_other,
            code_col[: 2 * CHUNK],
            code_row,
            dec_out,
        )
    with jax.named_scope("gather_attended"):
        own = gather_z(attended)
        other = [swap_req(v, 1) for v in own]
    with jax.named_scope("out_project"):
        mixed = out_project(scalars, own, other, output_weight)
    with jax.named_scope("sum_mp"):
        shares = [mixed[0]] + [swap_mp(mixed[k], k) for k in range(1, NM)]
    with jax.named_scope("return_z"):
        back = unpack_rows(scalars, tables, shares)
        back = [back[0]] + [swap_req(back[k], 2 * k) for k in range(1, NZ)]
        back_other = swap_req(jnp.concatenate([v[BLK:] for v in back], axis=0), 1)
    with jax.named_scope("return_plane"):
        joined = join_halves(scalars, back, back_other)
        joined = [joined[0]] + [swap_mp(joined[k], k) for k in range(1, NM)]
        return add_home(scalars, tokens, output_bias[None], joined)


def layer_norm(row_data, gain_vec, shift_vec):
    values = row_data.astype(jnp.float32)
    average = jnp.mean(values, axis=-1, keepdims=True)
    centred = values - average
    variance = jnp.mean(centred * centred, axis=-1, keepdims=True)
    scaled = centred * lax.rsqrt(variance + 1e-05)
    return (scaled * gain_vec + shift_vec).astype(jnp.bfloat16)


def on_device(
    tokens,
    layernorm_scale,
    layernorm_bias,
    query_key_value_weight,
    query_key_value_bias,
    adapter_down_weight,
    adapter_up_weight,
    adapter_index_table,
    prompt_length_list,
    cache,
    cache_length_list,
    output_weight,
    output_bias,
):
    rows_dev = tokens.shape[0]
    part_cols = tokens.shape[1]
    decode_count = cache.shape[0]
    slot_count = prompt_length_list.shape[0]
    prompt_rows = rows_dev - decode_count
    slot_len = prompt_rows // slot_count
    rank_size = ADAPTER_RANK
    head_count = query_key_value_weight.shape[2] // HEAD_DIM
    score_scale = HEAD_DIM ** (-0.5)
    gathered = lax.all_gather(tokens, "mp", axis=1, tiled=True)
    normed = layer_norm(gathered, layernorm_scale, layernorm_bias)
    column = lax.axis_index("mp")
    slice_m = lax.dynamic_slice_in_dim(normed, column * part_cols, part_cols, 1)
    spread = lax.all_to_all(normed, "req", split_axis=1, concat_axis=0, tiled=True)
    projected = lax.psum_scatter(
        jnp.einsum(
            "rd,cde->rce", spread, query_key_value_weight, preferred_element_type=jnp.float32
        ),
        "req",
        scatter_dimension=0,
        tiled=True,
    )
    projected = projected + query_key_value_bias[None]
    positions = jnp.arange(rows_dev)
    request_slot = jnp.where(
        positions < prompt_rows, positions // slot_len, slot_count + positions - prompt_rows
    )
    slot_match = request_slot[:, None] == jnp.arange(slot_count + decode_count)[None, :]
    row_adapter = jnp.sum(jnp.where(slot_match, adapter_index_table[0][None, :], 0), axis=1)
    adapter_on_device = adapter_down_weight.shape[0]
    owners = lax.axis_size("req")
    owner_row = row_adapter // adapter_on_device
    to_owner = owner_row[None, :] == jnp.arange(owners)[:, None]
    outgoing = jnp.where(to_owner[:, :, None], slice_m[None], jnp.zeros((), jnp.bfloat16))
    labels = jnp.where(to_owner, (row_adapter - owner_row * adapter_on_device)[None, :], -1)
    received_rows = lax.all_to_all(outgoing, "req", split_axis=0, concat_axis=0, tiled=True)
    arrived_labels = lax.all_to_all(labels, "req", split_axis=0, concat_axis=0, tiled=True)
    sources, items = arrived_labels.shape
    selection_mask = (
        arrived_labels[:, :, None] == jnp.arange(adapter_on_device)[None, None, :]
    ).astype(jnp.float32)
    adapter_wise_sums = jnp.einsum(
        "yju,ouv->yjov", received_rows, adapter_down_weight, preferred_element_type=jnp.float32
    )
    reduced_rank_rows = jnp.einsum("ogf,ogft->ogt", selection_mask, adapter_wise_sums)
    reduced_rank_rows = lax.psum(reduced_rank_rows, "mp").astype(jnp.bfloat16)
    broadcast_rank_rows = selection_mask.astype(jnp.bfloat16)[
        :, :, :, None, None
    ] * reduced_rank_rows.reshape(sources, items, 1, 2, rank_size)
    corrections = jnp.einsum(
        "pqwgd,wgdx->pqgx",
        broadcast_rank_rows,
        adapter_up_weight,
        preferred_element_type=jnp.float32,
    ).astype(jnp.bfloat16)
    returned = lax.all_to_all(corrections, "req", split_axis=0, concat_axis=0, tiled=True)
    adapter_delta = jnp.sum(returned.astype(jnp.float32), axis=0)
    queries = (projected[:, 0] + adapter_delta[:, 0]).astype(jnp.bfloat16)
    keys_new = projected[:, 1].astype(jnp.bfloat16)
    values_new = (projected[:, 2] + adapter_delta[:, 1]).astype(jnp.bfloat16)
    prompt_q = queries[:prompt_rows].reshape(slot_count, slot_len, head_count, HEAD_DIM)
    prompt_k = keys_new[:prompt_rows].reshape(slot_count, slot_len, head_count, HEAD_DIM)
    prompt_v = values_new[:prompt_rows].reshape(slot_count, slot_len, head_count, HEAD_DIM)
    scores = (
        jnp.einsum("sihd,sjhd->shij", prompt_q, prompt_k, preferred_element_type=jnp.float32)
        * score_scale
    )
    causal = jnp.arange(slot_len)[None, :] <= jnp.arange(slot_len)[:, None]
    scores = jnp.where(causal[None, None], scores, -1e30)
    highest = jnp.max(scores, axis=3, keepdims=True)
    weights = jnp.where(causal[None, None], jnp.exp(scores - highest), 0.0)
    weights = (weights / jnp.sum(weights, axis=3, keepdims=True)).astype(jnp.bfloat16)
    prompt_out = jnp.einsum(
        "shij,sjhd->sihd", weights, prompt_v, preferred_element_type=jnp.float32
    )
    active = jnp.arange(slot_len)[None, :] < prompt_length_list[:, None]
    prompt_out = (
        jnp.where(active[:, :, None, None], prompt_out, 0.0)
        .astype(jnp.bfloat16)
        .reshape(prompt_rows, -1)
    )
    cache_len = cache.shape[1]
    decode_q = queries[prompt_rows:].reshape(decode_count, head_count, HEAD_DIM)
    decode_k = keys_new[prompt_rows:].reshape(decode_count, head_count, HEAD_DIM)
    decode_v = values_new[prompt_rows:].reshape(decode_count, head_count, HEAD_DIM)
    keys_old = cache[:, :, 0].reshape(decode_count, cache_len, head_count, HEAD_DIM)
    values_old = cache[:, :, 1].reshape(decode_count, cache_len, head_count, HEAD_DIM)
    cache_scores = (
        jnp.einsum("dhe,dthe->dht", decode_q, keys_old, preferred_element_type=jnp.float32)
        * score_scale
    )
    live_cache = jnp.arange(cache_len)[None, None, :] < cache_length_list[:, None, None]
    cache_scores = jnp.where(live_cache, cache_scores, -1e30)
    self_score = (
        jnp.einsum("dhe,dhe->dh", decode_q, decode_k, preferred_element_type=jnp.float32)
        * score_scale
    )
    row_top = jnp.maximum(jnp.max(cache_scores, axis=2), self_score)
    cache_weights = jnp.where(live_cache, jnp.exp(cache_scores - row_top[:, :, None]), 0.0)
    self_weight = jnp.exp(self_score - row_top)
    totals = jnp.sum(cache_weights, axis=2) + self_weight
    cache_weights = (cache_weights / totals[:, :, None]).astype(jnp.bfloat16)
    self_weight = (self_weight / totals).astype(jnp.bfloat16)
    decode_out = jnp.einsum(
        "dht,dthe->dhe", cache_weights, values_old, preferred_element_type=jnp.float32
    )
    decode_out = decode_out + self_weight.astype(jnp.float32)[:, :, None] * decode_v.astype(
        jnp.float32
    )
    decode_out = decode_out.astype(jnp.bfloat16).reshape(decode_count, -1)
    attended = jnp.concatenate([prompt_out, decode_out], axis=0)
    mixed = jnp.dot(
        attended,
        lax.all_gather(output_weight, "req", axis=1, tiled=True),
        preferred_element_type=jnp.float32,
    )
    summed = lax.psum_scatter(
        mixed.astype(jnp.bfloat16), "mp", scatter_dimension=1, tiled=True
    ).astype(jnp.float32)
    return (tokens.astype(jnp.float32) + summed + output_bias[None]).astype(jnp.bfloat16)


def solution(mesh):
    placed = (
        P("req", "mp"),
        P(),
        P(),
        P(None, "req", "mp"),
        P(None, "mp"),
        P("req", "mp", None),
        P("req", None, None, "mp"),
        P("req", None),
        P("req"),
        P("req", None, None, "mp"),
        P("req"),
        P("mp", "req"),
        P("mp"),
    )
    quick = mesh.shape["req"] == 2 * NZ and mesh.shape["mp"] == NM
    return jax.shard_map(
        packed_device if quick else on_device, mesh=mesh, in_specs=placed, out_specs=P("req", "mp"), check_vma=False
    )
```

```python
import functools

import jax
import jax.numpy as jnp
from jax import lax
from jax.experimental import pallas as pl
from jax.experimental.pallas import tpu as pltpu
from jax.sharding import PartitionSpec as P

HEAD_DIM = 128
ADAPTER_RANK = 16
BF = jnp.bfloat16
F32 = jnp.float32
MIB = 1 << 20

NZ, NM = 4, 4
SLOTS, PLEN, DEC = 3, 32, 2
QROWS = 24
STAT_ROW = 26
BLK = 32
CHUNK = 128
DCH = 16
PACKED = NM * CHUNK + 2 * NZ * DEC
LANES = 128
DECODE_ROWS = 16
SMALL = pl.CostEstimate(flops=1, bytes_accessed=1, transcendentals=0)
VMEM = pl.BlockSpec(memory_space=pltpu.VMEM)
SMEM = pl.BlockSpec(memory_space=pltpu.SMEM)
ANY = pl.BlockSpec(memory_space=pl.ANY)


def swap_req(x, bits):
    return lax.ppermute(x, "req", [(i, i ^ bits) for i in range(2 * NZ)])


def swap_mp(x, bits):
    return lax.ppermute(x, "mp", [(i, i ^ bits) for i in range(NM)])


def gather_z(x):
    far, near = swap_req(x, 4), swap_req(x, 2)
    return [x, near, far, swap_req(far, 2)]


def limit(mib):
    return pltpu.CompilerParams(vmem_limit_bytes=mib * MIB)


def iota(shape, axis):
    return lax.broadcasted_iota(jnp.int32, shape, axis)


def three(x):
    a = x.astype(BF)
    rest = x - a.astype(F32)
    b = rest.astype(BF)
    return [a.astype(F32), b.astype(F32), (rest - b.astype(F32)).astype(BF).astype(F32)]


class Source:
    def __init__(self, s_ref, t_ref, j):
        z, core = s_ref[3], s_ref[6]
        self.z = jnp.bitwise_xor(z, j % NZ)
        self.core = jnp.bitwise_xor(core, j // NZ)
        self.index = self.z * 2 + self.core
        self.lens = [t_ref[j, i] for i in range(SLOTS)]
        self.adapters = [t_ref[j, SLOTS + i] for i in range(SLOTS + DEC)]
        self.live = self.lens[0] + self.lens[1] + self.lens[2]
        self.size = (self.live + 3) >> 2


def sources(s_ref, t_ref):
    found = [Source(s_ref, t_ref, j) for j in range(2 * NZ)]
    for a in found:
        a.offset = sum(jnp.where(b.index < a.index, b.size, 0) for b in found)
    return found


def by_slot(h, values):
    out = jnp.full_like(h, -1)
    for j in range(SLOTS):
        out = jnp.where((h >> 5) == j, values[j], out)
    return out


def chunk_places(found, other, t, seg, m):
    out = jnp.full_like(t, -1)
    for k in range(NZ):
        a = found[other * NZ + k]
        have = jnp.clip(a.live - m * a.size, 0, a.size)
        prompt = jnp.where(t < have, a.offset + t, -1)
        decode = jnp.where((t < QROWS + DEC) & (a.z == m), CHUNK + a.core * DEC + t - QROWS, -1)
        out = jnp.where(seg == k, jnp.where(t < QROWS, prompt, decode), out)
    return out


def packed_places(a, j, h, m, core):
    i = h & (PLEN - 1)
    starts = [0, a.lens[0], a.lens[0] + a.lens[1]]
    index = by_slot(h, starts) + i
    quarter = sum((index >= q * a.size).astype(jnp.int32) for q in range(1, NM))
    spot = jnp.bitwise_xor(quarter, m) * CHUNK + a.offset + index - quarter * a.size
    half = 2 * CHUNK
    spot = jnp.bitwise_xor(spot >> 8, core) * half + (spot & (half - 1))
    prompt = jnp.where(i < by_slot(h, a.lens), spot, -1)
    first = SLOTS * PLEN
    base = NM * CHUNK + (j // NZ * NZ + turned_bits(j % NZ)) * DEC - first
    decode = jnp.where(h < first + DEC, base + h, -1)
    return jnp.where(h < first, prompt, decode)


def home_adapters(a, h):
    out = by_slot(h, a.adapters)
    for j in range(DEC):
        out = jnp.where(h == SLOTS * PLEN + j, a.adapters[SLOTS + j], out)
    return out


def deal_kernel(s_ref, x_ref, *outs):
    len0, len1, len2, z, m = [s_ref[i] for i in range(5)]
    size = (len0 + len1 + len2 + 3) >> 2
    rows, cols = x_ref.shape
    prompt_rows = SLOTS * PLEN
    t, h = iota((BLK, rows), 0), iota((BLK, rows), 1)
    slot, i = h >> 5, h & (PLEN - 1)
    start = jnp.where(slot == 0, 0, jnp.where(slot == 1, len0, len0 + len1))
    length = jnp.where(slot == 0, len0, jnp.where(slot == 1, len1, len2))
    live = (i < length) & (h < prompt_rows) & (t < size)
    x = x_ref[...]
    wide = x.astype(F32)
    mean = jnp.sum(wide, axis=1, keepdims=True) / cols
    spread = jnp.sum((wide - mean) ** 2, axis=1, keepdims=True)
    lane = iota((rows, LANES), 1)
    stats = jnp.zeros((rows, LANES), F32)
    for j, term in enumerate(three(mean) + three(spread)):
        stats = jnp.where(lane == 2 + j, term, stats)
    same = (iota((rows, LANES), 0) == lane).astype(BF)
    turned = lax.dot_general(stats.astype(BF), same, (((0,), (0,)), ((), ())), preferred_element_type=F32)
    turned = jnp.concatenate([jnp.zeros((8, LANES), F32), turned[:8]], axis=0)
    for k, out in enumerate(outs):
        q = jnp.bitwise_xor(m, k)
        mine = live & (start + i - q * size == t)
        decode = (h >= prompt_rows) & (t == QROWS + h - prompt_rows) & (q == z)
        y = jnp.dot((mine | decode).astype(BF), x, preferred_element_type=F32)
        out[...] = y.astype(BF)
        out[16:32, :LANES] = (y[16:32, :LANES] + turned).astype(BF)


def deal(scalars, tokens):
    return pl.pallas_call(
        deal_kernel,
        out_shape=[jax.ShapeDtypeStruct((BLK, tokens.shape[1]), BF)] * NM,
        in_specs=[SMEM, VMEM],
        out_specs=[VMEM] * NM,
        compiler_params=limit(24),
        cost_estimate=SMALL,
        name="deal_rows",
    )(scalars, tokens)


def norm_kernel(s_ref, b0, b1, b2, b3, affine_ref, table_ref, _, __, o0, o1, o2, o3, held):
    z, m = s_ref[3], s_ref[4]
    cols = b0.shape[1]
    for k, ref in enumerate((b0, b1, b2, b3)):
        held[k] = ref[...].astype(F32)
    width = NM * cols
    means, spreads = [], []
    for k in range(NM):
        part = held[k, 24:32, :LANES]
        means.append(part[2:3] + part[3:4] + part[4:5])
        spreads.append(part[5:6] + part[6:7] + part[7:8])
    mean = sum(means) / NM
    var = (sum(spreads) + cols * sum((v - mean) ** 2 for v in means)) / width
    row = iota((BLK, LANES), 0)
    extra = []
    for value in (mean, lax.rsqrt(var + 1e-05)):
        block = jnp.zeros((BLK, LANES), F32)
        for j, term in enumerate(three(value)):
            block = jnp.where(row == STAT_ROW + j, term, block)
        extra.append(block)
    extra = jnp.concatenate(extra, axis=1)
    extra = jnp.where(iota(extra.shape, 0) == BLK - 1, table_ref[:, : 2 * LANES], extra)
    mean = sum(jnp.sum(held[k], axis=1, keepdims=True) for k in range(NM)) / width
    var = sum(jnp.sum((held[k] - mean) ** 2, axis=1, keepdims=True) for k in range(NM)) / width
    rstd = lax.rsqrt(var + 1e-05)
    last = iota((BLK, cols), 0) == BLK - 1
    stats = iota((BLK, 2 * LANES), 0) >= STAT_ROW
    for k, out in enumerate((o0, o1, o2, o3)):
        block = jnp.bitwise_xor(z, k)
        x = held[jnp.bitwise_xor(block, m)]
        y = (x - mean) * rstd * affine_ref[block] + affine_ref[NM + block]
        y = jnp.where(last, table_ref[...], y)
        out[...] = y.astype(BF)
        out[:, : 2 * LANES] = jnp.where(stats, extra, y[:, : 2 * LANES]).astype(BF)


def norm_rows(scalars, blocks, affine, table, near, far):
    return pl.pallas_call(
        norm_kernel,
        out_shape=[jax.ShapeDtypeStruct(blocks[0].shape, BF)] * NZ,
        in_specs=[SMEM] + [VMEM] * 6 + [ANY] * 2,
        out_specs=[VMEM] * NZ,
        scratch_shapes=[pltpu.VMEM((NM,) + blocks[0].shape, F32)],
        compiler_params=limit(32),
        cost_estimate=SMALL,
        name="norm_rows",
    )(scalars, *blocks, affine, table, near, far)


def cores_kernel(s_ref, b0, b1, b2, b3, mine_ref, theirs_ref):
    core = s_ref[6]
    width = mine_ref.shape[1]
    for k, ref in enumerate((b0, b1, b2, b3)):
        rows = slice(k * BLK, (k + 1) * BLK)
        mine_ref[rows, :] = ref[:, pl.ds(pl.multiple_of(core * width, LANES), width)]
        theirs_ref[rows, :] = ref[:, pl.ds(pl.multiple_of((1 - core) * width, LANES), width)]


def split_cores(scalars, blocks):
    out = jax.ShapeDtypeStruct((NZ * BLK, blocks[0].shape[1] // 2), BF)
    return pl.pallas_call(
        cores_kernel,
        out_shape=[out, out],
        in_specs=[SMEM] + [VMEM] * NZ,
        out_specs=[VMEM] * 2,
        compiler_params=limit(16),
        cost_estimate=SMALL,
        name="split_cores",
    )(scalars, *blocks)


def pack_kernel(s_ref, t_ref, a_ref, b_ref, o_ref):
    found = sources(s_ref, t_ref)
    half = a_ref.shape[0]
    lane = iota((1, half), 1)
    total = None
    for other, ref in enumerate((a_ref, b_ref)):
        to = chunk_places(found, other, lane & (BLK - 1), lane // BLK, s_ref[4])
        pick = (iota((o_ref.shape[0], half), 0) == to).astype(BF)
        term = jnp.dot(pick, ref[...], preferred_element_type=F32)
        total = term if total is None else total + term
    o_ref[...] = total.astype(BF)


def pack_rows(scalars, tables, mine, theirs):
    return pl.pallas_call(
        pack_kernel,
        out_shape=jax.ShapeDtypeStruct((CHUNK + DCH, mine.shape[1]), BF),
        in_specs=[SMEM] * 2 + [VMEM] * 2,
        out_specs=VMEM,
        compiler_params=limit(16),
        cost_estimate=SMALL,
        name="pack_rows",
    )(scalars, tables, mine, theirs)


def copy_kernel(x_ref, _, o_ref):
    o_ref[...] = x_ref[...]


def copy_rows(x, after):
    return pl.pallas_call(
        copy_kernel,
        out_shape=jax.ShapeDtypeStruct(x.shape, x.dtype),
        in_specs=[VMEM, ANY],
        out_specs=VMEM,
        compiler_params=limit(16),
        cost_estimate=SMALL,
        name="copy_rows",
    )(x, after)


def code_kernel(s_ref, t_ref, _, col_ref, row_ref):
    found = sources(s_ref, t_ref)
    m, core = s_ref[4], s_ref[6]
    n = NM * CHUNK
    lane, sub = iota((1, LANES), 1), iota((LANES, 1), 0)
    down, across = iota((n, LANES), 0), iota((LANES, n), 1)
    cols, rows = jnp.zeros((n, 1), jnp.int32), jnp.zeros((1, n), jnp.int32)
    for j, a in enumerate(found):
        first = a.index * SLOTS * PLEN + 1
        hit = down == packed_places(a, j, lane, m, core)
        cols = cols + jnp.sum(jnp.where(hit, first + lane, 0), axis=1, keepdims=True)
        hit = across == packed_places(a, j, sub, m, core)
        rows = rows + jnp.sum(jnp.where(hit, first + sub, 0), axis=0, keepdims=True)
    unused = (1 << 16) + PLEN * iota((n, 1), 0)
    col_ref[...] = jnp.where(cols > 0, cols - 1, unused)
    unused = (1 << 16) + PLEN * iota((1, n), 1)
    row_ref[...] = jnp.where(rows > 0, rows - 1, unused)


def packed_codes(scalars, tables, after):
    n = NM * CHUNK
    return pl.pallas_call(
        code_kernel,
        out_shape=[jax.ShapeDtypeStruct((n, 1), jnp.int32), jax.ShapeDtypeStruct((1, n), jnp.int32)],
        in_specs=[SMEM] * 2 + [ANY],
        out_specs=[VMEM] * 2,
        compiler_params=limit(16),
        cost_estimate=SMALL,
        name="packed_codes",
    )(scalars, tables, after)


def rank_kernel(s_ref, table_ref, da_ref, db_ref, x0, x1, x2, x3, t0, t1, t2, t3, affine_ref, o_ref):
    m, r = s_ref[4], s_ref[5]
    width = 2 * ADAPTER_RANK
    count = da_ref.shape[0] // width
    rows = x0.shape[0]
    same = (iota((rows, LANES), 0) == iota((rows, LANES), 1)).astype(BF)
    o_ref[...] = jnp.zeros_like(o_ref)
    for k, (x, stats) in enumerate(zip((x0, x1, x2, x3), (t0, t1, t2, t3))):

        def column(at):
            turned = lax.dot_general(
                same, stats[16:32, at], (((1,), (1,)), ((), ())), preferred_element_type=F32
            )
            j = STAT_ROW - 16
            return turned[:, j : j + 1] + turned[:, j + 1 : j + 2] + turned[:, j + 2 : j + 3]

        mean, rstd = column(slice(0, LANES)), column(slice(LANES, 2 * LANES))
        normed = ((x[...].astype(F32) - mean) * rstd * affine_ref[m] + affine_ref[NM + m]).astype(BF)
        ids = home_adapters(Source(s_ref, table_ref, k), iota((1, rows), 1))
        total = jnp.zeros((width, rows), F32)
        for core, d in enumerate((da_ref, db_ref)):
            y = lax.dot_general(d[...], normed, (((1,), (1,)), ((), ())), preferred_element_type=F32)
            first = jnp.bitwise_xor(r, core) * count
            for a in range(count):
                total = total + jnp.where(ids == first + a, y[a * width : (a + 1) * width], 0.0)
        o_ref[:, k * LANES : k * LANES + rows] = total


def low_rank_rows(scalars, tables, down, down_other, pieces, stats, affine):
    return pl.pallas_call(
        rank_kernel,
        out_shape=jax.ShapeDtypeStruct((2 * ADAPTER_RANK, NZ * LANES), F32),
        in_specs=[SMEM] * 2 + [VMEM] * 11,
        out_specs=VMEM,
        compiler_params=limit(32),
        cost_estimate=SMALL,
        name="low_rank_rows",
    )(scalars, tables, down, down_other, *pieces, *stats, affine)


def expand_kernel(s_ref, t_ref, low_ref, low_other_ref, base_ref, key_ref, up_ref, _, o_ref, keep_ref, send_ref, *, count):
    m, r, core = s_ref[4], s_ref[5], s_ref[6]
    found = sources(s_ref, t_ref)
    width = count * ADAPTER_RANK
    repeat = []
    for t in range(2):
        shape = (width, 2 * ADAPTER_RANK)
        repeat.append((iota(shape, 1) == t * ADAPTER_RANK + iota(shape, 0) % ADAPTER_RANK).astype(BF))
    repeat = jnp.concatenate(repeat, axis=0)
    adapter = r * count + (iota((2 * width, LANES), 0) % width) // ADAPTER_RANK
    lane = iota((1, LANES), 1)
    total = jnp.zeros((PACKED, 2 * width), F32)
    for j, a in enumerate(found):
        ref = low_other_ref if j >= NZ else low_ref
        k = j % NZ
        low = jnp.dot(repeat, ref[:, k * LANES : (k + 1) * LANES], preferred_element_type=F32)
        low = jnp.where(adapter == home_adapters(a, lane), low, 0.0).astype(BF)
        hit = (iota((PACKED, LANES), 0) == packed_places(a, j, lane, m, core)).astype(BF)
        total = total + lax.dot_general(hit, low, (((1,), (1,)), ((), ())), preferred_element_type=F32)
    feats = up_ref.shape[3]
    half = keep_ref.shape[0]
    keep_ref[:, feats : 2 * feats] = key_ref[:half, :]
    send_ref[:, feats : 2 * feats] = key_ref[half:, :]
    for t, first in ((0, 0), (1, 2 * feats)):
        rows = total[:, t * width : (t + 1) * width].astype(BF)
        o_ref[t] = rows
        up = up_ref[:, t].reshape(-1, feats)
        term = jnp.dot(rows[NM * CHUNK :, :], up, preferred_element_type=F32)
        term = term + base_ref[:, t * feats : (t + 1) * feats]
        keep_ref[:, first : first + feats] = term[:half]
        send_ref[:, first : first + feats] = term[half:]


def expand_rows(scalars, tables, low, low_other, base, keys, up, count, after):
    half = jax.ShapeDtypeStruct((keys.shape[0] // 2, 3 * keys.shape[1]), F32)
    return pl.pallas_call(
        functools.partial(expand_kernel, count=count),
        out_shape=[jax.ShapeDtypeStruct((2, PACKED, count * ADAPTER_RANK), BF), half, half],
        in_specs=[SMEM] * 2 + [VMEM] * 5 + [ANY],
        out_specs=[VMEM] * 3,
        compiler_params=limit(32),
        cost_estimate=SMALL,
        name="expand_rows",
    )(scalars, tables, low, low_other, base, keys, up, after)


def emit_sums(y, own_ref, other_ref):
    half = 2 * CHUNK
    own_ref[...] = y[:half].astype(BF)
    other_ref[...] = y[half : 2 * half].astype(BF)


def first_project_kernel(s_ref, c0, c1, c2, c3, w_ref, _, own_ref, other_ref, dec_ref, x):
    z, m, core = s_ref[3], s_ref[4], s_ref[6]

    @pl.when(pl.program_id(0) == 0)
    def _():
        chunks = (c0, c1, c2, c3)
        for k, chunk in enumerate(chunks):
            base = jnp.bitwise_xor(core, k >> 1) * 2 * CHUNK + (k & 1) * CHUNK
            x[pl.ds(pl.multiple_of(base, CHUNK), CHUNK), :] = chunk[:CHUNK, :]
        n, at = iota((2 * NZ * DEC, NM * DCH), 0), iota((2 * NZ * DEC, NM * DCH), 1)
        chip = jnp.bitwise_xor(z, turned_bits((n >> 1) & 3))
        want = jnp.bitwise_xor(chip, m) * DCH + jnp.bitwise_xor(core, n >> 3) * DEC + (n & 1)
        rows = jnp.concatenate([chunk[CHUNK:, :] for chunk in chunks], axis=0)
        x[NM * CHUNK :, :] = jnp.dot((want == at).astype(BF), rows, preferred_element_type=F32).astype(BF)

    y = jnp.dot(x[...], w_ref[0], preferred_element_type=F32)
    emit_sums(y, own_ref, other_ref)
    dec_ref[...] = y[NM * CHUNK :]


def project_rows(scalars, chunks, weight, part, after):
    _, depth, feats = weight.shape
    tile = feats // 2
    half = 2 * CHUNK
    whole = [pl.BlockSpec(v.shape, lambda j: (0, 0)) for v in chunks]
    out_shape = [
        jax.ShapeDtypeStruct((half, feats), BF),
        jax.ShapeDtypeStruct((half, feats), BF),
        jax.ShapeDtypeStruct((PACKED - NM * CHUNK, feats), F32),
        jax.ShapeDtypeStruct((PACKED, depth), BF),
    ]
    out_specs = [pl.BlockSpec((v.shape[0], tile), lambda j: (0, j)) for v in out_shape[:3]]
    out_specs.append(pl.BlockSpec((PACKED, depth), lambda j: (0, 0)))
    return pl.pallas_call(
        first_project_kernel,
        grid=(feats // tile,),
        out_shape=out_shape,
        in_specs=[SMEM] + whole + [pl.BlockSpec((1, depth, tile), lambda j: (part, 0, j)), ANY],
        out_specs=out_specs,
        compiler_params=limit(56),
        cost_estimate=SMALL,
        name="project_keys",
    )(scalars, *chunks, weight, after)


def adapted_kernel(x_ref, w_ref, e_ref, u_ref, _, *outs):
    y = jnp.dot(x_ref[: NM * CHUNK, :], w_ref[0], preferred_element_type=F32)
    up = u_ref[...].reshape(-1, u_ref.shape[-1])
    y = y + jnp.dot(e_ref[0, : NM * CHUNK, :], up, preferred_element_type=F32)
    emit_sums(y, *outs)


def project_adapted(rows, weight, part, expanded, up, after):
    _, depth, feats = weight.shape
    tile = feats // 2
    half = 2 * CHUNK
    which = part // 2
    out_shape = [
        jax.ShapeDtypeStruct((half, feats), BF),
        jax.ShapeDtypeStruct((half, feats), BF),
    ]
    return pl.pallas_call(
        adapted_kernel,
        grid=(2,),
        out_shape=out_shape,
        in_specs=[
            pl.BlockSpec(rows.shape, lambda j: (0, 0)),
            pl.BlockSpec((1, depth, tile), lambda j: (part, 0, j)),
            pl.BlockSpec((1,) + expanded.shape[1:], lambda j: (which, 0, 0)),
            pl.BlockSpec((up.shape[0], 1, up.shape[2], tile), lambda j: (0, which, 0, j)),
            ANY,
        ],
        out_specs=[pl.BlockSpec((v.shape[0], tile), lambda j: (0, j)) for v in out_shape],
        compiler_params=limit(56),
        cost_estimate=SMALL,
        name="project_adapted",
    )(rows, weight, expanded, up, after)


def add_kernel(a_ref, b_ref, _, o_ref):
    o_ref[...] = (a_ref[: b_ref.shape[0], :] + b_ref[...]).astype(o_ref.dtype)


def add_rows(a, b, after, dtype=F32):
    return pl.pallas_call(
        add_kernel,
        out_shape=jax.ShapeDtypeStruct(b.shape, dtype),
        in_specs=[VMEM] * 2 + [ANY],
        out_specs=VMEM,
        compiler_params=limit(16),
        cost_estimate=SMALL,
        name="add_rows",
    )(a, b, after)


def decode_finish_kernel(a_ref, b_ref, bias_ref, _, q_ref, k_ref, v_ref):
    total = a_ref[: b_ref.shape[0], :] + b_ref[...]
    feats = bias_ref.shape[1]
    for j, out in enumerate((q_ref, k_ref, v_ref)):
        part = total[:, j * feats : (j + 1) * feats] + bias_ref[j : j + 1, :]
        for i in range(out.shape[0]):
            out[i] = part[i : i + 1].astype(BF)


def decode_finish(a, b, bias, after):
    out = jax.ShapeDtypeStruct((b.shape[0], 1, bias.shape[1]), BF)
    return pl.pallas_call(
        decode_finish_kernel,
        out_shape=[out] * 3,
        in_specs=[VMEM] * 3 + [ANY],
        out_specs=[VMEM] * 3,
        compiler_params=limit(16),
        cost_estimate=SMALL,
        name="decode_finish",
    )(a, b, bias, after)


def decode_base_kernel(x_ref, w_ref, _, o_ref):
    o_ref[...] = jnp.dot(x_ref[...], w_ref[0], preferred_element_type=F32)


def decode_base(rows, weight, after):
    _, depth, feats = weight.shape
    count = PACKED - NM * CHUNK
    return pl.pallas_call(
        decode_base_kernel,
        grid=(2,),
        out_shape=jax.ShapeDtypeStruct((count, 2 * feats), F32),
        in_specs=[
            pl.BlockSpec((count, depth), lambda p: (NM * CHUNK // count, 0)),
            pl.BlockSpec((1, depth, feats), lambda p: (2 * p, 0, 0)),
            ANY,
        ],
        out_specs=pl.BlockSpec((count, feats), lambda p: (0, p)),
        compiler_params=limit(56),
        cost_estimate=SMALL,
        name="decode_base",
    )(rows, weight, after)


def halve_kernel(s_ref, *refs, bit, groups):
    *ins, _, send_ref, keep_ref = refs
    count = len(ins) // 2
    side = (s_ref[3] >> bit) & 1
    to = 0
    for total_ref, got_ref in zip(ins[:count], ins[count:]):
        width = total_ref.shape[1] // groups // 2

        for g in range(groups):

            def part(which):
                at = pl.ds(pl.multiple_of((2 * g + which) * width, LANES), width)
                return total_ref[:, at].astype(F32) + got_ref[:, at].astype(F32)

            send_ref[:, to : to + width] = part(1 - side).astype(BF)
            keep_ref[:, to : to + width] = part(side)
            to += width


def halve(scalars, totals, gots, bit, after, groups=1):
    rows = totals[0].shape[0]
    feats = sum(v.shape[1] for v in totals) // 2
    return pl.pallas_call(
        functools.partial(halve_kernel, bit=bit, groups=groups),
        out_shape=[jax.ShapeDtypeStruct((rows, feats), BF), jax.ShapeDtypeStruct((rows, feats), F32)],
        in_specs=[SMEM] + [VMEM] * (2 * len(totals)) + [ANY],
        out_specs=[VMEM, VMEM],
        compiler_params=limit(24),
        cost_estimate=SMALL,
        name="halve_sums",
    )(scalars, *totals, *gots, after)


def finish_kernel(s_ref, total_ref, got_ref, bias_ref, _, *outs, parts):
    for j, (part, out) in enumerate(zip(parts, outs)):
        width = out.shape[1]
        at = pl.ds(pl.multiple_of(place_of(s_ref[3]) * width, LANES), width)
        mine = slice(j * width, (j + 1) * width)
        total = total_ref[:, mine] + got_ref[:, mine].astype(F32) + bias_ref[part : part + 1, at]
        out[...] = total.astype(BF)


def finish(scalars, total, got, bias, parts, after):
    rows, feats = total.shape
    return pl.pallas_call(
        functools.partial(finish_kernel, parts=parts),
        out_shape=[jax.ShapeDtypeStruct((rows, feats // len(parts)), BF)] * len(parts),
        in_specs=[SMEM, VMEM, VMEM, VMEM, ANY],
        out_specs=[VMEM] * len(parts),
        compiler_params=limit(16),
        cost_estimate=SMALL,
        name="finish_sums",
    )(scalars, total, got, bias, after)


def prompt_kernel(q_ref, ka_ref, kb_ref, va_ref, vb_ref, cr_ref, cc_ref, d_ref, o_ref):
    rows = cr_ref[...]
    cols = cc_ref[...]
    allowed = ((rows >> 5) == (cols >> 5)) & (cols <= rows)
    keys = jnp.concatenate([ka_ref[...], kb_ref[...]], axis=0)
    values = jnp.concatenate([va_ref[...], vb_ref[...]], axis=0)
    for h in range(q_ref.shape[1] // HEAD_DIM):
        at = slice(h * HEAD_DIM, (h + 1) * HEAD_DIM)
        s = lax.dot_general(q_ref[:, at], keys[:, at], (((1,), (1,)), ((), ())), preferred_element_type=F32)
        s = jnp.where(allowed, s * HEAD_DIM**-0.5, -1e30)
        top = jnp.max(s, axis=1, keepdims=True)
        w = jnp.where(allowed, jnp.exp(s - top), 0.0)
        w = (w / jnp.sum(w, axis=1, keepdims=True)).astype(BF)
        o_ref[: q_ref.shape[0], at] = jnp.dot(w, values[:, at], preferred_element_type=F32).astype(BF)
    width = q_ref.shape[1]
    n = iota((DECODE_ROWS, width), 0)
    tail = jnp.zeros((DECODE_ROWS, width), F32)
    for b in range(NZ):
        for j in range(DEC):
            tail = jnp.where(n == b * DEC + j, d_ref[j : j + 1, b * width : (b + 1) * width].astype(F32), tail)
    o_ref[q_ref.shape[0] :, :] = tail.astype(BF)


def prompt_attention(q, ka, kb, va, vb, code_rows, code_cols, dec):
    return pl.pallas_call(
        prompt_kernel,
        out_shape=jax.ShapeDtypeStruct((q.shape[0] + DECODE_ROWS, q.shape[1]), BF),
        in_specs=[VMEM] * 8,
        out_specs=VMEM,
        compiler_params=limit(32),
        cost_estimate=SMALL,
        name="prompt_attention",
    )(q, ka, kb, va, vb, code_rows, code_cols, dec)


def decode_kernel(len_ref, q_ref, k_ref, v_ref, c_ref, _, o_ref, qbd, top, total, acc):
    d, t = pl.program_id(0), pl.program_id(1)
    span = c_ref.shape[1]
    live = len_ref[d]
    heads, feats = qbd.shape
    diag = lax.broadcasted_iota(jnp.int32, (heads, feats), 1) // HEAD_DIM == lax.broadcasted_iota(
        jnp.int32, (heads, feats), 0
    )

    @pl.when(t == 0)
    def _():
        q = jnp.where(diag, q_ref[0].astype(F32), 0.0)
        qbd[...] = q.astype(BF)
        own = jnp.sum(q * k_ref[0].astype(F32), axis=1, keepdims=True) * HEAD_DIM**-0.5
        top[...] = jnp.broadcast_to(own, top.shape)
        total[...] = jnp.ones_like(total)
        acc[...] = jnp.broadcast_to(v_ref[0].astype(F32), acc.shape)

    @pl.when(t * span < live)
    def _():
        x = c_ref[0].reshape(2 * span, feats)
        s = lax.dot_general(qbd[...], x, (((1,), (1,)), ((), ())), preferred_element_type=F32)
        column = lax.broadcasted_iota(jnp.int32, s.shape, 1)
        valid = (column % 2 == 0) & (t * span + column // 2 < live)
        s = jnp.where(valid, s * HEAD_DIM**-0.5, -1e30)
        before = top[:, :1]
        now = jnp.maximum(before, jnp.max(s, axis=1, keepdims=True))
        fade = jnp.exp(before - now)
        w = jnp.where(valid, jnp.exp(s - now), 0.0)
        total[...] = total[...] * fade + jnp.sum(w, axis=1, keepdims=True)
        top[...] = jnp.broadcast_to(now, top.shape)
        w = pltpu.roll(w, 1, 1).astype(BF)
        acc[...] = acc[...] * fade + jnp.dot(w, x, preferred_element_type=F32)

    @pl.when(t == pl.num_programs(1) - 1)
    def _():
        o = acc[...] / total[:, :1]
        o_ref[0] = jnp.sum(jnp.where(diag, o, 0.0), axis=0, keepdims=True).astype(BF)


def decode_attention(lengths, q, k, v, cache, after, span=256):
    count, positions, _, feats = cache.shape
    row = pl.BlockSpec((1, 1, feats), lambda d, t, n: (d, 0, 0))
    heads = 16
    return pl.pallas_call(
        decode_kernel,
        grid_spec=pltpu.PrefetchScalarGridSpec(
            num_scalar_prefetch=1,
            grid=(count, positions // span),
            in_specs=[row, row, row]
            + [pl.BlockSpec((1, span, 2, feats), lambda d, t, n: (d, jnp.minimum(t, (n[d] - 1) // span), 0, 0)), ANY],
            out_specs=row,
            scratch_shapes=[
                pltpu.VMEM((heads, feats), BF),
                pltpu.VMEM((heads, LANES), F32),
                pltpu.VMEM((heads, LANES), F32),
                pltpu.VMEM((heads, feats), F32),
            ],
        ),
        out_shape=jax.ShapeDtypeStruct((count, 1, feats), BF),
        compiler_params=limit(32),
        cost_estimate=SMALL,
        name="decode_attention",
    )(lengths, q, k, v, cache, after)


def out_term(z, k, own, other, w_ref):
    width = own.shape[1]
    half = own.shape[0] - DECODE_ROWS
    block = place_of(jnp.bitwise_xor(z, k))
    w = w_ref[pl.ds(pl.multiple_of(block * width, width), width), :]
    rows = jnp.concatenate([own[:half, :], other[:half, :]], axis=0)
    return jnp.dot(rows, w, preferred_element_type=F32)


def out_first_kernel(place_ref, *refs):
    own, other, w_ref, o_ref = refs[:3], refs[3:6], refs[6], refs[7]
    total = None
    for k in range(NZ - 1):
        term = out_term(place_ref[3], k, own[k], other[k], w_ref)
        total = term if total is None else total + term
    o_ref[...] = total


def out_first(scalars, own, other, weight):
    return pl.pallas_call(
        out_first_kernel,
        out_shape=jax.ShapeDtypeStruct((NM * CHUNK, weight.shape[1]), F32),
        in_specs=[SMEM] + [VMEM] * 7,
        out_specs=VMEM,
        compiler_params=limit(40),
        cost_estimate=SMALL,
        name="out_first",
    )(scalars, *own[:3], *other[:3], weight)


def out_kernel(place_ref, *refs):
    own, other, first_ref, w_ref, outs, mixed = refs[:4], refs[4:8], refs[8], refs[9], refs[10:14], refs[14]
    z, m, core = place_ref[3], place_ref[4], place_ref[6]
    width = own[0].shape[1]
    half = own[0].shape[0] - DECODE_ROWS
    mixed[...] = (first_ref[...] + out_term(z, NZ - 1, own[-1], other[-1], w_ref)).astype(BF)
    tails = jnp.concatenate([v[half:, :] for v in own + other], axis=0)
    count = 2 * NZ * DEC
    n, at = iota((count, tails.shape[0]), 0), iota((count, tails.shape[0]), 1)
    total = None
    for b in range(NZ):
        pick = (at == (n // DEC) * DECODE_ROWS + b * DEC + n % DEC).astype(BF)
        rows = jnp.dot(pick, tails, preferred_element_type=F32).astype(BF)
        term = jnp.dot(rows, w_ref[b * width : (b + 1) * width, :], preferred_element_type=F32)
        total = term if total is None else total + term
    decode = total.astype(BF)
    n, at = iota((DCH, count), 0), iota((DCH, count), 1)
    for k, out in enumerate(outs):
        base = jnp.bitwise_xor(core, k >> 1) * 2 * CHUNK + (k & 1) * CHUNK
        out[:CHUNK, :] = mixed[pl.ds(pl.multiple_of(base, CHUNK), CHUNK), :]
        far = jnp.bitwise_xor(jnp.bitwise_xor(m, k), z)
        want = (jnp.bitwise_xor(core, n >> 1) * NZ + far) * DEC + (n & 1)
        pick = ((at == want) & (n < 2 * DEC)).astype(BF)
        out[CHUNK:, :] = jnp.dot(pick, decode, preferred_element_type=F32).astype(BF)


def out_project(scalars, own, other, first, weight):
    feats = weight.shape[1]
    return pl.pallas_call(
        out_kernel,
        out_shape=[jax.ShapeDtypeStruct((CHUNK + DCH, feats), BF)] * NM,
        in_specs=[SMEM] + [VMEM] * 10,
        out_specs=[VMEM] * NM,
        scratch_shapes=[pltpu.VMEM((NM * CHUNK, feats), BF)],
        compiler_params=limit(40),
        cost_estimate=SMALL,
        name="out_project",
    )(scalars, *own, *other, first, weight)


def unpack_kernel(s_ref, t_ref, c0, c1, c2, c3, *outs):
    total = sum(c[...].astype(F32) for c in (c0, c1, c2, c3)).astype(BF)
    found = sources(s_ref, t_ref)
    n = iota((NZ * BLK, 1), 0)
    for other in range(2):
        to = chunk_places(found, other, n & (BLK - 1), n // BLK, s_ref[4])
        pick = (iota((NZ * BLK, total.shape[0]), 1) == to).astype(BF)
        rows = jnp.dot(pick, total, preferred_element_type=F32).astype(BF)
        for k, out in enumerate(outs):
            out[other * BLK : (other + 1) * BLK, :] = rows[k * BLK : (k + 1) * BLK]


def unpack_rows(scalars, tables, chunks):
    feats = chunks[0].shape[1]
    return pl.pallas_call(
        unpack_kernel,
        out_shape=[jax.ShapeDtypeStruct((2 * BLK, feats), BF)] * NZ,
        in_specs=[SMEM] * 2 + [VMEM] * 4,
        out_specs=[VMEM] * NZ,
        compiler_params=limit(16),
        cost_estimate=SMALL,
        name="unpack_rows",
    )(scalars, tables, *chunks)


def join_kernel(s_ref, a0, a1, a2, a3, other_ref, o0, o1, o2, o3, held):
    z, m, core = s_ref[3], s_ref[4], s_ref[6]
    width = a0.shape[1]
    mine = pl.ds(pl.multiple_of(core * width, LANES), width)
    theirs = pl.ds(pl.multiple_of((1 - core) * width, LANES), width)
    for k, ref in enumerate((a0, a1, a2, a3)):
        held[k, :, mine] = ref[:BLK, :]
        held[k, :, theirs] = other_ref[k * BLK : (k + 1) * BLK, :]
    for k, out in enumerate((o0, o1, o2, o3)):
        out[...] = held[jnp.bitwise_xor(jnp.bitwise_xor(z, m), k)]


def join_halves(scalars, parts, other):
    shape = (BLK, 2 * parts[0].shape[1])
    return pl.pallas_call(
        join_kernel,
        out_shape=[jax.ShapeDtypeStruct(shape, BF)] * NM,
        in_specs=[SMEM] + [VMEM] * 5,
        out_specs=[VMEM] * NM,
        scratch_shapes=[pltpu.VMEM((NZ,) + shape, BF)],
        compiler_params=limit(16),
        cost_estimate=SMALL,
        name="join_halves",
    )(scalars, *parts, other)


def home_kernel(s_ref, x_ref, bias_ref, b0, b1, b2, b3, o_ref):
    len0, len1, len2, z, m = [s_ref[i] for i in range(5)]
    size = (len0 + len1 + len2 + 3) >> 2
    rows = x_ref.shape[0]
    prompt_rows = SLOTS * PLEN
    t, h = iota((rows, BLK), 1), iota((rows, BLK), 0)
    slot, i = h >> 5, h & (PLEN - 1)
    start = jnp.where(slot == 0, 0, jnp.where(slot == 1, len0, len0 + len1))
    length = jnp.where(slot == 0, len0, jnp.where(slot == 1, len1, len2))
    live = (i < length) & (h < prompt_rows) & (t < size)
    total = x_ref[...].astype(F32) + bias_ref[...]
    for k, ref in enumerate((b0, b1, b2, b3)):
        q = jnp.bitwise_xor(m, k)
        mine = live & (start + i - q * size == t)
        decode = (h >= prompt_rows) & (t == QROWS + h - prompt_rows) & (q == z)
        total = total + jnp.dot((mine | decode).astype(BF), ref[...], preferred_element_type=F32)
    o_ref[...] = total.astype(BF)


def add_home(scalars, tokens, bias, blocks):
    return pl.pallas_call(
        home_kernel,
        out_shape=jax.ShapeDtypeStruct(tokens.shape, BF),
        in_specs=[SMEM] + [VMEM] * 6,
        out_specs=VMEM,
        compiler_params=limit(24),
        cost_estimate=SMALL,
        name="add_home",
    )(scalars, tokens, bias, *blocks)


def turned_bits(k):
    return (k & 1) * 2 + (k >> 1)


def place_of(z):
    return turned_bits(z)


def packed_device(
    tokens,
    layernorm_scale,
    layernorm_bias,
    query_key_value_weight,
    query_key_value_bias,
    adapter_down_weight,
    adapter_up_weight,
    adapter_index_table,
    prompt_length_list,
    cache,
    cache_length_list,
    output_weight,
    output_bias,
):
    i32 = jnp.int32
    r = lax.axis_index("req").astype(i32)
    m = lax.axis_index("mp").astype(i32)
    z, c = r >> 1, r & 1
    rows_dev, cols = tokens.shape
    prompt_rows = SLOTS * PLEN
    feats = query_key_value_weight.shape[2]
    depth = query_key_value_weight.shape[1]
    per_z = feats // NZ
    own_adapters = adapter_down_weight.shape[0]
    half = 2 * CHUNK
    order = jnp.arange(2 * NZ, dtype=i32)
    source = ((z ^ (order & 3)) << 1) + (c ^ (order >> 2))
    lens = prompt_length_list
    scalars = jnp.concatenate([lens, jnp.stack([z, m, r, c])])

    down = jnp.transpose(adapter_down_weight, (0, 2, 1)).reshape(own_adapters * 2 * ADAPTER_RANK, cols)

    with jax.named_scope("deal"):
        dealt = deal(scalars, tokens)
    with jax.named_scope("gather_home"):
        pieces = gather_z(tokens)
    with jax.named_scope("deal"):
        blocks = [dealt[0]] + [swap_mp(dealt[k], k) for k in range(1, NM)]
    with jax.named_scope("norm_rows"):
        table = jnp.concatenate([lens, adapter_index_table[0]]).astype(F32)
        table = jnp.pad(table, (0, depth - table.shape[0]))
        table = jnp.tile(table, 2)[None, :]
        affine = jnp.stack([layernorm_scale, layernorm_bias]).reshape(2 * NM, 1, cols)
        normed = norm_rows(scalars, blocks, affine, table, pieces[1], pieces[2])
    with jax.named_scope("spread_z"):
        spread = [normed[0]] + [swap_req(normed[k], 2 * k) for k in range(1, NZ)]
        mine, theirs = split_cores(scalars, spread)
        theirs = swap_req(theirs, 1)

    with jax.named_scope("tables"):
        tables = jnp.concatenate(
            [v.reshape(NZ, BLK, depth)[:, BLK - 1, : SLOTS + SLOTS + DEC] for v in (mine, theirs)], axis=0
        ).astype(i32)
    with jax.named_scope("pack"):
        chunk = pack_rows(scalars, tables, mine, theirs)
    with jax.named_scope("gather_chunks"):
        chunks = [chunk] + [swap_mp(chunk, k) for k in range(1, NM)]

    with jax.named_scope("low_rank"):
        down_other = swap_req(copy_rows(down, mine), 1)
        part = low_rank_rows(scalars, tables, down, down_other, pieces, spread, affine)
    with jax.named_scope("keys"):
        own_k, other_k, dec_k, x_rows = project_rows(scalars, chunks, query_key_value_weight, 1, part)
        core_k = swap_req(other_k, 1)
    with jax.named_scope("decode_rows"):
        base = decode_base(x_rows, query_key_value_weight, other_k)
    with jax.named_scope("low_rank"):
        two = add_rows(part, swap_mp(part, 1), base)
    with jax.named_scope("keys"):
        send_k, keep_k = halve(scalars, [own_k], [core_k], 0, two)
        got_k = swap_req(send_k, 2)
    with jax.named_scope("low_rank"):
        code_col, code_row = packed_codes(scalars, tables, send_k)
        low_rank = add_rows(two, swap_mp(two, 2), code_row, BF)
        expanded, dec, dec_sent = expand_rows(
            scalars, tables, low_rank, swap_req(low_rank, 1), base, dec_k, adapter_up_weight, own_adapters, base
        )
    with jax.named_scope("decode_rows"):
        dec_chip = add_rows(dec, swap_req(dec_sent, 1), expanded)
    with jax.named_scope("keys"):
        send_k, keep_k = halve(scalars, [keep_k], [got_k], 1, dec_chip)
        got_k = swap_req(send_k, 4)
    with jax.named_scope("values"):
        own_v, other_v = project_adapted(x_rows, query_key_value_weight, 2, expanded, adapter_up_weight, send_k)
        core_v = swap_req(other_v, 1)
    with jax.named_scope("decode_rows"):
        dec_pair = add_rows(dec_chip, swap_req(dec_chip[4:], 2), own_v)
    with jax.named_scope("keys"):
        (keys,) = finish(scalars, keep_k, got_k, query_key_value_bias, (1,), dec_pair)
        keys_other = swap_req(keys, 1)
    with jax.named_scope("decode_rows"):
        dec = decode_finish(dec_pair, swap_req(dec_pair[2:], 4), query_key_value_bias, keys)
    with jax.named_scope("queries"):
        own_q, other_q = project_adapted(x_rows, query_key_value_weight, 0, expanded, adapter_up_weight, dec[0])
        core_q = swap_req(other_q, 1)
    with jax.named_scope("reduce_z"):
        send, keep = halve(scalars, [own_v, own_q], [core_v, core_q], 0, core_q)
        got = swap_req(send, 2)
    with jax.named_scope("reduce_z"):
        send, keep = halve(scalars, [keep], [got], 1, send, groups=2)
        got = swap_req(send, 4)
    with jax.named_scope("decode_attention"):
        dec_out = decode_attention(cache_length_list, *dec, cache, send)
        dec_out = dec_out.reshape(DEC, feats)
    with jax.named_scope("reduce_z"):
        values, queries = finish(scalars, keep, got, query_key_value_bias, (2, 0), dec_out)
        values_other = swap_req(values, 1)
    with jax.named_scope("prompt_attention"):
        attended = prompt_attention(
            queries,
            keys,
            keys_other,
            values,
            values_other,
            code_col[: 2 * CHUNK],
            code_row,
            dec_out,
        )
    with jax.named_scope("gather_attended"):
        own = gather_z(attended)
        other = [swap_req(v, 1) for v in own]
    with jax.named_scope("out_project"):
        first = out_first(scalars, own, other, output_weight)
        mixed = out_project(scalars, own, other, first, output_weight)
    with jax.named_scope("sum_mp"):
        shares = [mixed[0]] + [swap_mp(mixed[k], k) for k in range(1, NM)]
    with jax.named_scope("return_z"):
        back = unpack_rows(scalars, tables, shares)
        back = [back[0]] + [swap_req(back[k], 2 * k) for k in range(1, NZ)]
        back_other = swap_req(jnp.concatenate([v[BLK:] for v in back], axis=0), 1)
    with jax.named_scope("return_plane"):
        joined = join_halves(scalars, back, back_other)
        joined = [joined[0]] + [swap_mp(joined[k], k) for k in range(1, NM)]
        return add_home(scalars, tokens, output_bias[None], joined)


def layer_norm(row_data, gain_vec, shift_vec):
    values = row_data.astype(jnp.float32)
    average = jnp.mean(values, axis=-1, keepdims=True)
    centred = values - average
    variance = jnp.mean(centred * centred, axis=-1, keepdims=True)
    scaled = centred * lax.rsqrt(variance + 1e-05)
    return (scaled * gain_vec + shift_vec).astype(jnp.bfloat16)


def on_device(
    tokens,
    layernorm_scale,
    layernorm_bias,
    query_key_value_weight,
    query_key_value_bias,
    adapter_down_weight,
    adapter_up_weight,
    adapter_index_table,
    prompt_length_list,
    cache,
    cache_length_list,
    output_weight,
    output_bias,
):
    rows_dev = tokens.shape[0]
    part_cols = tokens.shape[1]
    decode_count = cache.shape[0]
    slot_count = prompt_length_list.shape[0]
    prompt_rows = rows_dev - decode_count
    slot_len = prompt_rows // slot_count
    rank_size = ADAPTER_RANK
    head_count = query_key_value_weight.shape[2] // HEAD_DIM
    score_scale = HEAD_DIM ** (-0.5)
    gathered = lax.all_gather(tokens, "mp", axis=1, tiled=True)
    normed = layer_norm(gathered, layernorm_scale, layernorm_bias)
    column = lax.axis_index("mp")
    slice_m = lax.dynamic_slice_in_dim(normed, column * part_cols, part_cols, 1)
    spread = lax.all_to_all(normed, "req", split_axis=1, concat_axis=0, tiled=True)
    projected = lax.psum_scatter(
        jnp.einsum(
            "rd,cde->rce", spread, query_key_value_weight, preferred_element_type=jnp.float32
        ),
        "req",
        scatter_dimension=0,
        tiled=True,
    )
    projected = projected + query_key_value_bias[None]
    positions = jnp.arange(rows_dev)
    request_slot = jnp.where(
        positions < prompt_rows, positions // slot_len, slot_count + positions - prompt_rows
    )
    slot_match = request_slot[:, None] == jnp.arange(slot_count + decode_count)[None, :]
    row_adapter = jnp.sum(jnp.where(slot_match, adapter_index_table[0][None, :], 0), axis=1)
    adapter_on_device = adapter_down_weight.shape[0]
    owners = lax.axis_size("req")
    owner_row = row_adapter // adapter_on_device
    to_owner = owner_row[None, :] == jnp.arange(owners)[:, None]
    outgoing = jnp.where(to_owner[:, :, None], slice_m[None], jnp.zeros((), jnp.bfloat16))
    labels = jnp.where(to_owner, (row_adapter - owner_row * adapter_on_device)[None, :], -1)
    received_rows = lax.all_to_all(outgoing, "req", split_axis=0, concat_axis=0, tiled=True)
    arrived_labels = lax.all_to_all(labels, "req", split_axis=0, concat_axis=0, tiled=True)
    sources, items = arrived_labels.shape
    selection_mask = (
        arrived_labels[:, :, None] == jnp.arange(adapter_on_device)[None, None, :]
    ).astype(jnp.float32)
    adapter_wise_sums = jnp.einsum(
        "yju,ouv->yjov", received_rows, adapter_down_weight, preferred_element_type=jnp.float32
    )
    reduced_rank_rows = jnp.einsum("ogf,ogft->ogt", selection_mask, adapter_wise_sums)
    reduced_rank_rows = lax.psum(reduced_rank_rows, "mp").astype(jnp.bfloat16)
    broadcast_rank_rows = selection_mask.astype(jnp.bfloat16)[
        :, :, :, None, None
    ] * reduced_rank_rows.reshape(sources, items, 1, 2, rank_size)
    corrections = jnp.einsum(
        "pqwgd,wgdx->pqgx",
        broadcast_rank_rows,
        adapter_up_weight,
        preferred_element_type=jnp.float32,
    ).astype(jnp.bfloat16)
    returned = lax.all_to_all(corrections, "req", split_axis=0, concat_axis=0, tiled=True)
    adapter_delta = jnp.sum(returned.astype(jnp.float32), axis=0)
    queries = (projected[:, 0] + adapter_delta[:, 0]).astype(jnp.bfloat16)
    keys_new = projected[:, 1].astype(jnp.bfloat16)
    values_new = (projected[:, 2] + adapter_delta[:, 1]).astype(jnp.bfloat16)
    prompt_q = queries[:prompt_rows].reshape(slot_count, slot_len, head_count, HEAD_DIM)
    prompt_k = keys_new[:prompt_rows].reshape(slot_count, slot_len, head_count, HEAD_DIM)
    prompt_v = values_new[:prompt_rows].reshape(slot_count, slot_len, head_count, HEAD_DIM)
    scores = (
        jnp.einsum("sihd,sjhd->shij", prompt_q, prompt_k, preferred_element_type=jnp.float32)
        * score_scale
    )
    causal = jnp.arange(slot_len)[None, :] <= jnp.arange(slot_len)[:, None]
    scores = jnp.where(causal[None, None], scores, -1e30)
    highest = jnp.max(scores, axis=3, keepdims=True)
    weights = jnp.where(causal[None, None], jnp.exp(scores - highest), 0.0)
    weights = (weights / jnp.sum(weights, axis=3, keepdims=True)).astype(jnp.bfloat16)
    prompt_out = jnp.einsum(
        "shij,sjhd->sihd", weights, prompt_v, preferred_element_type=jnp.float32
    )
    active = jnp.arange(slot_len)[None, :] < prompt_length_list[:, None]
    prompt_out = (
        jnp.where(active[:, :, None, None], prompt_out, 0.0)
        .astype(jnp.bfloat16)
        .reshape(prompt_rows, -1)
    )
    cache_len = cache.shape[1]
    decode_q = queries[prompt_rows:].reshape(decode_count, head_count, HEAD_DIM)
    decode_k = keys_new[prompt_rows:].reshape(decode_count, head_count, HEAD_DIM)
    decode_v = values_new[prompt_rows:].reshape(decode_count, head_count, HEAD_DIM)
    keys_old = cache[:, :, 0].reshape(decode_count, cache_len, head_count, HEAD_DIM)
    values_old = cache[:, :, 1].reshape(decode_count, cache_len, head_count, HEAD_DIM)
    cache_scores = (
        jnp.einsum("dhe,dthe->dht", decode_q, keys_old, preferred_element_type=jnp.float32)
        * score_scale
    )
    live_cache = jnp.arange(cache_len)[None, None, :] < cache_length_list[:, None, None]
    cache_scores = jnp.where(live_cache, cache_scores, -1e30)
    self_score = (
        jnp.einsum("dhe,dhe->dh", decode_q, decode_k, preferred_element_type=jnp.float32)
        * score_scale
    )
    row_top = jnp.maximum(jnp.max(cache_scores, axis=2), self_score)
    cache_weights = jnp.where(live_cache, jnp.exp(cache_scores - row_top[:, :, None]), 0.0)
    self_weight = jnp.exp(self_score - row_top)
    totals = jnp.sum(cache_weights, axis=2) + self_weight
    cache_weights = (cache_weights / totals[:, :, None]).astype(jnp.bfloat16)
    self_weight = (self_weight / totals).astype(jnp.bfloat16)
    decode_out = jnp.einsum(
        "dht,dthe->dhe", cache_weights, values_old, preferred_element_type=jnp.float32
    )
    decode_out = decode_out + self_weight.astype(jnp.float32)[:, :, None] * decode_v.astype(
        jnp.float32
    )
    decode_out = decode_out.astype(jnp.bfloat16).reshape(decode_count, -1)
    attended = jnp.concatenate([prompt_out, decode_out], axis=0)
    mixed = jnp.dot(
        attended,
        lax.all_gather(output_weight, "req", axis=1, tiled=True),
        preferred_element_type=jnp.float32,
    )
    summed = lax.psum_scatter(
        mixed.astype(jnp.bfloat16), "mp", scatter_dimension=1, tiled=True
    ).astype(jnp.float32)
    return (tokens.astype(jnp.float32) + summed + output_bias[None]).astype(jnp.bfloat16)


def solution(mesh):
    placed = (
        P("req", "mp"),
        P(),
        P(),
        P(None, "req", "mp"),
        P(None, "mp"),
        P("req", "mp", None),
        P("req", None, None, "mp"),
        P("req", None),
        P("req"),
        P("req", None, None, "mp"),
        P("req"),
        P("mp", "req"),
        P("mp"),
    )
    quick = mesh.shape["req"] == 2 * NZ and mesh.shape["mp"] == NM
    return jax.shard_map(
        packed_device if quick else on_device, mesh=mesh, in_specs=placed, out_specs=P("req", "mp"), check_vma=False
    )
```

```python
import functools

import jax
import jax.numpy as jnp
from jax import lax
from jax.experimental import pallas as pl
from jax.experimental.pallas import tpu as pltpu
from jax.sharding import PartitionSpec as P

HEAD_DIM = 128
ADAPTER_RANK = 16
BF = jnp.bfloat16
F32 = jnp.float32
MIB = 1 << 20

NZ, NM = 4, 4
SLOTS, PLEN, DEC = 3, 32, 2
QROWS = 24
STAT_ROW = 26
BLK = 32
CHUNK = 128
DCH = 16
PACKED = NM * CHUNK + 2 * NZ * DEC
LANES = 128
DECODE_ROWS = 16
SMALL = pl.CostEstimate(flops=1, bytes_accessed=1, transcendentals=0)
VMEM = pl.BlockSpec(memory_space=pltpu.VMEM)
SMEM = pl.BlockSpec(memory_space=pltpu.SMEM)
ANY = pl.BlockSpec(memory_space=pl.ANY)


def swap_req(x, bits):
    return lax.ppermute(x, "req", [(i, i ^ bits) for i in range(2 * NZ)])


def swap_mp(x, bits):
    return lax.ppermute(x, "mp", [(i, i ^ bits) for i in range(NM)])


def gather_z(x):
    far, near = swap_req(x, 4), swap_req(x, 2)
    return [x, near, far, swap_req(far, 2)]


def limit(mib):
    return pltpu.CompilerParams(vmem_limit_bytes=mib * MIB)


def iota(shape, axis):
    return lax.broadcasted_iota(jnp.int32, shape, axis)


def three(x):
    a = x.astype(BF)
    rest = x - a.astype(F32)
    b = rest.astype(BF)
    return [a.astype(F32), b.astype(F32), (rest - b.astype(F32)).astype(BF).astype(F32)]


class Source:
    def __init__(self, s_ref, t_ref, j):
        z, core = s_ref[3], s_ref[6]
        self.z = jnp.bitwise_xor(z, j % NZ)
        self.core = jnp.bitwise_xor(core, j // NZ)
        self.index = self.z * 2 + self.core
        self.lens = [t_ref[j, i] for i in range(SLOTS)]
        self.adapters = [t_ref[j, SLOTS + i] for i in range(SLOTS + DEC)]
        self.live = self.lens[0] + self.lens[1] + self.lens[2]
        self.size = (self.live + 3) >> 2


def sources(s_ref, t_ref):
    found = [Source(s_ref, t_ref, j) for j in range(2 * NZ)]
    for a in found:
        a.offset = sum(jnp.where(b.index < a.index, b.size, 0) for b in found)
    return found


def by_slot(h, values):
    out = jnp.full_like(h, -1)
    for j in range(SLOTS):
        out = jnp.where((h >> 5) == j, values[j], out)
    return out


def chunk_places(found, other, t, seg, m):
    out = jnp.full_like(t, -1)
    for k in range(NZ):
        a = found[other * NZ + k]
        have = jnp.clip(a.live - m * a.size, 0, a.size)
        prompt = jnp.where(t < have, a.offset + t, -1)
        decode = jnp.where((t < QROWS + DEC) & (a.z == m), CHUNK + a.core * DEC + t - QROWS, -1)
        out = jnp.where(seg == k, jnp.where(t < QROWS, prompt, decode), out)
    return out


def packed_places(a, j, h, m, core):
    i = h & (PLEN - 1)
    starts = [0, a.lens[0], a.lens[0] + a.lens[1]]
    index = by_slot(h, starts) + i
    quarter = sum((index >= q * a.size).astype(jnp.int32) for q in range(1, NM))
    spot = jnp.bitwise_xor(quarter, m) * CHUNK + a.offset + index - quarter * a.size
    half = 2 * CHUNK
    spot = jnp.bitwise_xor(spot >> 8, core) * half + (spot & (half - 1))
    prompt = jnp.where(i < by_slot(h, a.lens), spot, -1)
    first = SLOTS * PLEN
    base = NM * CHUNK + (j // NZ * NZ + turned_bits(j % NZ)) * DEC - first
    decode = jnp.where(h < first + DEC, base + h, -1)
    return jnp.where(h < first, prompt, decode)


def home_adapters(a, h):
    out = by_slot(h, a.adapters)
    for j in range(DEC):
        out = jnp.where(h == SLOTS * PLEN + j, a.adapters[SLOTS + j], out)
    return out


def deal_kernel(s_ref, x_ref, *outs):
    len0, len1, len2, z, m = [s_ref[i] for i in range(5)]
    size = (len0 + len1 + len2 + 3) >> 2
    rows, cols = x_ref.shape
    prompt_rows = SLOTS * PLEN
    t, h = iota((BLK, rows), 0), iota((BLK, rows), 1)
    slot, i = h >> 5, h & (PLEN - 1)
    start = jnp.where(slot == 0, 0, jnp.where(slot == 1, len0, len0 + len1))
    length = jnp.where(slot == 0, len0, jnp.where(slot == 1, len1, len2))
    live = (i < length) & (h < prompt_rows) & (t < size)
    x = x_ref[...]
    wide = x.astype(F32)
    mean = jnp.sum(wide, axis=1, keepdims=True) / cols
    spread = jnp.sum((wide - mean) ** 2, axis=1, keepdims=True)
    lane = iota((rows, LANES), 1)
    stats = jnp.zeros((rows, LANES), F32)
    for j, term in enumerate(three(mean) + three(spread)):
        stats = jnp.where(lane == 2 + j, term, stats)
    same = (iota((rows, LANES), 0) == lane).astype(BF)
    turned = lax.dot_general(stats.astype(BF), same, (((0,), (0,)), ((), ())), preferred_element_type=F32)
    turned = jnp.concatenate([jnp.zeros((8, LANES), F32), turned[:8]], axis=0)
    for k, out in enumerate(outs):
        q = jnp.bitwise_xor(m, k)
        mine = live & (start + i - q * size == t)
        decode = (h >= prompt_rows) & (t == QROWS + h - prompt_rows) & (q == z)
        y = jnp.dot((mine | decode).astype(BF), x, preferred_element_type=F32)
        out[...] = y.astype(BF)
        out[16:32, :LANES] = (y[16:32, :LANES] + turned).astype(BF)


def deal(scalars, tokens):
    return pl.pallas_call(
        deal_kernel,
        out_shape=[jax.ShapeDtypeStruct((BLK, tokens.shape[1]), BF)] * NM,
        in_specs=[SMEM, VMEM],
        out_specs=[VMEM] * NM,
        compiler_params=limit(16),
        cost_estimate=SMALL,
        name="deal_rows",
    )(scalars, tokens)


def norm_kernel(s_ref, b0, b1, b2, b3, affine_ref, table_ref, _, __, o0, o1, o2, o3, held):
    z, m = s_ref[3], s_ref[4]
    cols = b0.shape[1]
    for k, ref in enumerate((b0, b1, b2, b3)):
        held[k] = ref[...].astype(F32)
    width = NM * cols
    means, spreads = [], []
    for k in range(NM):
        part = held[k, 24:32, :LANES]
        means.append(part[2:3] + part[3:4] + part[4:5])
        spreads.append(part[5:6] + part[6:7] + part[7:8])
    mean = sum(means) / NM
    var = (sum(spreads) + cols * sum((v - mean) ** 2 for v in means)) / width
    row = iota((BLK, LANES), 0)
    extra = []
    for value in (mean, lax.rsqrt(var + 1e-05)):
        block = jnp.zeros((BLK, LANES), F32)
        for j, term in enumerate(three(value)):
            block = jnp.where(row == STAT_ROW + j, term, block)
        extra.append(block)
    extra = jnp.concatenate(extra, axis=1)
    extra = jnp.where(iota(extra.shape, 0) == BLK - 1, table_ref[:, : 2 * LANES], extra)
    mean = sum(jnp.sum(held[k], axis=1, keepdims=True) for k in range(NM)) / width
    var = sum(jnp.sum((held[k] - mean) ** 2, axis=1, keepdims=True) for k in range(NM)) / width
    rstd = lax.rsqrt(var + 1e-05)
    last = iota((BLK, cols), 0) == BLK - 1
    stats = iota((BLK, 2 * LANES), 0) >= STAT_ROW
    for k, out in enumerate((o0, o1, o2, o3)):
        block = jnp.bitwise_xor(z, k)
        x = held[jnp.bitwise_xor(block, m)]
        y = (x - mean) * rstd * affine_ref[block] + affine_ref[NM + block]
        y = jnp.where(last, table_ref[...], y)
        out[...] = y.astype(BF)
        out[:, : 2 * LANES] = jnp.where(stats, extra, y[:, : 2 * LANES]).astype(BF)


def norm_rows(scalars, blocks, affine, table, near, far):
    return pl.pallas_call(
        norm_kernel,
        out_shape=[jax.ShapeDtypeStruct(blocks[0].shape, BF)] * NZ,
        in_specs=[SMEM] + [VMEM] * 6 + [ANY] * 2,
        out_specs=[VMEM] * NZ,
        scratch_shapes=[pltpu.VMEM((NM,) + blocks[0].shape, F32)],
        compiler_params=limit(16),
        cost_estimate=SMALL,
        name="norm_rows",
    )(scalars, *blocks, affine, table, near, far)


def cores_kernel(s_ref, b0, b1, b2, b3, mine_ref, theirs_ref):
    core = s_ref[6]
    width = mine_ref.shape[1]
    for k, ref in enumerate((b0, b1, b2, b3)):
        rows = slice(k * BLK, (k + 1) * BLK)
        mine_ref[rows, :] = ref[:, pl.ds(pl.multiple_of(core * width, LANES), width)]
        theirs_ref[rows, :] = ref[:, pl.ds(pl.multiple_of((1 - core) * width, LANES), width)]


def split_cores(scalars, blocks):
    out = jax.ShapeDtypeStruct((NZ * BLK, blocks[0].shape[1] // 2), BF)
    return pl.pallas_call(
        cores_kernel,
        out_shape=[out, out],
        in_specs=[SMEM] + [VMEM] * NZ,
        out_specs=[VMEM] * 2,
        compiler_params=limit(16),
        cost_estimate=SMALL,
        name="split_cores",
    )(scalars, *blocks)


def pack_kernel(s_ref, t_ref, a_ref, b_ref, o_ref):
    found = sources(s_ref, t_ref)
    half = a_ref.shape[0]
    lane = iota((1, half), 1)
    total = None
    for other, ref in enumerate((a_ref, b_ref)):
        to = chunk_places(found, other, lane & (BLK - 1), lane // BLK, s_ref[4])
        pick = (iota((o_ref.shape[0], half), 0) == to).astype(BF)
        term = jnp.dot(pick, ref[...], preferred_element_type=F32)
        total = term if total is None else total + term
    o_ref[...] = total.astype(BF)


def pack_rows(scalars, tables, mine, theirs):
    return pl.pallas_call(
        pack_kernel,
        out_shape=jax.ShapeDtypeStruct((CHUNK + DCH, mine.shape[1]), BF),
        in_specs=[SMEM] * 2 + [VMEM] * 2,
        out_specs=VMEM,
        compiler_params=limit(16),
        cost_estimate=SMALL,
        name="pack_rows",
    )(scalars, tables, mine, theirs)


def copy_kernel(x_ref, _, o_ref):
    o_ref[...] = x_ref[...]


def copy_rows(x, after):
    return pl.pallas_call(
        copy_kernel,
        out_shape=jax.ShapeDtypeStruct(x.shape, x.dtype),
        in_specs=[VMEM, ANY],
        out_specs=VMEM,
        compiler_params=limit(16),
        cost_estimate=SMALL,
        name="copy_rows",
    )(x, after)


def code_kernel(s_ref, t_ref, _, col_ref, row_ref):
    found = sources(s_ref, t_ref)
    m, core = s_ref[4], s_ref[6]
    n = NM * CHUNK
    lane, sub = iota((1, LANES), 1), iota((LANES, 1), 0)
    down, across = iota((n, LANES), 0), iota((LANES, n), 1)
    cols, rows = jnp.zeros((n, 1), jnp.int32), jnp.zeros((1, n), jnp.int32)
    for j, a in enumerate(found):
        first = a.index * SLOTS * PLEN + 1
        hit = down == packed_places(a, j, lane, m, core)
        cols = cols + jnp.sum(jnp.where(hit, first + lane, 0), axis=1, keepdims=True)
        hit = across == packed_places(a, j, sub, m, core)
        rows = rows + jnp.sum(jnp.where(hit, first + sub, 0), axis=0, keepdims=True)
    unused = (1 << 16) + PLEN * iota((n, 1), 0)
    col_ref[...] = jnp.where(cols > 0, cols - 1, unused)
    unused = (1 << 16) + PLEN * iota((1, n), 1)
    row_ref[...] = jnp.where(rows > 0, rows - 1, unused)


def packed_codes(scalars, tables, after):
    n = NM * CHUNK
    return pl.pallas_call(
        code_kernel,
        out_shape=[jax.ShapeDtypeStruct((n, 1), jnp.int32), jax.ShapeDtypeStruct((1, n), jnp.int32)],
        in_specs=[SMEM] * 2 + [ANY],
        out_specs=[VMEM] * 2,
        compiler_params=limit(16),
        cost_estimate=SMALL,
        name="packed_codes",
    )(scalars, tables, after)


def rank_kernel(s_ref, table_ref, da_ref, db_ref, x0, x1, x2, x3, t0, t1, t2, t3, affine_ref, o_ref):
    m, r = s_ref[4], s_ref[5]
    width = 2 * ADAPTER_RANK
    count = da_ref.shape[0] // width
    rows = x0.shape[0]
    same = (iota((rows, LANES), 0) == iota((rows, LANES), 1)).astype(BF)
    o_ref[...] = jnp.zeros_like(o_ref)
    for k, (x, stats) in enumerate(zip((x0, x1, x2, x3), (t0, t1, t2, t3))):

        def column(at):
            turned = lax.dot_general(
                same, stats[16:32, at], (((1,), (1,)), ((), ())), preferred_element_type=F32
            )
            j = STAT_ROW - 16
            return turned[:, j : j + 1] + turned[:, j + 1 : j + 2] + turned[:, j + 2 : j + 3]

        mean, rstd = column(slice(0, LANES)), column(slice(LANES, 2 * LANES))
        normed = ((x[...].astype(F32) - mean) * rstd * affine_ref[m] + affine_ref[NM + m]).astype(BF)
        ids = home_adapters(Source(s_ref, table_ref, k), iota((1, rows), 1))
        total = jnp.zeros((width, rows), F32)
        for core, d in enumerate((da_ref, db_ref)):
            y = lax.dot_general(d[...], normed, (((1,), (1,)), ((), ())), preferred_element_type=F32)
            first = jnp.bitwise_xor(r, core) * count
            for a in range(count):
                total = total + jnp.where(ids == first + a, y[a * width : (a + 1) * width], 0.0)
        o_ref[:, k * LANES : k * LANES + rows] = total


def low_rank_rows(scalars, tables, down, down_other, pieces, stats, affine):
    return pl.pallas_call(
        rank_kernel,
        out_shape=jax.ShapeDtypeStruct((2 * ADAPTER_RANK, NZ * LANES), F32),
        in_specs=[SMEM] * 2 + [VMEM] * 11,
        out_specs=VMEM,
        compiler_params=limit(16),
        cost_estimate=SMALL,
        name="low_rank_rows",
    )(scalars, tables, down, down_other, *pieces, *stats, affine)


def expand_kernel(s_ref, t_ref, low_ref, low_other_ref, base_ref, key_ref, up_ref, _, o_ref, keep_ref, send_ref, *, count):
    m, r, core = s_ref[4], s_ref[5], s_ref[6]
    found = sources(s_ref, t_ref)
    width = count * ADAPTER_RANK
    repeat = []
    for t in range(2):
        shape = (width, 2 * ADAPTER_RANK)
        repeat.append((iota(shape, 1) == t * ADAPTER_RANK + iota(shape, 0) % ADAPTER_RANK).astype(BF))
    repeat = jnp.concatenate(repeat, axis=0)
    adapter = r * count + (iota((2 * width, LANES), 0) % width) // ADAPTER_RANK
    lane = iota((1, LANES), 1)
    total = jnp.zeros((PACKED, 2 * width), F32)
    for j, a in enumerate(found):
        ref = low_other_ref if j >= NZ else low_ref
        k = j % NZ
        low = jnp.dot(repeat, ref[:, k * LANES : (k + 1) * LANES], preferred_element_type=F32)
        low = jnp.where(adapter == home_adapters(a, lane), low, 0.0).astype(BF)
        hit = (iota((PACKED, LANES), 0) == packed_places(a, j, lane, m, core)).astype(BF)
        total = total + lax.dot_general(hit, low, (((1,), (1,)), ((), ())), preferred_element_type=F32)
    feats = up_ref.shape[3]
    half = keep_ref.shape[0]
    keep_ref[:, feats : 2 * feats] = key_ref[:half, :]
    send_ref[:, feats : 2 * feats] = key_ref[half:, :]
    for t, first in ((0, 0), (1, 2 * feats)):
        rows = total[:, t * width : (t + 1) * width].astype(BF)
        o_ref[t] = rows
        up = up_ref[:, t].reshape(-1, feats)
        term = jnp.dot(rows[NM * CHUNK :, :], up, preferred_element_type=F32)
        term = term + base_ref[:, t * feats : (t + 1) * feats]
        keep_ref[:, first : first + feats] = term[:half]
        send_ref[:, first : first + feats] = term[half:]


def expand_rows(scalars, tables, low, low_other, base, keys, up, count, after):
    half = jax.ShapeDtypeStruct((keys.shape[0] // 2, 3 * keys.shape[1]), F32)
    return pl.pallas_call(
        functools.partial(expand_kernel, count=count),
        out_shape=[jax.ShapeDtypeStruct((2, PACKED, count * ADAPTER_RANK), BF), half, half],
        in_specs=[SMEM] * 2 + [VMEM] * 5 + [ANY],
        out_specs=[VMEM] * 3,
        compiler_params=limit(16),
        cost_estimate=SMALL,
        name="expand_rows",
    )(scalars, tables, low, low_other, base, keys, up, after)


def emit_sums(y, own_ref, other_ref):
    half = 2 * CHUNK
    own_ref[...] = y[:half].astype(BF)
    other_ref[...] = y[half : 2 * half].astype(BF)


def first_project_kernel(s_ref, c0, c1, c2, c3, w_ref, _, own_ref, other_ref, dec_ref, x):
    z, m, core = s_ref[3], s_ref[4], s_ref[6]

    @pl.when(pl.program_id(0) == 0)
    def _():
        chunks = (c0, c1, c2, c3)
        for k, chunk in enumerate(chunks):
            base = jnp.bitwise_xor(core, k >> 1) * 2 * CHUNK + (k & 1) * CHUNK
            x[pl.ds(pl.multiple_of(base, CHUNK), CHUNK), :] = chunk[:CHUNK, :]
        n, at = iota((2 * NZ * DEC, NM * DCH), 0), iota((2 * NZ * DEC, NM * DCH), 1)
        chip = jnp.bitwise_xor(z, turned_bits((n >> 1) & 3))
        want = jnp.bitwise_xor(chip, m) * DCH + jnp.bitwise_xor(core, n >> 3) * DEC + (n & 1)
        rows = jnp.concatenate([chunk[CHUNK:, :] for chunk in chunks], axis=0)
        x[NM * CHUNK :, :] = jnp.dot((want == at).astype(BF), rows, preferred_element_type=F32).astype(BF)

    y = jnp.dot(x[...], w_ref[0], preferred_element_type=F32)
    emit_sums(y, own_ref, other_ref)
    dec_ref[...] = y[NM * CHUNK :]


def project_rows(scalars, chunks, weight, part, after):
    _, depth, feats = weight.shape
    tile = feats // 2
    half = 2 * CHUNK
    whole = [pl.BlockSpec(v.shape, lambda j: (0, 0)) for v in chunks]
    out_shape = [
        jax.ShapeDtypeStruct((half, feats), BF),
        jax.ShapeDtypeStruct((half, feats), BF),
        jax.ShapeDtypeStruct((PACKED - NM * CHUNK, feats), F32),
        jax.ShapeDtypeStruct((PACKED, depth), BF),
    ]
    out_specs = [pl.BlockSpec((v.shape[0], tile), lambda j: (0, j)) for v in out_shape[:3]]
    out_specs.append(pl.BlockSpec((PACKED, depth), lambda j: (0, 0)))
    return pl.pallas_call(
        first_project_kernel,
        grid=(feats // tile,),
        out_shape=out_shape,
        in_specs=[SMEM] + whole + [pl.BlockSpec((1, depth, tile), lambda j: (part, 0, j)), ANY],
        out_specs=out_specs,
        compiler_params=limit(16),
        cost_estimate=SMALL,
        name="project_keys",
    )(scalars, *chunks, weight, after)


def adapted_kernel(x_ref, w_ref, e_ref, u_ref, _, *outs):
    y = jnp.dot(x_ref[: NM * CHUNK, :], w_ref[0], preferred_element_type=F32)
    up = u_ref[...].reshape(-1, u_ref.shape[-1])
    y = y + jnp.dot(e_ref[0, : NM * CHUNK, :], up, preferred_element_type=F32)
    emit_sums(y, *outs)


def project_adapted(rows, weight, part, expanded, up, after):
    _, depth, feats = weight.shape
    tile = feats // 2
    half = 2 * CHUNK
    which = part // 2
    out_shape = [
        jax.ShapeDtypeStruct((half, feats), BF),
        jax.ShapeDtypeStruct((half, feats), BF),
    ]
    return pl.pallas_call(
        adapted_kernel,
        grid=(2,),
        out_shape=out_shape,
        in_specs=[
            pl.BlockSpec(rows.shape, lambda j: (0, 0)),
            pl.BlockSpec((1, depth, tile), lambda j: (part, 0, j)),
            pl.BlockSpec((1,) + expanded.shape[1:], lambda j: (which, 0, 0)),
            pl.BlockSpec((up.shape[0], 1, up.shape[2], tile), lambda j: (0, which, 0, j)),
            ANY,
        ],
        out_specs=[pl.BlockSpec((v.shape[0], tile), lambda j: (0, j)) for v in out_shape],
        compiler_params=limit(16),
        cost_estimate=SMALL,
        name="project_adapted",
    )(rows, weight, expanded, up, after)


def add_kernel(a_ref, b_ref, _, o_ref):
    o_ref[...] = (a_ref[: b_ref.shape[0], :] + b_ref[...]).astype(o_ref.dtype)


def add_rows(a, b, after, dtype=F32):
    return pl.pallas_call(
        add_kernel,
        out_shape=jax.ShapeDtypeStruct(b.shape, dtype),
        in_specs=[VMEM] * 2 + [ANY],
        out_specs=VMEM,
        compiler_params=limit(16),
        cost_estimate=SMALL,
        name="add_rows",
    )(a, b, after)


def decode_finish_kernel(a_ref, b_ref, bias_ref, _, q_ref, k_ref, v_ref):
    total = a_ref[: b_ref.shape[0], :] + b_ref[...]
    feats = bias_ref.shape[1]
    for j, out in enumerate((q_ref, k_ref, v_ref)):
        part = total[:, j * feats : (j + 1) * feats] + bias_ref[j : j + 1, :]
        for i in range(out.shape[0]):
            out[i] = part[i : i + 1].astype(BF)


def decode_finish(a, b, bias, after):
    out = jax.ShapeDtypeStruct((b.shape[0], 1, bias.shape[1]), BF)
    return pl.pallas_call(
        decode_finish_kernel,
        out_shape=[out] * 3,
        in_specs=[VMEM] * 3 + [ANY],
        out_specs=[VMEM] * 3,
        compiler_params=limit(16),
        cost_estimate=SMALL,
        name="decode_finish",
    )(a, b, bias, after)


def decode_base_kernel(x_ref, w_ref, _, o_ref):
    o_ref[...] = jnp.dot(x_ref[...], w_ref[0], preferred_element_type=F32)


def decode_base(rows, weight, after):
    _, depth, feats = weight.shape
    count = PACKED - NM * CHUNK
    return pl.pallas_call(
        decode_base_kernel,
        grid=(2,),
        out_shape=jax.ShapeDtypeStruct((count, 2 * feats), F32),
        in_specs=[
            pl.BlockSpec((count, depth), lambda p: (NM * CHUNK // count, 0)),
            pl.BlockSpec((1, depth, feats), lambda p: (2 * p, 0, 0)),
            ANY,
        ],
        out_specs=pl.BlockSpec((count, feats), lambda p: (0, p)),
        compiler_params=limit(16),
        cost_estimate=SMALL,
        name="decode_base",
    )(rows, weight, after)


def halve_kernel(s_ref, *refs, bit, groups):
    *ins, _, send_ref, keep_ref = refs
    count = len(ins) // 2
    side = (s_ref[3] >> bit) & 1
    to = 0
    for total_ref, got_ref in zip(ins[:count], ins[count:]):
        width = total_ref.shape[1] // groups // 2

        for g in range(groups):

            def part(which):
                at = pl.ds(pl.multiple_of((2 * g + which) * width, LANES), width)
                return total_ref[:, at].astype(F32) + got_ref[:, at].astype(F32)

            send_ref[:, to : to + width] = part(1 - side).astype(BF)
            keep_ref[:, to : to + width] = part(side)
            to += width


def halve(scalars, totals, gots, bit, after, groups=1):
    rows = totals[0].shape[0]
    feats = sum(v.shape[1] for v in totals) // 2
    return pl.pallas_call(
        functools.partial(halve_kernel, bit=bit, groups=groups),
        out_shape=[jax.ShapeDtypeStruct((rows, feats), BF), jax.ShapeDtypeStruct((rows, feats), F32)],
        in_specs=[SMEM] + [VMEM] * (2 * len(totals)) + [ANY],
        out_specs=[VMEM, VMEM],
        compiler_params=limit(16),
        cost_estimate=SMALL,
        name="halve_sums",
    )(scalars, *totals, *gots, after)


def finish_kernel(s_ref, total_ref, got_ref, bias_ref, _, *outs, parts):
    for j, (part, out) in enumerate(zip(parts, outs)):
        width = out.shape[1]
        at = pl.ds(pl.multiple_of(place_of(s_ref[3]) * width, LANES), width)
        mine = slice(j * width, (j + 1) * width)
        total = total_ref[:, mine] + got_ref[:, mine].astype(F32) + bias_ref[part : part + 1, at]
        out[...] = total.astype(BF)


def finish(scalars, total, got, bias, parts, after):
    rows, feats = total.shape
    return pl.pallas_call(
        functools.partial(finish_kernel, parts=parts),
        out_shape=[jax.ShapeDtypeStruct((rows, feats // len(parts)), BF)] * len(parts),
        in_specs=[SMEM, VMEM, VMEM, VMEM, ANY],
        out_specs=[VMEM] * len(parts),
        compiler_params=limit(16),
        cost_estimate=SMALL,
        name="finish_sums",
    )(scalars, total, got, bias, after)


def prompt_kernel(q_ref, ka_ref, kb_ref, va_ref, vb_ref, cr_ref, cc_ref, d_ref, o_ref):
    rows = cr_ref[...]
    cols = cc_ref[...]
    allowed = ((rows >> 5) == (cols >> 5)) & (cols <= rows)
    keys = jnp.concatenate([ka_ref[...], kb_ref[...]], axis=0)
    values = jnp.concatenate([va_ref[...], vb_ref[...]], axis=0)
    for h in range(q_ref.shape[1] // HEAD_DIM):
        at = slice(h * HEAD_DIM, (h + 1) * HEAD_DIM)
        s = lax.dot_general(q_ref[:, at], keys[:, at], (((1,), (1,)), ((), ())), preferred_element_type=F32)
        s = jnp.where(allowed, s * HEAD_DIM**-0.5, -1e30)
        top = jnp.max(s, axis=1, keepdims=True)
        w = jnp.where(allowed, jnp.exp(s - top), 0.0)
        w = (w / jnp.sum(w, axis=1, keepdims=True)).astype(BF)
        o_ref[: q_ref.shape[0], at] = jnp.dot(w, values[:, at], preferred_element_type=F32).astype(BF)
    width = q_ref.shape[1]
    n = iota((DECODE_ROWS, width), 0)
    tail = jnp.zeros((DECODE_ROWS, width), F32)
    for b in range(NZ):
        for j in range(DEC):
            tail = jnp.where(n == b * DEC + j, d_ref[j : j + 1, b * width : (b + 1) * width].astype(F32), tail)
    o_ref[q_ref.shape[0] :, :] = tail.astype(BF)


def prompt_attention(q, ka, kb, va, vb, code_rows, code_cols, dec):
    return pl.pallas_call(
        prompt_kernel,
        out_shape=jax.ShapeDtypeStruct((q.shape[0] + DECODE_ROWS, q.shape[1]), BF),
        in_specs=[VMEM] * 8,
        out_specs=VMEM,
        compiler_params=limit(16),
        cost_estimate=SMALL,
        name="prompt_attention",
    )(q, ka, kb, va, vb, code_rows, code_cols, dec)


def decode_kernel(len_ref, q_ref, k_ref, v_ref, c_ref, _, o_ref, qbd, top, total, acc):
    d, t = pl.program_id(0), pl.program_id(1)
    span = c_ref.shape[1]
    live = len_ref[d]
    heads, feats = qbd.shape
    diag = lax.broadcasted_iota(jnp.int32, (heads, feats), 1) // HEAD_DIM == lax.broadcasted_iota(
        jnp.int32, (heads, feats), 0
    )

    @pl.when(t == 0)
    def _():
        q = jnp.where(diag, q_ref[0].astype(F32), 0.0)
        qbd[...] = q.astype(BF)
        own = jnp.sum(q * k_ref[0].astype(F32), axis=1, keepdims=True) * HEAD_DIM**-0.5
        top[...] = jnp.broadcast_to(own, top.shape)
        total[...] = jnp.ones_like(total)
        acc[...] = jnp.broadcast_to(v_ref[0].astype(F32), acc.shape)

    @pl.when(t * span < live)
    def _():
        x = c_ref[0].reshape(2 * span, feats)
        s = lax.dot_general(qbd[...], x, (((1,), (1,)), ((), ())), preferred_element_type=F32)
        column = lax.broadcasted_iota(jnp.int32, s.shape, 1)
        valid = (column % 2 == 0) & (t * span + column // 2 < live)
        s = jnp.where(valid, s * HEAD_DIM**-0.5, -1e30)
        before = top[:, :1]
        now = jnp.maximum(before, jnp.max(s, axis=1, keepdims=True))
        fade = jnp.exp(before - now)
        w = jnp.where(valid, jnp.exp(s - now), 0.0)
        total[...] = total[...] * fade + jnp.sum(w, axis=1, keepdims=True)
        top[...] = jnp.broadcast_to(now, top.shape)
        w = pltpu.roll(w, 1, 1).astype(BF)
        acc[...] = acc[...] * fade + jnp.dot(w, x, preferred_element_type=F32)

    @pl.when(t == pl.num_programs(1) - 1)
    def _():
        o = acc[...] / total[:, :1]
        o_ref[0] = jnp.sum(jnp.where(diag, o, 0.0), axis=0, keepdims=True).astype(BF)


def decode_attention(lengths, q, k, v, cache, after, span=256):
    count, positions, _, feats = cache.shape
    row = pl.BlockSpec((1, 1, feats), lambda d, t, n: (d, 0, 0))
    heads = 16
    return pl.pallas_call(
        decode_kernel,
        grid_spec=pltpu.PrefetchScalarGridSpec(
            num_scalar_prefetch=1,
            grid=(count, positions // span),
            in_specs=[row, row, row]
            + [pl.BlockSpec((1, span, 2, feats), lambda d, t, n: (d, jnp.minimum(t, (n[d] - 1) // span), 0, 0)), ANY],
            out_specs=row,
            scratch_shapes=[
                pltpu.VMEM((heads, feats), BF),
                pltpu.VMEM((heads, LANES), F32),
                pltpu.VMEM((heads, LANES), F32),
                pltpu.VMEM((heads, feats), F32),
            ],
        ),
        out_shape=jax.ShapeDtypeStruct((count, 1, feats), BF),
        compiler_params=limit(44),
        cost_estimate=SMALL,
        name="decode_attention",
    )(lengths, q, k, v, cache, after)


def out_term(z, k, own, other, w_ref):
    width = own.shape[1]
    half = own.shape[0] - DECODE_ROWS
    block = place_of(jnp.bitwise_xor(z, k))
    w = w_ref[pl.ds(pl.multiple_of(block * width, width), width), :]
    rows = jnp.concatenate([own[:half, :], other[:half, :]], axis=0)
    return jnp.dot(rows, w, preferred_element_type=F32)


def out_first_kernel(place_ref, *refs):
    own, other, w_ref, o_ref = refs[:3], refs[3:6], refs[6], refs[7]
    total = None
    for k in range(NZ - 1):
        term = out_term(place_ref[3], k, own[k], other[k], w_ref)
        total = term if total is None else total + term
    o_ref[...] = total


def out_first(scalars, own, other, weight):
    return pl.pallas_call(
        out_first_kernel,
        out_shape=jax.ShapeDtypeStruct((NM * CHUNK, weight.shape[1]), F32),
        in_specs=[SMEM] + [VMEM] * 7,
        out_specs=VMEM,
        compiler_params=limit(16),
        cost_estimate=SMALL,
        name="out_first",
    )(scalars, *own[:3], *other[:3], weight)


def out_kernel(place_ref, *refs):
    own, other, first_ref, w_ref, outs, mixed = refs[:4], refs[4:8], refs[8], refs[9], refs[10:14], refs[14]
    z, m, core = place_ref[3], place_ref[4], place_ref[6]
    width = own[0].shape[1]
    half = own[0].shape[0] - DECODE_ROWS
    mixed[...] = (first_ref[...] + out_term(z, NZ - 1, own[-1], other[-1], w_ref)).astype(BF)
    tails = jnp.concatenate([v[half:, :] for v in own + other], axis=0)
    count = 2 * NZ * DEC
    n, at = iota((count, tails.shape[0]), 0), iota((count, tails.shape[0]), 1)
    total = None
    for b in range(NZ):
        pick = (at == (n // DEC) * DECODE_ROWS + b * DEC + n % DEC).astype(BF)
        rows = jnp.dot(pick, tails, preferred_element_type=F32).astype(BF)
        term = jnp.dot(rows, w_ref[b * width : (b + 1) * width, :], preferred_element_type=F32)
        total = term if total is None else total + term
    decode = total.astype(BF)
    n, at = iota((DCH, count), 0), iota((DCH, count), 1)
    for k, out in enumerate(outs):
        base = jnp.bitwise_xor(core, k >> 1) * 2 * CHUNK + (k & 1) * CHUNK
        out[:CHUNK, :] = mixed[pl.ds(pl.multiple_of(base, CHUNK), CHUNK), :]
        far = jnp.bitwise_xor(jnp.bitwise_xor(m, k), z)
        want = (jnp.bitwise_xor(core, n >> 1) * NZ + far) * DEC + (n & 1)
        pick = ((at == want) & (n < 2 * DEC)).astype(BF)
        out[CHUNK:, :] = jnp.dot(pick, decode, preferred_element_type=F32).astype(BF)


def out_project(scalars, own, other, first, weight):
    feats = weight.shape[1]
    return pl.pallas_call(
        out_kernel,
        out_shape=[jax.ShapeDtypeStruct((CHUNK + DCH, feats), BF)] * NM,
        in_specs=[SMEM] + [VMEM] * 10,
        out_specs=[VMEM] * NM,
        scratch_shapes=[pltpu.VMEM((NM * CHUNK, feats), BF)],
        compiler_params=limit(16),
        cost_estimate=SMALL,
        name="out_project",
    )(scalars, *own, *other, first, weight)


def unpack_kernel(s_ref, t_ref, c0, c1, c2, c3, *outs):
    total = sum(c[...].astype(F32) for c in (c0, c1, c2, c3)).astype(BF)
    found = sources(s_ref, t_ref)
    n = iota((NZ * BLK, 1), 0)
    for other in range(2):
        to = chunk_places(found, other, n & (BLK - 1), n // BLK, s_ref[4])
        pick = (iota((NZ * BLK, total.shape[0]), 1) == to).astype(BF)
        rows = jnp.dot(pick, total, preferred_element_type=F32).astype(BF)
        for k, out in enumerate(outs):
            out[other * BLK : (other + 1) * BLK, :] = rows[k * BLK : (k + 1) * BLK]


def unpack_rows(scalars, tables, chunks):
    feats = chunks[0].shape[1]
    return pl.pallas_call(
        unpack_kernel,
        out_shape=[jax.ShapeDtypeStruct((2 * BLK, feats), BF)] * NZ,
        in_specs=[SMEM] * 2 + [VMEM] * 4,
        out_specs=[VMEM] * NZ,
        compiler_params=limit(16),
        cost_estimate=SMALL,
        name="unpack_rows",
    )(scalars, tables, *chunks)


def join_kernel(s_ref, a0, a1, a2, a3, other_ref, o0, o1, o2, o3, held):
    z, m, core = s_ref[3], s_ref[4], s_ref[6]
    width = a0.shape[1]
    mine = pl.ds(pl.multiple_of(core * width, LANES), width)
    theirs = pl.ds(pl.multiple_of((1 - core) * width, LANES), width)
    for k, ref in enumerate((a0, a1, a2, a3)):
        held[k, :, mine] = ref[:BLK, :]
        held[k, :, theirs] = other_ref[k * BLK : (k + 1) * BLK, :]
    for k, out in enumerate((o0, o1, o2, o3)):
        out[...] = held[jnp.bitwise_xor(jnp.bitwise_xor(z, m), k)]


def join_halves(scalars, parts, other):
    shape = (BLK, 2 * parts[0].shape[1])
    return pl.pallas_call(
        join_kernel,
        out_shape=[jax.ShapeDtypeStruct(shape, BF)] * NM,
        in_specs=[SMEM] + [VMEM] * 5,
        out_specs=[VMEM] * NM,
        scratch_shapes=[pltpu.VMEM((NZ,) + shape, BF)],
        compiler_params=limit(16),
        cost_estimate=SMALL,
        name="join_halves",
    )(scalars, *parts, other)


def home_kernel(s_ref, x_ref, bias_ref, b0, b1, b2, b3, o_ref):
    len0, len1, len2, z, m = [s_ref[i] for i in range(5)]
    size = (len0 + len1 + len2 + 3) >> 2
    rows = x_ref.shape[0]
    prompt_rows = SLOTS * PLEN
    t, h = iota((rows, BLK), 1), iota((rows, BLK), 0)
    slot, i = h >> 5, h & (PLEN - 1)
    start = jnp.where(slot == 0, 0, jnp.where(slot == 1, len0, len0 + len1))
    length = jnp.where(slot == 0, len0, jnp.where(slot == 1, len1, len2))
    live = (i < length) & (h < prompt_rows) & (t < size)
    total = x_ref[...].astype(F32) + bias_ref[...]
    for k, ref in enumerate((b0, b1, b2, b3)):
        q = jnp.bitwise_xor(m, k)
        mine = live & (start + i - q * size == t)
        decode = (h >= prompt_rows) & (t == QROWS + h - prompt_rows) & (q == z)
        total = total + jnp.dot((mine | decode).astype(BF), ref[...], preferred_element_type=F32)
    o_ref[...] = total.astype(BF)


def add_home(scalars, tokens, bias, blocks):
    return pl.pallas_call(
        home_kernel,
        out_shape=jax.ShapeDtypeStruct(tokens.shape, BF),
        in_specs=[SMEM] + [VMEM] * 6,
        out_specs=VMEM,
        compiler_params=limit(16),
        cost_estimate=SMALL,
        name="add_home",
    )(scalars, tokens, bias, *blocks)


def turned_bits(k):
    return (k & 1) * 2 + (k >> 1)


def place_of(z):
    return turned_bits(z)


def packed_device(
    tokens,
    layernorm_scale,
    layernorm_bias,
    query_key_value_weight,
    query_key_value_bias,
    adapter_down_weight,
    adapter_up_weight,
    adapter_index_table,
    prompt_length_list,
    cache,
    cache_length_list,
    output_weight,
    output_bias,
):
    i32 = jnp.int32
    r = lax.axis_index("req").astype(i32)
    m = lax.axis_index("mp").astype(i32)
    z, c = r >> 1, r & 1
    rows_dev, cols = tokens.shape
    prompt_rows = SLOTS * PLEN
    feats = query_key_value_weight.shape[2]
    depth = query_key_value_weight.shape[1]
    per_z = feats // NZ
    own_adapters = adapter_down_weight.shape[0]
    half = 2 * CHUNK
    order = jnp.arange(2 * NZ, dtype=i32)
    source = ((z ^ (order & 3)) << 1) + (c ^ (order >> 2))
    lens = prompt_length_list
    scalars = jnp.concatenate([lens, jnp.stack([z, m, r, c])])

    down = jnp.transpose(adapter_down_weight, (0, 2, 1)).reshape(own_adapters * 2 * ADAPTER_RANK, cols)

    with jax.named_scope("deal"):
        dealt = deal(scalars, tokens)
    with jax.named_scope("gather_home"):
        pieces = gather_z(tokens)
    with jax.named_scope("deal"):
        blocks = [dealt[0]] + [swap_mp(dealt[k], k) for k in range(1, NM)]
    with jax.named_scope("norm_rows"):
        table = jnp.concatenate([lens, adapter_index_table[0]]).astype(F32)
        table = jnp.pad(table, (0, depth - table.shape[0]))
        table = jnp.tile(table, 2)[None, :]
        affine = jnp.stack([layernorm_scale, layernorm_bias]).reshape(2 * NM, 1, cols)
        normed = norm_rows(scalars, blocks, affine, table, pieces[1], pieces[2])
    with jax.named_scope("spread_z"):
        spread = [normed[0]] + [swap_req(normed[k], 2 * k) for k in range(1, NZ)]
        mine, theirs = split_cores(scalars, spread)
        theirs = swap_req(theirs, 1)

    with jax.named_scope("tables"):
        tables = jnp.concatenate(
            [v.reshape(NZ, BLK, depth)[:, BLK - 1, : SLOTS + SLOTS + DEC] for v in (mine, theirs)], axis=0
        ).astype(i32)
    with jax.named_scope("pack"):
        chunk = pack_rows(scalars, tables, mine, theirs)
    with jax.named_scope("gather_chunks"):
        chunks = [chunk] + [swap_mp(chunk, k) for k in range(1, NM)]

    with jax.named_scope("low_rank"):
        down_other = swap_req(copy_rows(down, mine), 1)
        part = low_rank_rows(scalars, tables, down, down_other, pieces, spread, affine)
        two = add_rows(part, swap_mp(part, 1), part)
    with jax.named_scope("keys"):
        own_k, other_k, dec_k, x_rows = project_rows(scalars, chunks, query_key_value_weight, 1, two)
        core_k = swap_req(other_k, 1)
    with jax.named_scope("decode_rows"):
        base = decode_base(x_rows, query_key_value_weight, other_k)
    with jax.named_scope("low_rank"):
        low_rank = add_rows(two, swap_mp(two, 2), base, BF)
    with jax.named_scope("keys"):
        send_k, keep_k = halve(scalars, [own_k], [core_k], 0, low_rank)
        got_k = swap_req(send_k, 2)
    with jax.named_scope("low_rank"):
        expanded, dec, dec_sent = expand_rows(
            scalars, tables, low_rank, swap_req(low_rank, 1), base, dec_k, adapter_up_weight, own_adapters, send_k
        )
    with jax.named_scope("decode_rows"):
        dec_chip = add_rows(dec, swap_req(dec_sent, 1), expanded)
    with jax.named_scope("values"):
        own_v, other_v = project_adapted(x_rows, query_key_value_weight, 2, expanded, adapter_up_weight, dec_chip)
        core_v = swap_req(other_v, 1)
    with jax.named_scope("decode_rows"):
        dec_pair = add_rows(dec_chip, swap_req(dec_chip[4:], 2), own_v)
    with jax.named_scope("keys"):
        send_k, keep_k = halve(scalars, [keep_k], [got_k], 1, dec_pair)
        got_k = swap_req(send_k, 4)
    with jax.named_scope("decode_rows"):
        dec = decode_finish(dec_pair, swap_req(dec_pair[2:], 4), query_key_value_bias, send_k)
    with jax.named_scope("queries"):
        own_q, other_q = project_adapted(x_rows, query_key_value_weight, 0, expanded, adapter_up_weight, dec[0])
        core_q = swap_req(other_q, 1)
    with jax.named_scope("reduce_z"):
        send, keep = halve(scalars, [own_v, own_q], [core_v, core_q], 0, core_q)
        got = swap_req(send, 2)
    with jax.named_scope("codes"):
        code_col, code_row = packed_codes(scalars, tables, send)
    with jax.named_scope("keys"):
        (keys,) = finish(scalars, keep_k, got_k, query_key_value_bias, (1,), code_row)
        keys_other = swap_req(keys, 1)
    with jax.named_scope("reduce_z"):
        send, keep = halve(scalars, [keep], [got], 1, keys, groups=2)
        got = swap_req(send, 4)
    with jax.named_scope("decode_attention"):
        dec_out = decode_attention(cache_length_list, *dec, cache, send)
        dec_out = dec_out.reshape(DEC, feats)
    with jax.named_scope("reduce_z"):
        values, queries = finish(scalars, keep, got, query_key_value_bias, (2, 0), dec_out)
        values_other = swap_req(values, 1)
    with jax.named_scope("prompt_attention"):
        attended = prompt_attention(
            queries,
            keys,
            keys_other,
            values,
            values_other,
            code_col[: 2 * CHUNK],
            code_row,
            dec_out,
        )
    with jax.named_scope("gather_attended"):
        own = gather_z(attended)
        other = [swap_req(v, 1) for v in own]
    with jax.named_scope("out_project"):
        first = out_first(scalars, own, other, output_weight)
        mixed = out_project(scalars, own, other, first, output_weight)
    with jax.named_scope("sum_mp"):
        shares = [mixed[0]] + [swap_mp(mixed[k], k) for k in range(1, NM)]
    with jax.named_scope("return_z"):
        back = unpack_rows(scalars, tables, shares)
        back = [back[0]] + [swap_req(back[k], 2 * k) for k in range(1, NZ)]
        back_other = swap_req(jnp.concatenate([v[BLK:] for v in back], axis=0), 1)
    with jax.named_scope("return_plane"):
        joined = join_halves(scalars, back, back_other)
        joined = [joined[0]] + [swap_mp(joined[k], k) for k in range(1, NM)]
        return add_home(scalars, tokens, output_bias[None], joined)


def layer_norm(row_data, gain_vec, shift_vec):
    values = row_data.astype(jnp.float32)
    average = jnp.mean(values, axis=-1, keepdims=True)
    centred = values - average
    variance = jnp.mean(centred * centred, axis=-1, keepdims=True)
    scaled = centred * lax.rsqrt(variance + 1e-05)
    return (scaled * gain_vec + shift_vec).astype(jnp.bfloat16)


def on_device(
    tokens,
    layernorm_scale,
    layernorm_bias,
    query_key_value_weight,
    query_key_value_bias,
    adapter_down_weight,
    adapter_up_weight,
    adapter_index_table,
    prompt_length_list,
    cache,
    cache_length_list,
    output_weight,
    output_bias,
):
    rows_dev = tokens.shape[0]
    part_cols = tokens.shape[1]
    decode_count = cache.shape[0]
    slot_count = prompt_length_list.shape[0]
    prompt_rows = rows_dev - decode_count
    slot_len = prompt_rows // slot_count
    rank_size = ADAPTER_RANK
    head_count = query_key_value_weight.shape[2] // HEAD_DIM
    score_scale = HEAD_DIM ** (-0.5)
    gathered = lax.all_gather(tokens, "mp", axis=1, tiled=True)
    normed = layer_norm(gathered, layernorm_scale, layernorm_bias)
    column = lax.axis_index("mp")
    slice_m = lax.dynamic_slice_in_dim(normed, column * part_cols, part_cols, 1)
    spread = lax.all_to_all(normed, "req", split_axis=1, concat_axis=0, tiled=True)
    projected = lax.psum_scatter(
        jnp.einsum(
            "rd,cde->rce", spread, query_key_value_weight, preferred_element_type=jnp.float32
        ),
        "req",
        scatter_dimension=0,
        tiled=True,
    )
    projected = projected + query_key_value_bias[None]
    positions = jnp.arange(rows_dev)
    request_slot = jnp.where(
        positions < prompt_rows, positions // slot_len, slot_count + positions - prompt_rows
    )
    slot_match = request_slot[:, None] == jnp.arange(slot_count + decode_count)[None, :]
    row_adapter = jnp.sum(jnp.where(slot_match, adapter_index_table[0][None, :], 0), axis=1)
    adapter_on_device = adapter_down_weight.shape[0]
    owners = lax.axis_size("req")
    owner_row = row_adapter // adapter_on_device
    to_owner = owner_row[None, :] == jnp.arange(owners)[:, None]
    outgoing = jnp.where(to_owner[:, :, None], slice_m[None], jnp.zeros((), jnp.bfloat16))
    labels = jnp.where(to_owner, (row_adapter - owner_row * adapter_on_device)[None, :], -1)
    received_rows = lax.all_to_all(outgoing, "req", split_axis=0, concat_axis=0, tiled=True)
    arrived_labels = lax.all_to_all(labels, "req", split_axis=0, concat_axis=0, tiled=True)
    sources, items = arrived_labels.shape
    selection_mask = (
        arrived_labels[:, :, None] == jnp.arange(adapter_on_device)[None, None, :]
    ).astype(jnp.float32)
    adapter_wise_sums = jnp.einsum(
        "yju,ouv->yjov", received_rows, adapter_down_weight, preferred_element_type=jnp.float32
    )
    reduced_rank_rows = jnp.einsum("ogf,ogft->ogt", selection_mask, adapter_wise_sums)
    reduced_rank_rows = lax.psum(reduced_rank_rows, "mp").astype(jnp.bfloat16)
    broadcast_rank_rows = selection_mask.astype(jnp.bfloat16)[
        :, :, :, None, None
    ] * reduced_rank_rows.reshape(sources, items, 1, 2, rank_size)
    corrections = jnp.einsum(
        "pqwgd,wgdx->pqgx",
        broadcast_rank_rows,
        adapter_up_weight,
        preferred_element_type=jnp.float32,
    ).astype(jnp.bfloat16)
    returned = lax.all_to_all(corrections, "req", split_axis=0, concat_axis=0, tiled=True)
    adapter_delta = jnp.sum(returned.astype(jnp.float32), axis=0)
    queries = (projected[:, 0] + adapter_delta[:, 0]).astype(jnp.bfloat16)
    keys_new = projected[:, 1].astype(jnp.bfloat16)
    values_new = (projected[:, 2] + adapter_delta[:, 1]).astype(jnp.bfloat16)
    prompt_q = queries[:prompt_rows].reshape(slot_count, slot_len, head_count, HEAD_DIM)
    prompt_k = keys_new[:prompt_rows].reshape(slot_count, slot_len, head_count, HEAD_DIM)
    prompt_v = values_new[:prompt_rows].reshape(slot_count, slot_len, head_count, HEAD_DIM)
    scores = (
        jnp.einsum("sihd,sjhd->shij", prompt_q, prompt_k, preferred_element_type=jnp.float32)
        * score_scale
    )
    causal = jnp.arange(slot_len)[None, :] <= jnp.arange(slot_len)[:, None]
    scores = jnp.where(causal[None, None], scores, -1e30)
    highest = jnp.max(scores, axis=3, keepdims=True)
    weights = jnp.where(causal[None, None], jnp.exp(scores - highest), 0.0)
    weights = (weights / jnp.sum(weights, axis=3, keepdims=True)).astype(jnp.bfloat16)
    prompt_out = jnp.einsum(
        "shij,sjhd->sihd", weights, prompt_v, preferred_element_type=jnp.float32
    )
    active = jnp.arange(slot_len)[None, :] < prompt_length_list[:, None]
    prompt_out = (
        jnp.where(active[:, :, None, None], prompt_out, 0.0)
        .astype(jnp.bfloat16)
        .reshape(prompt_rows, -1)
    )
    cache_len = cache.shape[1]
    decode_q = queries[prompt_rows:].reshape(decode_count, head_count, HEAD_DIM)
    decode_k = keys_new[prompt_rows:].reshape(decode_count, head_count, HEAD_DIM)
    decode_v = values_new[prompt_rows:].reshape(decode_count, head_count, HEAD_DIM)
    keys_old = cache[:, :, 0].reshape(decode_count, cache_len, head_count, HEAD_DIM)
    values_old = cache[:, :, 1].reshape(decode_count, cache_len, head_count, HEAD_DIM)
    cache_scores = (
        jnp.einsum("dhe,dthe->dht", decode_q, keys_old, preferred_element_type=jnp.float32)
        * score_scale
    )
    live_cache = jnp.arange(cache_len)[None, None, :] < cache_length_list[:, None, None]
    cache_scores = jnp.where(live_cache, cache_scores, -1e30)
    self_score = (
        jnp.einsum("dhe,dhe->dh", decode_q, decode_k, preferred_element_type=jnp.float32)
        * score_scale
    )
    row_top = jnp.maximum(jnp.max(cache_scores, axis=2), self_score)
    cache_weights = jnp.where(live_cache, jnp.exp(cache_scores - row_top[:, :, None]), 0.0)
    self_weight = jnp.exp(self_score - row_top)
    totals = jnp.sum(cache_weights, axis=2) + self_weight
    cache_weights = (cache_weights / totals[:, :, None]).astype(jnp.bfloat16)
    self_weight = (self_weight / totals).astype(jnp.bfloat16)
    decode_out = jnp.einsum(
        "dht,dthe->dhe", cache_weights, values_old, preferred_element_type=jnp.float32
    )
    decode_out = decode_out + self_weight.astype(jnp.float32)[:, :, None] * decode_v.astype(
        jnp.float32
    )
    decode_out = decode_out.astype(jnp.bfloat16).reshape(decode_count, -1)
    attended = jnp.concatenate([prompt_out, decode_out], axis=0)
    mixed = jnp.dot(
        attended,
        lax.all_gather(output_weight, "req", axis=1, tiled=True),
        preferred_element_type=jnp.float32,
    )
    summed = lax.psum_scatter(
        mixed.astype(jnp.bfloat16), "mp", scatter_dimension=1, tiled=True
    ).astype(jnp.float32)
    return (tokens.astype(jnp.float32) + summed + output_bias[None]).astype(jnp.bfloat16)


def solution(mesh):
    placed = (
        P("req", "mp"),
        P(),
        P(),
        P(None, "req", "mp"),
        P(None, "mp"),
        P("req", "mp", None),
        P("req", None, None, "mp"),
        P("req", None),
        P("req"),
        P("req", None, None, "mp"),
        P("req"),
        P("mp", "req"),
        P("mp"),
    )
    quick = mesh.shape["req"] == 2 * NZ and mesh.shape["mp"] == NM
    return jax.shard_map(
        packed_device if quick else on_device, mesh=mesh, in_specs=placed, out_specs=P("req", "mp"), check_vma=False
    )
```

```python
import functools

import jax
import jax.numpy as jnp
from jax import lax
from jax.experimental import pallas as pl
from jax.experimental.pallas import tpu as pltpu
from jax.sharding import PartitionSpec as P

HEAD_DIM = 128
ADAPTER_RANK = 16
BF = jnp.bfloat16
F32 = jnp.float32
MIB = 1 << 20

NZ, NM = 4, 4
SLOTS, PLEN, DEC = 3, 32, 2
QROWS = 24
STAT_ROW = 26
BLK = 32
CHUNK = 128
DCH = 16
PACKED = NM * CHUNK + 2 * NZ * DEC
LANES = 128
DECODE_ROWS = 16
SMALL = pl.CostEstimate(flops=1, bytes_accessed=1, transcendentals=0)
VMEM = pl.BlockSpec(memory_space=pltpu.VMEM)
SMEM = pl.BlockSpec(memory_space=pltpu.SMEM)
ANY = pl.BlockSpec(memory_space=pl.ANY)


def swap_req(x, bits):
    return lax.ppermute(x, "req", [(i, i ^ bits) for i in range(2 * NZ)])


def swap_mp(x, bits):
    return lax.ppermute(x, "mp", [(i, i ^ bits) for i in range(NM)])


def gather_z(x):
    far, near = swap_req(x, 4), swap_req(x, 2)
    return [x, near, far, swap_req(far, 2)]


def limit(mib):
    return pltpu.CompilerParams(vmem_limit_bytes=mib * MIB)


def iota(shape, axis):
    return lax.broadcasted_iota(jnp.int32, shape, axis)


def three(x):
    a = x.astype(BF)
    rest = x - a.astype(F32)
    b = rest.astype(BF)
    return [a.astype(F32), b.astype(F32), (rest - b.astype(F32)).astype(BF).astype(F32)]


class Source:
    def __init__(self, s_ref, t_ref, j):
        z, core = s_ref[3], s_ref[6]
        self.z = jnp.bitwise_xor(z, j % NZ)
        self.core = jnp.bitwise_xor(core, j // NZ)
        self.index = self.z * 2 + self.core
        self.lens = [t_ref[j, i] for i in range(SLOTS)]
        self.adapters = [t_ref[j, SLOTS + i] for i in range(SLOTS + DEC)]
        self.live = self.lens[0] + self.lens[1] + self.lens[2]
        self.size = (self.live + 3) >> 2


def sources(s_ref, t_ref):
    found = [Source(s_ref, t_ref, j) for j in range(2 * NZ)]
    for a in found:
        a.offset = sum(jnp.where(b.index < a.index, b.size, 0) for b in found)
    return found


def by_slot(h, values):
    out = jnp.full_like(h, -1)
    for j in range(SLOTS):
        out = jnp.where((h >> 5) == j, values[j], out)
    return out


def chunk_places(found, other, t, seg, m):
    out = jnp.full_like(t, -1)
    for k in range(NZ):
        a = found[other * NZ + k]
        have = jnp.clip(a.live - m * a.size, 0, a.size)
        prompt = jnp.where(t < have, a.offset + t, -1)
        decode = jnp.where((t < QROWS + DEC) & (a.z == m), CHUNK + a.core * DEC + t - QROWS, -1)
        out = jnp.where(seg == k, jnp.where(t < QROWS, prompt, decode), out)
    return out


def packed_places(a, j, h, m, core):
    i = h & (PLEN - 1)
    starts = [0, a.lens[0], a.lens[0] + a.lens[1]]
    index = by_slot(h, starts) + i
    quarter = sum((index >= q * a.size).astype(jnp.int32) for q in range(1, NM))
    spot = jnp.bitwise_xor(quarter, m) * CHUNK + a.offset + index - quarter * a.size
    half = 2 * CHUNK
    spot = jnp.bitwise_xor(spot >> 8, core) * half + (spot & (half - 1))
    prompt = jnp.where(i < by_slot(h, a.lens), spot, -1)
    first = SLOTS * PLEN
    base = NM * CHUNK + (j // NZ * NZ + turned_bits(j % NZ)) * DEC - first
    decode = jnp.where(h < first + DEC, base + h, -1)
    return jnp.where(h < first, prompt, decode)


def home_adapters(a, h):
    out = by_slot(h, a.adapters)
    for j in range(DEC):
        out = jnp.where(h == SLOTS * PLEN + j, a.adapters[SLOTS + j], out)
    return out


def deal_kernel(s_ref, x_ref, *outs):
    len0, len1, len2, z, m = [s_ref[i] for i in range(5)]
    size = (len0 + len1 + len2 + 3) >> 2
    rows, cols = x_ref.shape
    prompt_rows = SLOTS * PLEN
    t, h = iota((BLK, rows), 0), iota((BLK, rows), 1)
    slot, i = h >> 5, h & (PLEN - 1)
    start = jnp.where(slot == 0, 0, jnp.where(slot == 1, len0, len0 + len1))
    length = jnp.where(slot == 0, len0, jnp.where(slot == 1, len1, len2))
    live = (i < length) & (h < prompt_rows) & (t < size)
    x = x_ref[...]
    wide = x.astype(F32)
    mean = jnp.sum(wide, axis=1, keepdims=True) / cols
    spread = jnp.sum((wide - mean) ** 2, axis=1, keepdims=True)
    lane = iota((rows, LANES), 1)
    stats = jnp.zeros((rows, LANES), F32)
    for j, term in enumerate(three(mean) + three(spread)):
        stats = jnp.where(lane == 2 + j, term, stats)
    same = (iota((rows, LANES), 0) == lane).astype(BF)
    turned = lax.dot_general(stats.astype(BF), same, (((0,), (0,)), ((), ())), preferred_element_type=F32)
    turned = jnp.concatenate([jnp.zeros((8, LANES), F32), turned[:8]], axis=0)
    for k, out in enumerate(outs):
        q = jnp.bitwise_xor(m, k)
        mine = live & (start + i - q * size == t)
        decode = (h >= prompt_rows) & (t == QROWS + h - prompt_rows) & (q == z)
        y = jnp.dot((mine | decode).astype(BF), x, preferred_element_type=F32)
        out[...] = y.astype(BF)
        out[16:32, :LANES] = (y[16:32, :LANES] + turned).astype(BF)


def deal(scalars, tokens):
    return pl.pallas_call(
        deal_kernel,
        out_shape=[jax.ShapeDtypeStruct((BLK, tokens.shape[1]), BF)] * NM,
        in_specs=[SMEM, VMEM],
        out_specs=[VMEM] * NM,
        compiler_params=limit(12),
        cost_estimate=SMALL,
        name="deal_rows",
    )(scalars, tokens)


def norm_kernel(s_ref, b0, b1, b2, b3, affine_ref, table_ref, _, __, o0, o1, o2, o3, held):
    z, m = s_ref[3], s_ref[4]
    cols = b0.shape[1]
    for k, ref in enumerate((b0, b1, b2, b3)):
        held[k] = ref[...].astype(F32)
    width = NM * cols
    means, spreads = [], []
    for k in range(NM):
        part = held[k, 24:32, :LANES]
        means.append(part[2:3] + part[3:4] + part[4:5])
        spreads.append(part[5:6] + part[6:7] + part[7:8])
    mean = sum(means) / NM
    var = (sum(spreads) + cols * sum((v - mean) ** 2 for v in means)) / width
    row = iota((BLK, LANES), 0)
    extra = []
    for value in (mean, lax.rsqrt(var + 1e-05)):
        block = jnp.zeros((BLK, LANES), F32)
        for j, term in enumerate(three(value)):
            block = jnp.where(row == STAT_ROW + j, term, block)
        extra.append(block)
    extra = jnp.concatenate(extra, axis=1)
    extra = jnp.where(iota(extra.shape, 0) == BLK - 1, table_ref[:, : 2 * LANES], extra)
    mean = sum(jnp.sum(held[k], axis=1, keepdims=True) for k in range(NM)) / width
    var = sum(jnp.sum((held[k] - mean) ** 2, axis=1, keepdims=True) for k in range(NM)) / width
    rstd = lax.rsqrt(var + 1e-05)
    last = iota((BLK, cols), 0) == BLK - 1
    stats = iota((BLK, 2 * LANES), 0) >= STAT_ROW
    for k, out in enumerate((o0, o1, o2, o3)):
        block = jnp.bitwise_xor(z, k)
        x = held[jnp.bitwise_xor(block, m)]
        y = (x - mean) * rstd * affine_ref[block] + affine_ref[NM + block]
        y = jnp.where(last, table_ref[...], y)
        out[...] = y.astype(BF)
        out[:, : 2 * LANES] = jnp.where(stats, extra, y[:, : 2 * LANES]).astype(BF)


def norm_rows(scalars, blocks, affine, table, near, far):
    return pl.pallas_call(
        norm_kernel,
        out_shape=[jax.ShapeDtypeStruct(blocks[0].shape, BF)] * NZ,
        in_specs=[SMEM] + [VMEM] * 6 + [ANY] * 2,
        out_specs=[VMEM] * NZ,
        scratch_shapes=[pltpu.VMEM((NM,) + blocks[0].shape, F32)],
        compiler_params=limit(12),
        cost_estimate=SMALL,
        name="norm_rows",
    )(scalars, *blocks, affine, table, near, far)


def cores_kernel(s_ref, b0, b1, b2, b3, mine_ref, theirs_ref):
    core = s_ref[6]
    width = mine_ref.shape[1]
    for k, ref in enumerate((b0, b1, b2, b3)):
        rows = slice(k * BLK, (k + 1) * BLK)
        mine_ref[rows, :] = ref[:, pl.ds(pl.multiple_of(core * width, LANES), width)]
        theirs_ref[rows, :] = ref[:, pl.ds(pl.multiple_of((1 - core) * width, LANES), width)]


def split_cores(scalars, blocks):
    out = jax.ShapeDtypeStruct((NZ * BLK, blocks[0].shape[1] // 2), BF)
    return pl.pallas_call(
        cores_kernel,
        out_shape=[out, out],
        in_specs=[SMEM] + [VMEM] * NZ,
        out_specs=[VMEM] * 2,
        compiler_params=limit(12),
        cost_estimate=SMALL,
        name="split_cores",
    )(scalars, *blocks)


def pack_kernel(s_ref, t_ref, a_ref, b_ref, o_ref):
    found = sources(s_ref, t_ref)
    half = a_ref.shape[0]
    lane = iota((1, half), 1)
    total = None
    for other, ref in enumerate((a_ref, b_ref)):
        to = chunk_places(found, other, lane & (BLK - 1), lane // BLK, s_ref[4])
        pick = (iota((o_ref.shape[0], half), 0) == to).astype(BF)
        term = jnp.dot(pick, ref[...], preferred_element_type=F32)
        total = term if total is None else total + term
    o_ref[...] = total.astype(BF)


def pack_rows(scalars, tables, mine, theirs):
    return pl.pallas_call(
        pack_kernel,
        out_shape=jax.ShapeDtypeStruct((CHUNK + DCH, mine.shape[1]), BF),
        in_specs=[SMEM] * 2 + [VMEM] * 2,
        out_specs=VMEM,
        compiler_params=limit(12),
        cost_estimate=SMALL,
        name="pack_rows",
    )(scalars, tables, mine, theirs)


def copy_kernel(x_ref, _, o_ref):
    o_ref[...] = x_ref[...]


def copy_rows(x, after):
    return pl.pallas_call(
        copy_kernel,
        out_shape=jax.ShapeDtypeStruct(x.shape, x.dtype),
        in_specs=[VMEM, ANY],
        out_specs=VMEM,
        compiler_params=limit(12),
        cost_estimate=SMALL,
        name="copy_rows",
    )(x, after)


def code_kernel(s_ref, t_ref, _, col_ref, row_ref):
    found = sources(s_ref, t_ref)
    m, core = s_ref[4], s_ref[6]
    n = NM * CHUNK
    lane, sub = iota((1, LANES), 1), iota((LANES, 1), 0)
    down, across = iota((n, LANES), 0), iota((LANES, n), 1)
    cols, rows = jnp.zeros((n, 1), jnp.int32), jnp.zeros((1, n), jnp.int32)
    for j, a in enumerate(found):
        first = a.index * SLOTS * PLEN + 1
        hit = down == packed_places(a, j, lane, m, core)
        cols = cols + jnp.sum(jnp.where(hit, first + lane, 0), axis=1, keepdims=True)
        hit = across == packed_places(a, j, sub, m, core)
        rows = rows + jnp.sum(jnp.where(hit, first + sub, 0), axis=0, keepdims=True)
    unused = (1 << 16) + PLEN * iota((n, 1), 0)
    col_ref[...] = jnp.where(cols > 0, cols - 1, unused)
    unused = (1 << 16) + PLEN * iota((1, n), 1)
    row_ref[...] = jnp.where(rows > 0, rows - 1, unused)


def packed_codes(scalars, tables, after):
    n = NM * CHUNK
    return pl.pallas_call(
        code_kernel,
        out_shape=[jax.ShapeDtypeStruct((n, 1), jnp.int32), jax.ShapeDtypeStruct((1, n), jnp.int32)],
        in_specs=[SMEM] * 2 + [ANY],
        out_specs=[VMEM] * 2,
        compiler_params=limit(12),
        cost_estimate=SMALL,
        name="packed_codes",
    )(scalars, tables, after)


def rank_kernel(s_ref, table_ref, da_ref, db_ref, x0, x1, x2, x3, t0, t1, t2, t3, affine_ref, o_ref):
    m, r = s_ref[4], s_ref[5]
    width = 2 * ADAPTER_RANK
    count = da_ref.shape[0] // width
    rows = x0.shape[0]
    same = (iota((rows, LANES), 0) == iota((rows, LANES), 1)).astype(BF)
    o_ref[...] = jnp.zeros_like(o_ref)
    for k, (x, stats) in enumerate(zip((x0, x1, x2, x3), (t0, t1, t2, t3))):

        def column(at):
            turned = lax.dot_general(
                same, stats[16:32, at], (((1,), (1,)), ((), ())), preferred_element_type=F32
            )
            j = STAT_ROW - 16
            return turned[:, j : j + 1] + turned[:, j + 1 : j + 2] + turned[:, j + 2 : j + 3]

        mean, rstd = column(slice(0, LANES)), column(slice(LANES, 2 * LANES))
        normed = ((x[...].astype(F32) - mean) * rstd * affine_ref[m] + affine_ref[NM + m]).astype(BF)
        ids = home_adapters(Source(s_ref, table_ref, k), iota((1, rows), 1))
        total = jnp.zeros((width, rows), F32)
        for core, d in enumerate((da_ref, db_ref)):
            y = lax.dot_general(d[...], normed, (((1,), (1,)), ((), ())), preferred_element_type=F32)
            first = jnp.bitwise_xor(r, core) * count
            for a in range(count):
                total = total + jnp.where(ids == first + a, y[a * width : (a + 1) * width], 0.0)
        o_ref[:, k * LANES : k * LANES + rows] = total


def low_rank_rows(scalars, tables, down, down_other, pieces, stats, affine):
    return pl.pallas_call(
        rank_kernel,
        out_shape=jax.ShapeDtypeStruct((2 * ADAPTER_RANK, NZ * LANES), F32),
        in_specs=[SMEM] * 2 + [VMEM] * 11,
        out_specs=VMEM,
        compiler_params=limit(12),
        cost_estimate=SMALL,
        name="low_rank_rows",
    )(scalars, tables, down, down_other, *pieces, *stats, affine)


def expand_kernel(s_ref, t_ref, low_ref, low_other_ref, base_ref, key_ref, up_ref, _, o_ref, keep_ref, send_ref, *, count):
    m, r, core = s_ref[4], s_ref[5], s_ref[6]
    found = sources(s_ref, t_ref)
    width = count * ADAPTER_RANK
    repeat = []
    for t in range(2):
        shape = (width, 2 * ADAPTER_RANK)
        repeat.append((iota(shape, 1) == t * ADAPTER_RANK + iota(shape, 0) % ADAPTER_RANK).astype(BF))
    repeat = jnp.concatenate(repeat, axis=0)
    adapter = r * count + (iota((2 * width, LANES), 0) % width) // ADAPTER_RANK
    lane = iota((1, LANES), 1)
    total = jnp.zeros((PACKED, 2 * width), F32)
    for j, a in enumerate(found):
        ref = low_other_ref if j >= NZ else low_ref
        k = j % NZ
        low = jnp.dot(repeat, ref[:, k * LANES : (k + 1) * LANES], preferred_element_type=F32)
        low = jnp.where(adapter == home_adapters(a, lane), low, 0.0).astype(BF)
        hit = (iota((PACKED, LANES), 0) == packed_places(a, j, lane, m, core)).astype(BF)
        total = total + lax.dot_general(hit, low, (((1,), (1,)), ((), ())), preferred_element_type=F32)
    feats = up_ref.shape[3]
    half = keep_ref.shape[0]
    keep_ref[:, feats : 2 * feats] = key_ref[:half, :]
    send_ref[:, feats : 2 * feats] = key_ref[half:, :]
    for t, first in ((0, 0), (1, 2 * feats)):
        rows = total[:, t * width : (t + 1) * width].astype(BF)
        o_ref[t] = rows
        up = up_ref[:, t].reshape(-1, feats)
        term = jnp.dot(rows[NM * CHUNK :, :], up, preferred_element_type=F32)
        term = term + base_ref[:, t * feats : (t + 1) * feats]
        keep_ref[:, first : first + feats] = term[:half]
        send_ref[:, first : first + feats] = term[half:]


def expand_rows(scalars, tables, low, low_other, base, keys, up, count, after):
    half = jax.ShapeDtypeStruct((keys.shape[0] // 2, 3 * keys.shape[1]), F32)
    return pl.pallas_call(
        functools.partial(expand_kernel, count=count),
        out_shape=[jax.ShapeDtypeStruct((2, PACKED, count * ADAPTER_RANK), BF), half, half],
        in_specs=[SMEM] * 2 + [VMEM] * 5 + [ANY],
        out_specs=[VMEM] * 3,
        compiler_params=limit(12),
        cost_estimate=SMALL,
        name="expand_rows",
    )(scalars, tables, low, low_other, base, keys, up, after)


def emit_sums(y, own_ref, other_ref):
    half = 2 * CHUNK
    own_ref[...] = y[:half].astype(BF)
    other_ref[...] = y[half : 2 * half].astype(BF)


def first_project_kernel(s_ref, c0, c1, c2, c3, w_ref, _, own_ref, other_ref, dec_ref, x):
    z, m, core = s_ref[3], s_ref[4], s_ref[6]

    @pl.when(pl.program_id(0) == 0)
    def _():
        chunks = (c0, c1, c2, c3)
        for k, chunk in enumerate(chunks):
            base = jnp.bitwise_xor(core, k >> 1) * 2 * CHUNK + (k & 1) * CHUNK
            x[pl.ds(pl.multiple_of(base, CHUNK), CHUNK), :] = chunk[:CHUNK, :]
        n, at = iota((2 * NZ * DEC, NM * DCH), 0), iota((2 * NZ * DEC, NM * DCH), 1)
        chip = jnp.bitwise_xor(z, turned_bits((n >> 1) & 3))
        want = jnp.bitwise_xor(chip, m) * DCH + jnp.bitwise_xor(core, n >> 3) * DEC + (n & 1)
        rows = jnp.concatenate([chunk[CHUNK:, :] for chunk in chunks], axis=0)
        x[NM * CHUNK :, :] = jnp.dot((want == at).astype(BF), rows, preferred_element_type=F32).astype(BF)

    y = jnp.dot(x[...], w_ref[0], preferred_element_type=F32)
    emit_sums(y, own_ref, other_ref)
    dec_ref[...] = y[NM * CHUNK :]


def project_rows(scalars, chunks, weight, part, after):
    _, depth, feats = weight.shape
    tile = feats // 2
    half = 2 * CHUNK
    whole = [pl.BlockSpec(v.shape, lambda j: (0, 0)) for v in chunks]
    out_shape = [
        jax.ShapeDtypeStruct((half, feats), BF),
        jax.ShapeDtypeStruct((half, feats), BF),
        jax.ShapeDtypeStruct((PACKED - NM * CHUNK, feats), F32),
        jax.ShapeDtypeStruct((PACKED, depth), BF),
    ]
    out_specs = [pl.BlockSpec((v.shape[0], tile), lambda j: (0, j)) for v in out_shape[:3]]
    out_specs.append(pl.BlockSpec((PACKED, depth), lambda j: (0, 0)))
    return pl.pallas_call(
        first_project_kernel,
        grid=(feats // tile,),
        out_shape=out_shape,
        in_specs=[SMEM] + whole + [pl.BlockSpec((1, depth, tile), lambda j: (part, 0, j)), ANY],
        out_specs=out_specs,
        compiler_params=limit(12),
        cost_estimate=SMALL,
        name="project_keys",
    )(scalars, *chunks, weight, after)


def adapted_kernel(x_ref, w_ref, e_ref, u_ref, _, *outs):
    y = jnp.dot(x_ref[: NM * CHUNK, :], w_ref[0], preferred_element_type=F32)
    up = u_ref[...].reshape(-1, u_ref.shape[-1])
    y = y + jnp.dot(e_ref[0, : NM * CHUNK, :], up, preferred_element_type=F32)
    emit_sums(y, *outs)


def project_adapted(rows, weight, part, expanded, up, after):
    _, depth, feats = weight.shape
    tile = feats // 2
    half = 2 * CHUNK
    which = part // 2
    out_shape = [
        jax.ShapeDtypeStruct((half, feats), BF),
        jax.ShapeDtypeStruct((half, feats), BF),
    ]
    return pl.pallas_call(
        adapted_kernel,
        grid=(2,),
        out_shape=out_shape,
        in_specs=[
            pl.BlockSpec(rows.shape, lambda j: (0, 0)),
            pl.BlockSpec((1, depth, tile), lambda j: (part, 0, j)),
            pl.BlockSpec((1,) + expanded.shape[1:], lambda j: (which, 0, 0)),
            pl.BlockSpec((up.shape[0], 1, up.shape[2], tile), lambda j: (0, which, 0, j)),
            ANY,
        ],
        out_specs=[pl.BlockSpec((v.shape[0], tile), lambda j: (0, j)) for v in out_shape],
        compiler_params=limit(12),
        cost_estimate=SMALL,
        name="project_adapted",
    )(rows, weight, expanded, up, after)


def add_kernel(a_ref, b_ref, _, o_ref):
    o_ref[...] = (a_ref[: b_ref.shape[0], :] + b_ref[...]).astype(o_ref.dtype)


def add_rows(a, b, after, dtype=F32):
    return pl.pallas_call(
        add_kernel,
        out_shape=jax.ShapeDtypeStruct(b.shape, dtype),
        in_specs=[VMEM] * 2 + [ANY],
        out_specs=VMEM,
        compiler_params=limit(12),
        cost_estimate=SMALL,
        name="add_rows",
    )(a, b, after)


def decode_finish_kernel(a_ref, b_ref, bias_ref, _, q_ref, k_ref, v_ref):
    total = a_ref[: b_ref.shape[0], :] + b_ref[...]
    feats = bias_ref.shape[1]
    for j, out in enumerate((q_ref, k_ref, v_ref)):
        part = total[:, j * feats : (j + 1) * feats] + bias_ref[j : j + 1, :]
        for i in range(out.shape[0]):
            out[i] = part[i : i + 1].astype(BF)


def decode_finish(a, b, bias, after):
    out = jax.ShapeDtypeStruct((b.shape[0], 1, bias.shape[1]), BF)
    return pl.pallas_call(
        decode_finish_kernel,
        out_shape=[out] * 3,
        in_specs=[VMEM] * 3 + [ANY],
        out_specs=[VMEM] * 3,
        compiler_params=limit(12),
        cost_estimate=SMALL,
        name="decode_finish",
    )(a, b, bias, after)


def decode_base_kernel(x_ref, w_ref, _, o_ref):
    o_ref[...] = jnp.dot(x_ref[...], w_ref[0], preferred_element_type=F32)


def decode_base(rows, weight, after):
    _, depth, feats = weight.shape
    count = PACKED - NM * CHUNK
    return pl.pallas_call(
        decode_base_kernel,
        grid=(2,),
        out_shape=jax.ShapeDtypeStruct((count, 2 * feats), F32),
        in_specs=[
            pl.BlockSpec((count, depth), lambda p: (NM * CHUNK // count, 0)),
            pl.BlockSpec((1, depth, feats), lambda p: (2 * p, 0, 0)),
            ANY,
        ],
        out_specs=pl.BlockSpec((count, feats), lambda p: (0, p)),
        compiler_params=limit(12),
        cost_estimate=SMALL,
        name="decode_base",
    )(rows, weight, after)


def halve_kernel(s_ref, *refs, bit, groups):
    *ins, _, send_ref, keep_ref = refs
    count = len(ins) // 2
    side = (s_ref[3] >> bit) & 1
    to = 0
    for total_ref, got_ref in zip(ins[:count], ins[count:]):
        width = total_ref.shape[1] // groups // 2

        for g in range(groups):

            def part(which):
                at = pl.ds(pl.multiple_of((2 * g + which) * width, LANES), width)
                return total_ref[:, at].astype(F32) + got_ref[:, at].astype(F32)

            send_ref[:, to : to + width] = part(1 - side).astype(BF)
            keep_ref[:, to : to + width] = part(side)
            to += width


def halve(scalars, totals, gots, bit, after, groups=1):
    rows = totals[0].shape[0]
    feats = sum(v.shape[1] for v in totals) // 2
    return pl.pallas_call(
        functools.partial(halve_kernel, bit=bit, groups=groups),
        out_shape=[jax.ShapeDtypeStruct((rows, feats), BF), jax.ShapeDtypeStruct((rows, feats), F32)],
        in_specs=[SMEM] + [VMEM] * (2 * len(totals)) + [ANY],
        out_specs=[VMEM, VMEM],
        compiler_params=limit(12),
        cost_estimate=SMALL,
        name="halve_sums",
    )(scalars, *totals, *gots, after)


def finish_kernel(s_ref, total_ref, got_ref, bias_ref, _, *outs, parts):
    for j, (part, out) in enumerate(zip(parts, outs)):
        width = out.shape[1]
        at = pl.ds(pl.multiple_of(place_of(s_ref[3]) * width, LANES), width)
        mine = slice(j * width, (j + 1) * width)
        total = total_ref[:, mine] + got_ref[:, mine].astype(F32) + bias_ref[part : part + 1, at]
        out[...] = total.astype(BF)


def finish(scalars, total, got, bias, parts, after):
    rows, feats = total.shape
    return pl.pallas_call(
        functools.partial(finish_kernel, parts=parts),
        out_shape=[jax.ShapeDtypeStruct((rows, feats // len(parts)), BF)] * len(parts),
        in_specs=[SMEM, VMEM, VMEM, VMEM, ANY],
        out_specs=[VMEM] * len(parts),
        compiler_params=limit(12),
        cost_estimate=SMALL,
        name="finish_sums",
    )(scalars, total, got, bias, after)


def prompt_kernel(q_ref, ka_ref, kb_ref, va_ref, vb_ref, cr_ref, cc_ref, d_ref, o_ref):
    rows = cr_ref[...]
    cols = cc_ref[...]
    allowed = ((rows >> 5) == (cols >> 5)) & (cols <= rows)
    keys = jnp.concatenate([ka_ref[...], kb_ref[...]], axis=0)
    values = jnp.concatenate([va_ref[...], vb_ref[...]], axis=0)
    for h in range(q_ref.shape[1] // HEAD_DIM):
        at = slice(h * HEAD_DIM, (h + 1) * HEAD_DIM)
        s = lax.dot_general(q_ref[:, at], keys[:, at], (((1,), (1,)), ((), ())), preferred_element_type=F32)
        s = jnp.where(allowed, s * HEAD_DIM**-0.5, -1e30)
        top = jnp.max(s, axis=1, keepdims=True)
        w = jnp.where(allowed, jnp.exp(s - top), 0.0)
        w = (w / jnp.sum(w, axis=1, keepdims=True)).astype(BF)
        o_ref[: q_ref.shape[0], at] = jnp.dot(w, values[:, at], preferred_element_type=F32).astype(BF)
    width = q_ref.shape[1]
    n = iota((DECODE_ROWS, width), 0)
    tail = jnp.zeros((DECODE_ROWS, width), F32)
    for b in range(NZ):
        for j in range(DEC):
            tail = jnp.where(n == b * DEC + j, d_ref[j : j + 1, b * width : (b + 1) * width].astype(F32), tail)
    o_ref[q_ref.shape[0] :, :] = tail.astype(BF)


def prompt_attention(q, ka, kb, va, vb, code_rows, code_cols, dec):
    return pl.pallas_call(
        prompt_kernel,
        out_shape=jax.ShapeDtypeStruct((q.shape[0] + DECODE_ROWS, q.shape[1]), BF),
        in_specs=[VMEM] * 8,
        out_specs=VMEM,
        compiler_params=limit(12),
        cost_estimate=SMALL,
        name="prompt_attention",
    )(q, ka, kb, va, vb, code_rows, code_cols, dec)


def decode_kernel(len_ref, q_ref, k_ref, v_ref, c_ref, _, o_ref, qbd, top, total, acc):
    d, t = pl.program_id(0), pl.program_id(1)
    span = c_ref.shape[1]
    live = len_ref[d]
    heads, feats = qbd.shape
    diag = lax.broadcasted_iota(jnp.int32, (heads, feats), 1) // HEAD_DIM == lax.broadcasted_iota(
        jnp.int32, (heads, feats), 0
    )

    @pl.when(t == 0)
    def _():
        q = jnp.where(diag, q_ref[0].astype(F32), 0.0)
        qbd[...] = q.astype(BF)
        own = jnp.sum(q * k_ref[0].astype(F32), axis=1, keepdims=True) * HEAD_DIM**-0.5
        top[...] = jnp.broadcast_to(own, top.shape)
        total[...] = jnp.ones_like(total)
        acc[...] = jnp.broadcast_to(v_ref[0].astype(F32), acc.shape)

    @pl.when(t * span < live)
    def _():
        x = c_ref[0].reshape(2 * span, feats)
        s = lax.dot_general(qbd[...], x, (((1,), (1,)), ((), ())), preferred_element_type=F32)
        column = lax.broadcasted_iota(jnp.int32, s.shape, 1)
        valid = (column % 2 == 0) & (t * span + column // 2 < live)
        s = jnp.where(valid, s * HEAD_DIM**-0.5, -1e30)
        before = top[:, :1]
        now = jnp.maximum(before, jnp.max(s, axis=1, keepdims=True))
        fade = jnp.exp(before - now)
        w = jnp.where(valid, jnp.exp(s - now), 0.0)
        total[...] = total[...] * fade + jnp.sum(w, axis=1, keepdims=True)
        top[...] = jnp.broadcast_to(now, top.shape)
        w = pltpu.roll(w, 1, 1).astype(BF)
        acc[...] = acc[...] * fade + jnp.dot(w, x, preferred_element_type=F32)

    @pl.when(t == pl.num_programs(1) - 1)
    def _():
        o = acc[...] / total[:, :1]
        o_ref[0] = jnp.sum(jnp.where(diag, o, 0.0), axis=0, keepdims=True).astype(BF)


def decode_attention(lengths, q, k, v, cache, after, span=512):
    count, positions, _, feats = cache.shape
    row = pl.BlockSpec((1, 1, feats), lambda d, t, n: (d, 0, 0))
    heads = 16
    return pl.pallas_call(
        decode_kernel,
        grid_spec=pltpu.PrefetchScalarGridSpec(
            num_scalar_prefetch=1,
            grid=(count, positions // span),
            in_specs=[row, row, row]
            + [pl.BlockSpec((1, span, 2, feats), lambda d, t, n: (d, jnp.minimum(t, (n[d] - 1) // span), 0, 0)), ANY],
            out_specs=row,
            scratch_shapes=[
                pltpu.VMEM((heads, feats), BF),
                pltpu.VMEM((heads, LANES), F32),
                pltpu.VMEM((heads, LANES), F32),
                pltpu.VMEM((heads, feats), F32),
            ],
        ),
        out_shape=jax.ShapeDtypeStruct((count, 1, feats), BF),
        compiler_params=limit(44),
        cost_estimate=SMALL,
        name="decode_attention",
    )(lengths, q, k, v, cache, after)


def out_term(z, k, own, other, w_ref):
    width = own.shape[1]
    half = own.shape[0] - DECODE_ROWS
    block = place_of(jnp.bitwise_xor(z, k))
    w = w_ref[pl.ds(pl.multiple_of(block * width, width), width), :]
    rows = jnp.concatenate([own[:half, :], other[:half, :]], axis=0)
    return jnp.dot(rows, w, preferred_element_type=F32)


def out_first_kernel(place_ref, *refs):
    own, other, w_ref, o_ref = refs[:3], refs[3:6], refs[6], refs[7]
    total = None
    for k in range(NZ - 1):
        term = out_term(place_ref[3], k, own[k], other[k], w_ref)
        total = term if total is None else total + term
    o_ref[...] = total


def out_first(scalars, own, other, weight):
    return pl.pallas_call(
        out_first_kernel,
        out_shape=jax.ShapeDtypeStruct((NM * CHUNK, weight.shape[1]), F32),
        in_specs=[SMEM] + [VMEM] * 7,
        out_specs=VMEM,
        compiler_params=limit(12),
        cost_estimate=SMALL,
        name="out_first",
    )(scalars, *own[:3], *other[:3], weight)


def out_kernel(place_ref, *refs):
    own, other, first_ref, w_ref, outs, mixed = refs[:4], refs[4:8], refs[8], refs[9], refs[10:14], refs[14]
    z, m, core = place_ref[3], place_ref[4], place_ref[6]
    width = own[0].shape[1]
    half = own[0].shape[0] - DECODE_ROWS
    mixed[...] = (first_ref[...] + out_term(z, NZ - 1, own[-1], other[-1], w_ref)).astype(BF)
    tails = jnp.concatenate([v[half:, :] for v in own + other], axis=0)
    count = 2 * NZ * DEC
    n, at = iota((count, tails.shape[0]), 0), iota((count, tails.shape[0]), 1)
    total = None
    for b in range(NZ):
        pick = (at == (n // DEC) * DECODE_ROWS + b * DEC + n % DEC).astype(BF)
        rows = jnp.dot(pick, tails, preferred_element_type=F32).astype(BF)
        term = jnp.dot(rows, w_ref[b * width : (b + 1) * width, :], preferred_element_type=F32)
        total = term if total is None else total + term
    decode = total.astype(BF)
    n, at = iota((DCH, count), 0), iota((DCH, count), 1)
    for k, out in enumerate(outs):
        base = jnp.bitwise_xor(core, k >> 1) * 2 * CHUNK + (k & 1) * CHUNK
        out[:CHUNK, :] = mixed[pl.ds(pl.multiple_of(base, CHUNK), CHUNK), :]
        far = jnp.bitwise_xor(jnp.bitwise_xor(m, k), z)
        want = (jnp.bitwise_xor(core, n >> 1) * NZ + far) * DEC + (n & 1)
        pick = ((at == want) & (n < 2 * DEC)).astype(BF)
        out[CHUNK:, :] = jnp.dot(pick, decode, preferred_element_type=F32).astype(BF)


def out_project(scalars, own, other, first, weight):
    feats = weight.shape[1]
    return pl.pallas_call(
        out_kernel,
        out_shape=[jax.ShapeDtypeStruct((CHUNK + DCH, feats), BF)] * NM,
        in_specs=[SMEM] + [VMEM] * 10,
        out_specs=[VMEM] * NM,
        scratch_shapes=[pltpu.VMEM((NM * CHUNK, feats), BF)],
        compiler_params=limit(12),
        cost_estimate=SMALL,
        name="out_project",
    )(scalars, *own, *other, first, weight)


def unpack_kernel(s_ref, t_ref, c0, c1, c2, c3, *outs):
    total = sum(c[...].astype(F32) for c in (c0, c1, c2, c3)).astype(BF)
    found = sources(s_ref, t_ref)
    n = iota((NZ * BLK, 1), 0)
    for other in range(2):
        to = chunk_places(found, other, n & (BLK - 1), n // BLK, s_ref[4])
        pick = (iota((NZ * BLK, total.shape[0]), 1) == to).astype(BF)
        rows = jnp.dot(pick, total, preferred_element_type=F32).astype(BF)
        for k, out in enumerate(outs):
            out[other * BLK : (other + 1) * BLK, :] = rows[k * BLK : (k + 1) * BLK]


def unpack_rows(scalars, tables, chunks):
    feats = chunks[0].shape[1]
    return pl.pallas_call(
        unpack_kernel,
        out_shape=[jax.ShapeDtypeStruct((2 * BLK, feats), BF)] * NZ,
        in_specs=[SMEM] * 2 + [VMEM] * 4,
        out_specs=[VMEM] * NZ,
        compiler_params=limit(12),
        cost_estimate=SMALL,
        name="unpack_rows",
    )(scalars, tables, *chunks)


def join_kernel(s_ref, a0, a1, a2, a3, other_ref, o0, o1, o2, o3, held):
    z, m, core = s_ref[3], s_ref[4], s_ref[6]
    width = a0.shape[1]
    mine = pl.ds(pl.multiple_of(core * width, LANES), width)
    theirs = pl.ds(pl.multiple_of((1 - core) * width, LANES), width)
    for k, ref in enumerate((a0, a1, a2, a3)):
        held[k, :, mine] = ref[:BLK, :]
        held[k, :, theirs] = other_ref[k * BLK : (k + 1) * BLK, :]
    for k, out in enumerate((o0, o1, o2, o3)):
        out[...] = held[jnp.bitwise_xor(jnp.bitwise_xor(z, m), k)]


def join_halves(scalars, parts, other):
    shape = (BLK, 2 * parts[0].shape[1])
    return pl.pallas_call(
        join_kernel,
        out_shape=[jax.ShapeDtypeStruct(shape, BF)] * NM,
        in_specs=[SMEM] + [VMEM] * 5,
        out_specs=[VMEM] * NM,
        scratch_shapes=[pltpu.VMEM((NZ,) + shape, BF)],
        compiler_params=limit(12),
        cost_estimate=SMALL,
        name="join_halves",
    )(scalars, *parts, other)


def home_kernel(s_ref, x_ref, bias_ref, b0, b1, b2, b3, o_ref):
    len0, len1, len2, z, m = [s_ref[i] for i in range(5)]
    size = (len0 + len1 + len2 + 3) >> 2
    rows = x_ref.shape[0]
    prompt_rows = SLOTS * PLEN
    t, h = iota((rows, BLK), 1), iota((rows, BLK), 0)
    slot, i = h >> 5, h & (PLEN - 1)
    start = jnp.where(slot == 0, 0, jnp.where(slot == 1, len0, len0 + len1))
    length = jnp.where(slot == 0, len0, jnp.where(slot == 1, len1, len2))
    live = (i < length) & (h < prompt_rows) & (t < size)
    total = x_ref[...].astype(F32) + bias_ref[...]
    for k, ref in enumerate((b0, b1, b2, b3)):
        q = jnp.bitwise_xor(m, k)
        mine = live & (start + i - q * size == t)
        decode = (h >= prompt_rows) & (t == QROWS + h - prompt_rows) & (q == z)
        total = total + jnp.dot((mine | decode).astype(BF), ref[...], preferred_element_type=F32)
    o_ref[...] = total.astype(BF)


def add_home(scalars, tokens, bias, blocks):
    return pl.pallas_call(
        home_kernel,
        out_shape=jax.ShapeDtypeStruct(tokens.shape, BF),
        in_specs=[SMEM] + [VMEM] * 6,
        out_specs=VMEM,
        compiler_params=limit(12),
        cost_estimate=SMALL,
        name="add_home",
    )(scalars, tokens, bias, *blocks)


def turned_bits(k):
    return (k & 1) * 2 + (k >> 1)


def place_of(z):
    return turned_bits(z)


def packed_device(
    tokens,
    layernorm_scale,
    layernorm_bias,
    query_key_value_weight,
    query_key_value_bias,
    adapter_down_weight,
    adapter_up_weight,
    adapter_index_table,
    prompt_length_list,
    cache,
    cache_length_list,
    output_weight,
    output_bias,
):
    i32 = jnp.int32
    r = lax.axis_index("req").astype(i32)
    m = lax.axis_index("mp").astype(i32)
    z, c = r >> 1, r & 1
    rows_dev, cols = tokens.shape
    prompt_rows = SLOTS * PLEN
    feats = query_key_value_weight.shape[2]
    depth = query_key_value_weight.shape[1]
    per_z = feats // NZ
    own_adapters = adapter_down_weight.shape[0]
    half = 2 * CHUNK
    order = jnp.arange(2 * NZ, dtype=i32)
    source = ((z ^ (order & 3)) << 1) + (c ^ (order >> 2))
    lens = prompt_length_list
    scalars = jnp.concatenate([lens, jnp.stack([z, m, r, c])])

    down = jnp.transpose(adapter_down_weight, (0, 2, 1)).reshape(own_adapters * 2 * ADAPTER_RANK, cols)

    with jax.named_scope("deal"):
        dealt = deal(scalars, tokens)
    with jax.named_scope("gather_home"):
        pieces = gather_z(tokens)
    with jax.named_scope("deal"):
        blocks = [dealt[0]] + [swap_mp(dealt[k], k) for k in range(1, NM)]
    with jax.named_scope("norm_rows"):
        table = jnp.concatenate([lens, adapter_index_table[0]]).astype(F32)
        table = jnp.pad(table, (0, depth - table.shape[0]))
        table = jnp.tile(table, 2)[None, :]
        affine = jnp.stack([layernorm_scale, layernorm_bias]).reshape(2 * NM, 1, cols)
        normed = norm_rows(scalars, blocks, affine, table, pieces[1], pieces[2])
    with jax.named_scope("spread_z"):
        spread = [normed[0]] + [swap_req(normed[k], 2 * k) for k in range(1, NZ)]
        mine, theirs = split_cores(scalars, spread)
        theirs = swap_req(theirs, 1)

    with jax.named_scope("tables"):
        tables = jnp.concatenate(
            [v.reshape(NZ, BLK, depth)[:, BLK - 1, : SLOTS + SLOTS + DEC] for v in (mine, theirs)], axis=0
        ).astype(i32)
    with jax.named_scope("pack"):
        chunk = pack_rows(scalars, tables, mine, theirs)
    with jax.named_scope("gather_chunks"):
        chunks = [chunk] + [swap_mp(chunk, k) for k in range(1, NM)]

    with jax.named_scope("low_rank"):
        down_other = swap_req(copy_rows(down, mine), 1)
        part = low_rank_rows(scalars, tables, down, down_other, pieces, spread, affine)
        two = add_rows(part, swap_mp(part, 1), part)
    with jax.named_scope("keys"):
        own_k, other_k, dec_k, x_rows = project_rows(scalars, chunks, query_key_value_weight, 1, two)
        core_k = swap_req(other_k, 1)
    with jax.named_scope("decode_rows"):
        base = decode_base(x_rows, query_key_value_weight, other_k)
    with jax.named_scope("low_rank"):
        low_rank = add_rows(two, swap_mp(two, 2), base, BF)
    with jax.named_scope("keys"):
        send_k, keep_k = halve(scalars, [own_k], [core_k], 0, low_rank)
        got_k = swap_req(send_k, 2)
    with jax.named_scope("low_rank"):
        expanded, dec, dec_sent = expand_rows(
            scalars, tables, low_rank, swap_req(low_rank, 1), base, dec_k, adapter_up_weight, own_adapters, send_k
        )
    with jax.named_scope("decode_rows"):
        dec_chip = add_rows(dec, swap_req(dec_sent, 1), expanded)
    with jax.named_scope("values"):
        own_v, other_v = project_adapted(x_rows, query_key_value_weight, 2, expanded, adapter_up_weight, dec_chip)
        core_v = swap_req(other_v, 1)
    with jax.named_scope("decode_rows"):
        dec_pair = add_rows(dec_chip, swap_req(dec_chip[4:], 2), own_v)
    with jax.named_scope("keys"):
        send_k, keep_k = halve(scalars, [keep_k], [got_k], 1, dec_pair)
        got_k = swap_req(send_k, 4)
    with jax.named_scope("decode_rows"):
        dec = decode_finish(dec_pair, swap_req(dec_pair[2:], 4), query_key_value_bias, send_k)
    with jax.named_scope("queries"):
        own_q, other_q = project_adapted(x_rows, query_key_value_weight, 0, expanded, adapter_up_weight, dec[0])
        core_q = swap_req(other_q, 1)
    with jax.named_scope("reduce_z"):
        send, keep = halve(scalars, [own_v, own_q], [core_v, core_q], 0, core_q)
        got = swap_req(send, 2)
    with jax.named_scope("codes"):
        code_col, code_row = packed_codes(scalars, tables, send)
    with jax.named_scope("keys"):
        (keys,) = finish(scalars, keep_k, got_k, query_key_value_bias, (1,), code_row)
        keys_other = swap_req(keys, 1)
    with jax.named_scope("reduce_z"):
        send, keep = halve(scalars, [keep], [got], 1, keys, groups=2)
        got = swap_req(send, 4)
    with jax.named_scope("decode_attention"):
        dec_out = decode_attention(cache_length_list, *dec, cache, send)
        dec_out = dec_out.reshape(DEC, feats)
    with jax.named_scope("reduce_z"):
        values, queries = finish(scalars, keep, got, query_key_value_bias, (2, 0), dec_out)
        values_other = swap_req(values, 1)
    with jax.named_scope("prompt_attention"):
        attended = prompt_attention(
            queries,
            keys,
            keys_other,
            values,
            values_other,
            code_col[: 2 * CHUNK],
            code_row,
            dec_out,
        )
    with jax.named_scope("gather_attended"):
        own = gather_z(attended)
        other = [swap_req(v, 1) for v in own]
    with jax.named_scope("out_project"):
        first = out_first(scalars, own, other, output_weight)
        mixed = out_project(scalars, own, other, first, output_weight)
    with jax.named_scope("sum_mp"):
        shares = [mixed[0]] + [swap_mp(mixed[k], k) for k in range(1, NM)]
    with jax.named_scope("return_z"):
        back = unpack_rows(scalars, tables, shares)
        back = [back[0]] + [swap_req(back[k], 2 * k) for k in range(1, NZ)]
        back_other = swap_req(jnp.concatenate([v[BLK:] for v in back], axis=0), 1)
    with jax.named_scope("return_plane"):
        joined = join_halves(scalars, back, back_other)
        joined = [joined[0]] + [swap_mp(joined[k], k) for k in range(1, NM)]
        return add_home(scalars, tokens, output_bias[None], joined)


def layer_norm(row_data, gain_vec, shift_vec):
    values = row_data.astype(jnp.float32)
    average = jnp.mean(values, axis=-1, keepdims=True)
    centred = values - average
    variance = jnp.mean(centred * centred, axis=-1, keepdims=True)
    scaled = centred * lax.rsqrt(variance + 1e-05)
    return (scaled * gain_vec + shift_vec).astype(jnp.bfloat16)


def on_device(
    tokens,
    layernorm_scale,
    layernorm_bias,
    query_key_value_weight,
    query_key_value_bias,
    adapter_down_weight,
    adapter_up_weight,
    adapter_index_table,
    prompt_length_list,
    cache,
    cache_length_list,
    output_weight,
    output_bias,
):
    rows_dev = tokens.shape[0]
    part_cols = tokens.shape[1]
    decode_count = cache.shape[0]
    slot_count = prompt_length_list.shape[0]
    prompt_rows = rows_dev - decode_count
    slot_len = prompt_rows // slot_count
    rank_size = ADAPTER_RANK
    head_count = query_key_value_weight.shape[2] // HEAD_DIM
    score_scale = HEAD_DIM ** (-0.5)
    gathered = lax.all_gather(tokens, "mp", axis=1, tiled=True)
    normed = layer_norm(gathered, layernorm_scale, layernorm_bias)
    column = lax.axis_index("mp")
    slice_m = lax.dynamic_slice_in_dim(normed, column * part_cols, part_cols, 1)
    spread = lax.all_to_all(normed, "req", split_axis=1, concat_axis=0, tiled=True)
    projected = lax.psum_scatter(
        jnp.einsum(
            "rd,cde->rce", spread, query_key_value_weight, preferred_element_type=jnp.float32
        ),
        "req",
        scatter_dimension=0,
        tiled=True,
    )
    projected = projected + query_key_value_bias[None]
    positions = jnp.arange(rows_dev)
    request_slot = jnp.where(
        positions < prompt_rows, positions // slot_len, slot_count + positions - prompt_rows
    )
    slot_match = request_slot[:, None] == jnp.arange(slot_count + decode_count)[None, :]
    row_adapter = jnp.sum(jnp.where(slot_match, adapter_index_table[0][None, :], 0), axis=1)
    adapter_on_device = adapter_down_weight.shape[0]
    owners = lax.axis_size("req")
    owner_row = row_adapter // adapter_on_device
    to_owner = owner_row[None, :] == jnp.arange(owners)[:, None]
    outgoing = jnp.where(to_owner[:, :, None], slice_m[None], jnp.zeros((), jnp.bfloat16))
    labels = jnp.where(to_owner, (row_adapter - owner_row * adapter_on_device)[None, :], -1)
    received_rows = lax.all_to_all(outgoing, "req", split_axis=0, concat_axis=0, tiled=True)
    arrived_labels = lax.all_to_all(labels, "req", split_axis=0, concat_axis=0, tiled=True)
    sources, items = arrived_labels.shape
    selection_mask = (
        arrived_labels[:, :, None] == jnp.arange(adapter_on_device)[None, None, :]
    ).astype(jnp.float32)
    adapter_wise_sums = jnp.einsum(
        "yju,ouv->yjov", received_rows, adapter_down_weight, preferred_element_type=jnp.float32
    )
    reduced_rank_rows = jnp.einsum("ogf,ogft->ogt", selection_mask, adapter_wise_sums)
    reduced_rank_rows = lax.psum(reduced_rank_rows, "mp").astype(jnp.bfloat16)
    broadcast_rank_rows = selection_mask.astype(jnp.bfloat16)[
        :, :, :, None, None
    ] * reduced_rank_rows.reshape(sources, items, 1, 2, rank_size)
    corrections = jnp.einsum(
        "pqwgd,wgdx->pqgx",
        broadcast_rank_rows,
        adapter_up_weight,
        preferred_element_type=jnp.float32,
    ).astype(jnp.bfloat16)
    returned = lax.all_to_all(corrections, "req", split_axis=0, concat_axis=0, tiled=True)
    adapter_delta = jnp.sum(returned.astype(jnp.float32), axis=0)
    queries = (projected[:, 0] + adapter_delta[:, 0]).astype(jnp.bfloat16)
    keys_new = projected[:, 1].astype(jnp.bfloat16)
    values_new = (projected[:, 2] + adapter_delta[:, 1]).astype(jnp.bfloat16)
    prompt_q = queries[:prompt_rows].reshape(slot_count, slot_len, head_count, HEAD_DIM)
    prompt_k = keys_new[:prompt_rows].reshape(slot_count, slot_len, head_count, HEAD_DIM)
    prompt_v = values_new[:prompt_rows].reshape(slot_count, slot_len, head_count, HEAD_DIM)
    scores = (
        jnp.einsum("sihd,sjhd->shij", prompt_q, prompt_k, preferred_element_type=jnp.float32)
        * score_scale
    )
    causal = jnp.arange(slot_len)[None, :] <= jnp.arange(slot_len)[:, None]
    scores = jnp.where(causal[None, None], scores, -1e30)
    highest = jnp.max(scores, axis=3, keepdims=True)
    weights = jnp.where(causal[None, None], jnp.exp(scores - highest), 0.0)
    weights = (weights / jnp.sum(weights, axis=3, keepdims=True)).astype(jnp.bfloat16)
    prompt_out = jnp.einsum(
        "shij,sjhd->sihd", weights, prompt_v, preferred_element_type=jnp.float32
    )
    active = jnp.arange(slot_len)[None, :] < prompt_length_list[:, None]
    prompt_out = (
        jnp.where(active[:, :, None, None], prompt_out, 0.0)
        .astype(jnp.bfloat16)
        .reshape(prompt_rows, -1)
    )
    cache_len = cache.shape[1]
    decode_q = queries[prompt_rows:].reshape(decode_count, head_count, HEAD_DIM)
    decode_k = keys_new[prompt_rows:].reshape(decode_count, head_count, HEAD_DIM)
    decode_v = values_new[prompt_rows:].reshape(decode_count, head_count, HEAD_DIM)
    keys_old = cache[:, :, 0].reshape(decode_count, cache_len, head_count, HEAD_DIM)
    values_old = cache[:, :, 1].reshape(decode_count, cache_len, head_count, HEAD_DIM)
    cache_scores = (
        jnp.einsum("dhe,dthe->dht", decode_q, keys_old, preferred_element_type=jnp.float32)
        * score_scale
    )
    live_cache = jnp.arange(cache_len)[None, None, :] < cache_length_list[:, None, None]
    cache_scores = jnp.where(live_cache, cache_scores, -1e30)
    self_score = (
        jnp.einsum("dhe,dhe->dh", decode_q, decode_k, preferred_element_type=jnp.float32)
        * score_scale
    )
    row_top = jnp.maximum(jnp.max(cache_scores, axis=2), self_score)
    cache_weights = jnp.where(live_cache, jnp.exp(cache_scores - row_top[:, :, None]), 0.0)
    self_weight = jnp.exp(self_score - row_top)
    totals = jnp.sum(cache_weights, axis=2) + self_weight
    cache_weights = (cache_weights / totals[:, :, None]).astype(jnp.bfloat16)
    self_weight = (self_weight / totals).astype(jnp.bfloat16)
    decode_out = jnp.einsum(
        "dht,dthe->dhe", cache_weights, values_old, preferred_element_type=jnp.float32
    )
    decode_out = decode_out + self_weight.astype(jnp.float32)[:, :, None] * decode_v.astype(
        jnp.float32
    )
    decode_out = decode_out.astype(jnp.bfloat16).reshape(decode_count, -1)
    attended = jnp.concatenate([prompt_out, decode_out], axis=0)
    mixed = jnp.dot(
        attended,
        lax.all_gather(output_weight, "req", axis=1, tiled=True),
        preferred_element_type=jnp.float32,
    )
    summed = lax.psum_scatter(
        mixed.astype(jnp.bfloat16), "mp", scatter_dimension=1, tiled=True
    ).astype(jnp.float32)
    return (tokens.astype(jnp.float32) + summed + output_bias[None]).astype(jnp.bfloat16)


def solution(mesh):
    placed = (
        P("req", "mp"),
        P(),
        P(),
        P(None, "req", "mp"),
        P(None, "mp"),
        P("req", "mp", None),
        P("req", None, None, "mp"),
        P("req", None),
        P("req"),
        P("req", None, None, "mp"),
        P("req"),
        P("mp", "req"),
        P("mp"),
    )
    quick = mesh.shape["req"] == 2 * NZ and mesh.shape["mp"] == NM
    return jax.shard_map(
        packed_device if quick else on_device, mesh=mesh, in_specs=placed, out_specs=P("req", "mp"), check_vma=False
    )
```
